32 devices in a mesh: batch: 8 (over y, x, core), tensor: 4 (over z).
Axes of the slice: x: 2, y: 2, z: 4, core: 2. Of those that a mesh axis runs over, the one named last changes fastest.
Arguments:
- block_input: bfloat16 [75264, 256], P(('batch', 'tensor')), may hold values from -6 to 6
- cotangent: bfloat16 [75264, 256], P(('batch', 'tensor')), may hold values from -6 to 6
- qkv_master: float32 [3, 256, 256], P(None, 'batch', 'tensor'), may hold values from -0.375 to 0.375
- qkv_moments: float32 [2, 3, 256, 256], P(None, None, 'batch', 'tensor'), as said below
- proj_master: float32 [256, 256], P('tensor', 'batch'), may hold values from -0.75 to 0.75
- proj_moments: float32 [2, 256, 256], P(None, 'tensor', 'batch'), as said below
- fc1_master: float32 [256, 1024], P('batch', 'tensor'), may hold values from -0.375 to 0.375
- fc1_moments: float32 [2, 256, 1024], P(None, 'batch', 'tensor'), as said below
- fc2_master: float32 [1024, 256], P('tensor', 'batch'), may hold values from -0.25 to 0.25
- fc2_moments: float32 [2, 1024, 256], P(None, 'tensor', 'batch'), as said below
- norm_params: float32 [6, 256], replicated, may hold values from -1.3 to 1.3, as said below
- norm_moments: float32 [2, 6, 256], replicated, as said below
- lepe_params: float32 [10, 256], replicated, may hold values from -1 to 1
- lepe_moments: float32 [2, 10, 256], replicated, as said below
- fc1_bias: float32 [1024], replicated, may hold values from -1.5 to 1.5
- fc1_bias_moments: float32 [2, 1024], replicated, as said below
Outputs:
- output: bfloat16 [75264, 256], P(('batch', 'tensor'))
- input_grad: float32 [75264, 256], P(('batch', 'tensor'))
- qkv_grad: float32 [3, 256, 256], P(None, 'batch', 'tensor')
- qkv_new: float32 [3, 256, 256], P(None, 'batch', 'tensor')
- qkv_low: bfloat16 [3, 256, 256], P(None, 'batch', 'tensor')
- qkv_moments_new: float32 [2, 3, 256, 256], P(None, None, 'batch', 'tensor')
- proj_grad: float32 [256, 256], P('tensor', 'batch')
- proj_new: float32 [256, 256], P('tensor', 'batch')
- proj_low: bfloat16 [256, 256], P('tensor', 'batch')
- proj_moments_new: float32 [2, 256, 256], P(None, 'tensor', 'batch')
- fc1_grad: float32 [256, 1024], P('batch', 'tensor')
- fc1_new: float32 [256, 1024], P('batch', 'tensor')
- fc1_low: bfloat16 [256, 1024], P('batch', 'tensor')
- fc1_moments_new: float32 [2, 256, 1024], P(None, 'batch', 'tensor')
- fc2_grad: float32 [1024, 256], P('tensor', 'batch')
- fc2_new: float32 [1024, 256], P('tensor', 'batch')
- fc2_low: bfloat16 [1024, 256], P('tensor', 'batch')
- fc2_moments_new: float32 [2, 1024, 256], P(None, 'tensor', 'batch')
- norm_grad: float32 [6, 256], replicated
- norm_new: float32 [6, 256], replicated
- norm_moments_new: float32 [2, 6, 256], replicated
- lepe_grad: float32 [10, 256], replicated
- lepe_new: float32 [10, 256], replicated
- lepe_moments_new: float32 [2, 10, 256], replicated
- fc1_bias_grad: float32 [1024], replicated
- fc1_bias_new: float32 [1024], replicated
- fc1_bias_moments_new: float32 [2, 1024], replicated
- grad_norm: float32 [], replicated
- rms: float32 [4], replicated
The draws below stay inside these ranges and needn't reach their ends.
Inputs may be any that keep to these rules, and one draw needn't show every extreme that they name: `qkv_moments`: member 0 holds first moments of both signs, member 1 positive second moments. `proj_moments`: member 0 holds first moments of both signs, member 1 positive second moments. `fc1_moments`: member 0 holds first moments of both signs, member 1 positive second moments. `fc2_moments`: member 0 holds first moments of both signs, member 1 positive second moments. `norm_moments`: member 0 holds first moments of both signs, member 1 positive second moments. `lepe_moments`: member 0 holds first moments of both signs, member 1 positive second moments. `fc1_bias_moments`: member 0 holds first moments of both signs, member 1 positive second moments. `norm_params`: rows 0 and 3 are gains near one, the others signed.
All inputs are finite; a program needn't handle non-finite values.
Results may differ from the reference program's by a relative error of at most 0.0078.
The reference program's roundings to bfloat16 on the way count: a program that leaves them out, or rounds other values in their place, can miss the bound.
Values may be sent and summed in bfloat16 or wider, within the bound.
A program may use at most 256 MiB of HBM per device.

```python
import math
import jax
import jax.numpy as jnp
from jax import lax

D = 256
FF = 1024
HD = 32
GRID = 14
SPLIT = 7
STEP = 10
TOKENS = 75264
NPARAM = 791552


CLIP_SCALE = 6.0


def moment_pair(key, shape):
    entry_size = CLIP_SCALE
    first = jax.random.normal(jax.random.fold_in(key, 11), shape, jnp.float32) * (0.1 / 0.9) * entry_size
    spread = jnp.exp(jax.random.uniform(jax.random.fold_in(key, 12), shape, jnp.float32, 0.0, math.log(4.0)))
    second = spread * (0.001 / 0.999) * entry_size * entry_size
    return jnp.stack([first, second])


def draw_qkv_moments(key, part):
    return moment_pair(key, (3, D, D))


def draw_proj_moments(key, part):
    return moment_pair(key, (D, D))


def draw_fc1_moments(key, part):
    return moment_pair(key, (D, FF))


def draw_fc2_moments(key, part):
    return moment_pair(key, (FF, D))


def draw_norm_moments(key, part):
    return moment_pair(key, (6, D))


def draw_lepe_moments(key, part):
    return moment_pair(key, (10, D))


def draw_fc1_bias_moments(key, part):
    return moment_pair(key, (FF,))


def draw_norm_params(key, part):
    noise = jnp.clip(jax.random.normal(jax.random.fold_in(key, 21), (6, D), jnp.float32), -4.0, 4.0)
    level = jax.random.uniform(jax.random.fold_in(key, 22), (6, D), jnp.float32, -0.3, 0.3)
    is_gain = (jnp.arange(6) % 3 == 0)[:, None]
    return jnp.where(is_gain, 1.0 + level, 0.3 * noise)


def steps_of(key, shape, pieces, low, largest):
    level = 1.0
    for axis_at, shards_of in pieces:
        heights = jax.random.uniform(jax.random.fold_in(jax.random.fold_in(key, 6), axis_at), (shards_of,), jnp.float32, low / len(pieces), largest / len(pieces))
        level = level * jnp.repeat(jnp.exp(heights), shape[axis_at] // shards_of).reshape((-1,) + (1,) * (len(shape) - 1 - axis_at))
    return level


def scatter_about(own_key, dims, scale, limit, pieces=(), held_as=jnp.bfloat16):
    entries = jax.random.normal(own_key, dims, jnp.float32) * scale
    if len(pieces) > 0:
        entries = steps_of(own_key, dims, pieces, -0.22, 0.18) * entries
    return jnp.clip(entries, min=-limit, max=limit).astype(held_as)


def setup_inputs(seed: int = 0) -> dict:
    arg_keys = jax.random.split(jax.random.key(seed), 17)
    return {
        "block_input": scatter_about(arg_keys[0], (TOKENS, D), 1.0, 6.0, ((0, 32),)),
        "cotangent": scatter_about(arg_keys[1], (TOKENS, D), 1.0, 6.0, ((0, 32),)),
        "qkv_master": scatter_about(arg_keys[2], (3, D, D), D ** -0.5, 0.375, ((1, 8), (2, 4)), jnp.float32),
        "qkv_moments": draw_qkv_moments(jax.random.fold_in(arg_keys[16], 71), 0),
        "proj_master": scatter_about(arg_keys[4], (D, D), (D // 4) ** -0.5, 0.75, ((0, 4), (1, 8)), jnp.float32),
        "proj_moments": draw_proj_moments(jax.random.fold_in(arg_keys[16], 71), 0),
        "fc1_master": scatter_about(arg_keys[6], (D, FF), D ** -0.5, 0.375, ((0, 8), (1, 4)), jnp.float32),
        "fc1_moments": draw_fc1_moments(jax.random.fold_in(arg_keys[16], 71), 0),
        "fc2_master": scatter_about(arg_keys[8], (FF, D), (FF // 2) ** -0.5, 0.25, ((0, 4), (1, 8)), jnp.float32),
        "fc2_moments": draw_fc2_moments(jax.random.fold_in(arg_keys[16], 71), 0),
        "norm_params": draw_norm_params(jax.random.fold_in(arg_keys[16], 71), 0),
        "norm_moments": draw_norm_moments(jax.random.fold_in(arg_keys[16], 71), 0),
        "lepe_params": scatter_about(arg_keys[12], (10, D), 36 ** -0.5, 1.0, (), jnp.float32),
        "lepe_moments": draw_lepe_moments(jax.random.fold_in(arg_keys[16], 71), 0),
        "fc1_bias": scatter_about(arg_keys[14], (FF,), 0.3, 1.5, (), jnp.float32),
        "fc1_bias_moments": draw_fc1_bias_moments(jax.random.fold_in(arg_keys[16], 71), 0),
    }


CLIP_SCALE = 6.0
BETA_ONE = 0.9
BETA_TWO = 0.999
ADAM_EPS = 1e-08
DECAY_RATE = 0.05
RATE_MATRIX = 0.1
RATE_VECTOR = 0.6
NORM_EPS = 1e-05

@jax.custom_vjp
def low(v):
    return lax.optimization_barrier(v.astype(jnp.bfloat16)).astype(jnp.float32)

@jax.custom_vjp
def low_back(v):
    return v

def low_keep(v):
    return (low(v), None)

def low_pass(kept, grad):
    return (grad,)

def back_keep(v):
    return (v, None)

def back_low(kept, grad):
    return (low(grad),)
low.defvjp(low_keep, low_pass)
low_back.defvjp(back_keep, back_low)

def clip_limit():
    return CLIP_SCALE * math.sqrt(NPARAM)

def layer_norm(values, gain, shift_term):
    centre = lax.optimization_barrier(jnp.mean(values, -1, keepdims=True))
    centred = values - centre
    spread = lax.optimization_barrier(jnp.mean(centred * centred, -1, keepdims=True))
    return centred * lax.rsqrt(spread + NORM_EPS) * gain + shift_term

def to_windows(values, branch):
    trailing = values.shape[3:]
    images = values.shape[0]
    stripes = GRID // SPLIT
    if branch == 0:
        return values.reshape((images * stripes, SPLIT, GRID) + trailing)
    moved = jnp.swapaxes(values.reshape((images, GRID, stripes, SPLIT) + trailing), 1, 2)
    return moved.reshape((images * stripes, GRID, SPLIT) + trailing)

def from_windows(values, branch, images):
    trailing = values.shape[3:]
    stripes = GRID // SPLIT
    if branch == 0:
        return values.reshape((images, GRID, GRID) + trailing)
    moved = jnp.swapaxes(values.reshape((images, stripes, GRID, SPLIT) + trailing), 1, 2)
    return moved.reshape((images, GRID, GRID) + trailing)

def flat_rows(window):
    return window.reshape((window.shape[0], window.shape[1] * window.shape[2]) + window.shape[3:])

def position_term(window, kernel, bias_term):
    height = window.shape[1]
    across = window.shape[2]
    padded = jnp.pad(window, ((0, 0), (1, 1), (1, 1), (0, 0), (0, 0)))
    summed = jnp.zeros_like(window) + bias_term
    for offset in range(9):
        summed = summed + padded[:, offset // 3:offset // 3 + height, offset % 3:offset % 3 + across] * kernel[offset]
    return summed

def split_heads(rows_in, branch, images):
    halves = rows_in.shape[1] // (2 * HD)
    return to_windows(rows_in.reshape(images, GRID, GRID, halves, 2, HD)[:, :, :, :, branch], branch)

def branch_params(lepe_local, branch):
    halves = lepe_local.shape[1] // (2 * HD)
    shaped = lepe_local.reshape(10, halves, 2, HD)
    return (shaped[:9, :, branch], shaped[9, :, branch])

def join_heads(windows, images, channels):
    merged = [from_windows(window, branch, images) for branch, window in enumerate(windows)]
    return jnp.stack(merged, -2).reshape(images * GRID * GRID, channels)

def stripe_exact(queries, key_rows, value_rows, kernel, bias_term, factor):
    scores = low_back(jnp.einsum('sqhe,skhe->shqk', flat_rows(queries), flat_rows(key_rows), precision=lax.Precision.HIGHEST) * factor)
    attend = low(jax.nn.softmax(scores, axis=-1))
    mixed = jnp.einsum('shqk,skhe->sqhe', attend, flat_rows(value_rows), precision=lax.Precision.HIGHEST)
    return mixed + flat_rows(position_term(value_rows, kernel, bias_term))

def attend_exact(query_rows, key_rows, value_rows, lepe_local):
    images = query_rows.shape[0] // (GRID * GRID)
    outputs = []
    for branch in range(2):
        windows = [split_heads(source, branch, images) for source in (query_rows, key_rows, value_rows)]
        kernel, bias_term = branch_params(lepe_local, branch)
        mixed = stripe_exact(windows[0], windows[1], windows[2], kernel, bias_term, HD ** (-0.5))
        outputs.append(mixed.reshape(windows[2].shape))
    return join_heads(outputs, images, query_rows.shape[1])

def matmul(left, right):
    return jnp.dot(left, right, precision=lax.Precision.HIGHEST)

def layer_exact(input_float, qkv_weight, proj_weight, fc1_weight, fc2_weight, norm_values, lepe_values, fc1_shift):
    normed = low(layer_norm(input_float, norm_values[0], norm_values[1]))
    qkv_rounded = low(qkv_weight)
    query_rows = low_back(low(matmul(normed, qkv_rounded[0])))
    key_rows = low_back(low(matmul(normed, qkv_rounded[1])))
    value_rows = low_back(low(matmul(normed, qkv_rounded[2])))
    attended = low_back(low(attend_exact(query_rows, key_rows, value_rows, lepe_values)))
    branch_one = low_back(matmul(attended, low(proj_weight)) + norm_values[2])
    middle = input_float + branch_one
    normed_two = low(layer_norm(middle, norm_values[3], norm_values[4]))
    hidden = low_back(matmul(normed_two, low(fc1_weight)) + fc1_shift)
    activated = low(jax.nn.gelu(hidden, approximate=False))
    branch_two = low_back(matmul(activated, low(fc2_weight)) + norm_values[5])
    result = middle + branch_two
    squares = jnp.stack([jnp.sum(branch_one * branch_one), jnp.sum(middle * middle), jnp.sum(branch_two * branch_two), jnp.sum(result * result)])
    return (result, squares)

def adam_step(master, moments, clipped, learn_rate, decay_term):
    first = BETA_ONE * moments[0] + (1.0 - BETA_ONE) * clipped
    second = BETA_TWO * moments[1] + (1.0 - BETA_TWO) * clipped * clipped
    first_hat = first / (1.0 - BETA_ONE ** STEP)
    second_hat = second / (1.0 - BETA_TWO ** STEP)
    updated = master - learn_rate * (first_hat / (jnp.sqrt(second_hat) + ADAM_EPS) + decay_term * master)
    return (updated, jnp.stack([first, second]))

def reference(block_input, cotangent, qkv_master, qkv_moments, proj_master, proj_moments, fc1_master, fc1_moments, fc2_master, fc2_moments, norm_params, norm_moments, lepe_params, lepe_moments, fc1_bias, fc1_bias_moments):
    block_rows = 16 * GRID * GRID
    blocks = block_input.shape[0] // block_rows
    features = block_input.shape[1]
    masters = (qkv_master, proj_master, fc1_master, fc2_master, norm_params, lepe_params, fc1_bias)

    def block_step(carry, inputs):
        input_block, cot_block = inputs
        result, pull_back, squares = jax.vjp(layer_exact, input_block.astype(jnp.float32), masters[0], masters[1], masters[2], masters[3], masters[4], masters[5], masters[6], has_aux=True)
        grads = pull_back(cot_block.astype(jnp.float32))
        sums = tuple((carry[0][member] + grads[member + 1] for member in range(7)))
        return ((sums, carry[1] + squares), (result.astype(jnp.bfloat16), grads[0]))
    start_state = (tuple((jnp.zeros_like(master) for master in masters)), jnp.zeros((4,), jnp.float32))
    scanned = lax.scan(block_step, start_state, (block_input.reshape(blocks, block_rows, features), cotangent.reshape(blocks, block_rows, features)))
    sums, squares = scanned[0]
    outputs, grad_input = scanned[1]
    square_total = sum((jnp.sum(gradient * gradient) for gradient in sums))
    grad_norm = jnp.sqrt(square_total)
    factor = jnp.minimum(1.0, clip_limit() / (grad_norm + 1e-06))
    moments_in = (qkv_moments, proj_moments, fc1_moments, fc2_moments, norm_moments, lepe_moments, fc1_bias_moments)
    results = []
    for member in range(7):
        clipped = sums[member] * factor
        learn_rate = RATE_MATRIX if member < 4 else RATE_VECTOR
        decay_term = DECAY_RATE if member < 4 else 0.0
        updated, moments_new = adam_step(masters[member], moments_in[member], clipped, learn_rate, decay_term)
        results.append((clipped, updated, moments_new))
    rms_values = jnp.sqrt(squares / (block_input.shape[0] * block_input.shape[1]))
    return (outputs.reshape(block_input.shape), grad_input.reshape(block_input.shape), results[0][0], results[0][1], results[0][1].astype(jnp.bfloat16), results[0][2], results[1][0], results[1][1], results[1][1].astype(jnp.bfloat16), results[1][2], results[2][0], results[2][1], results[2][1].astype(jnp.bfloat16), results[2][2], results[3][0], results[3][1], results[3][1].astype(jnp.bfloat16), results[3][2], results[4][0], results[4][1], results[4][2], results[5][0], results[5][1], results[5][2], results[6][0], results[6][1], results[6][2], grad_norm, rms_values)
```

```python
import functools, math
import numpy as np
import jax, jax.numpy as jnp
from jax import lax
from jax.experimental import pallas as pl
from jax.experimental.pallas import tpu as pltpu
from jax.sharding import PartitionSpec as P

HD = 32
STEP = 10
NPARAM = 791552
CLIP_SCALE = 6.0
BETA_ONE = 0.9
BETA_TWO = 0.999
ADAM_EPS = 1e-08
DECAY_RATE = 0.05
RATE_MATRIX = 0.1
RATE_VECTOR = 0.6
GRID = 14
SPLIT = 7
CELLS = 196
PAD = 112
D = 256
FF = 1024
NORM_EPS = 1e-5
BF = jnp.bfloat16
F32 = jnp.float32
SCALE = HD ** -0.5
LOG2E = 1.4426950408889634


def slot_of(branch, cell):
    row, col = divmod(cell, GRID)
    if branch == 0:
        return row * 16 + col
    stripe, inner = divmod(col, SPLIT)
    return stripe * PAD + row * 8 + inner


def spread_tables():
    into = np.zeros((2, 4, 2 * PAD, 208), np.float32)
    for branch in range(2):
        for cell in range(CELLS):
            for j in range(4):
                into[branch, j, slot_of(branch, cell), cell + 4 * j] = 1.0
    return into.reshape(8, 2 * PAD, 208), into.transpose(0, 1, 3, 2).reshape(8, 208, 2 * PAD)


def key_mask():
    mask = np.full((2, PAD, 128), -1e30, np.float32)
    for branch in range(2):
        for cell in range(CELLS):
            slot = slot_of(branch, cell)
            if slot < PAD:
                mask[branch, slot] = 0.0
    return mask


def lane_table(tensor):
    heads = 4 // tensor
    assert heads == 1
    table = np.zeros((512, 512), np.float32)
    for t in range(4):
        for j in range(2):
            for b in range(2):
                for e in range(HD):
                    table[t * 128 + j * 64 + b * 32 + e, b * 256 + j * 128 + t * 32 + e] = 1.0
    return table


def dot(a, b):
    return lax.dot_general(a, b, (((1,), (0,)), ((), ())), preferred_element_type=F32)


def dot_nt(a, b):
    return lax.dot_general(a, b, (((1,), (1,)), ((), ())), preferred_element_type=F32)


def norm_stats(v):
    centre = jnp.mean(v, -1, keepdims=True)
    centred = v - centre
    spread = jnp.mean(centred * centred, -1, keepdims=True)
    rate = lax.rsqrt(spread + NORM_EPS)
    return centred * rate, rate


def norm_back(grad, gain, xhat, rate):
    gx = grad * gain
    first = jnp.mean(gx, -1, keepdims=True)
    second = jnp.mean(gx * xhat, -1, keepdims=True)
    return rate * (gx - first - xhat * second)


def fold8(v):
    return jnp.sum(v.reshape(v.shape[0] // 8, 8, v.shape[1]), axis=0)


def gelu_pair(h):
    e = jnp.exp2(h * h * (-0.5 * LOG2E))
    t = 1.0 / (1.0 + (0.3275911 * math.sqrt(0.5)) * jnp.abs(h))
    poly = t * (0.5 * 0.254829592 + t * (0.5 * -0.284496736 + t * (0.5 * 1.421413741 + t * (0.5 * -1.453152027 + t * (0.5 * 1.061405429)))))
    tail = poly * e
    phi = jnp.where(h < 0, tail, 1.0 - tail)
    return h * phi, phi + h * e * (1.0 / math.sqrt(2 * math.pi))


def head_masks():
    lane = lax.broadcasted_iota(jnp.int32, (128, 128), 1) // HD
    return [jnp.where(lane == h, 1.0, 0.0).astype(BF) for h in range(4)]


def head_blocks(z, masks):
    zp = jnp.concatenate([z, jnp.zeros((16, 128), BF)], 0)
    return [zp * masks[h] for h in range(4)]


def col_shift(v):
    return pltpu.roll(v, 1, 0), v, pltpu.roll(v, PAD - 1, 0)


def row_up(u, pitch):
    return jnp.concatenate([u[pitch:], jnp.zeros((pitch, 128), F32)], 0)


def row_down(u, pitch):
    return jnp.concatenate([jnp.zeros((pitch, 128), F32), u[:-pitch]], 0)


def window_sum(v, taps, pitch):
    cols = col_shift(v)
    rows = [sum(taps[3 * i + j] * cols[j] for j in range(3)) for i in range(3)]
    return row_down(rows[0], pitch) + rows[1] + row_up(rows[2], pitch)


def window_sum_back(d, taps, pitch):
    cols = col_shift(d)
    rows = [sum(taps[3 * i + j] * cols[2 - j] for j in range(3)) for i in range(3)]
    return row_up(rows[0], pitch) + rows[1] + row_down(rows[2], pitch)


def tap_sums(d, v, pitch):
    cols = col_shift(v)
    out = []
    for i in range(3):
        moved = row_up(d, pitch) if i == 0 else (d if i == 1 else row_down(d, pitch))
        for j in range(3):
            out.append(fold8(moved * cols[j]))
    return out


MT = 336
NT_TILES = 7


def compute_kernel(
    x_ref, cot_ref, w_ref, norm_ref, lepe_ref, bias_ref, into_ref, outof_ref, mask_ref, lane_ref,
    out_ref, ig_ref, grad_ref, small_ref,
    fc1_s, fc2_s, wcat_s, proj_s, lepe_s, n1_s, q_s, k_s, v_s, a_s, p_s, att_s, n2_s, act_s, gh_s, gb_s, ga_s, do_s, dqkv_s, acc_s, tacc_s, pack_s,
):
    rows = x_ref.shape[0]
    images = rows // CELLS
    chunks = images // 4

    parts, depth = w_ref.shape[0], w_ref.shape[2]
    for t in range(4):
        for n in range(parts):
            at = slice(n * depth, (n + 1) * depth)
            fc1_s[at, t * 256:(t + 1) * 256] = w_ref[n, t, :, 0:256]
            fc2_s[at, t * 256:(t + 1) * 256] = w_ref[n, t, :, 256:512]
            pack_s[0, at, t * 128:(t + 1) * 128] = w_ref[n, t, :, 512:640]
            pack_s[1, at, t * 128:(t + 1) * 128] = w_ref[n, t, :, 640:768]
    for half in range(2):
        work = dot(pack_s[half], lane_ref[...]).astype(BF)
        for b in range(2):
            if half == 0:
                wcat_s[:, b * 384:b * 384 + 256] = work[:, b * 256:b * 256 + 256]
            else:
                wcat_s[:, b * 384 + 256:b * 384 + 384] = work[:, b * 256:b * 256 + 128]
                proj_s[:, b * 128:b * 128 + 128] = work[:, b * 256 + 128:b * 256 + 256]
    lp = lepe_ref[...]
    lepe_s[0:10, :] = jnp.concatenate([lp[:, h * 64 + b * 32:h * 64 + b * 32 + 32] for b in range(2) for h in range(4)], 1)
    acc_s[...] = jnp.zeros_like(acc_s)
    tacc_s[...] = jnp.zeros_like(tacc_s)

    @pl.loop(0, NT_TILES)
    def _(i):
        sl = pl.ds(pl.multiple_of(i * MT, 16), MT)
        xhat, rate = norm_stats(x_ref[sl, :].astype(F32))
        n1_s[sl, :] = (xhat * norm_ref[0:1, :] + norm_ref[1:2, :]).astype(BF)

    @pl.loop(0, chunks)
    def _(c):
        for j in range(4):
            window = n1_s[pl.ds(pl.multiple_of(c * 784 + 192 * j, 16), 208), :]
            for b in range(2):
                spread = dot(into_ref[b * 4 + j], window).astype(BF)
                qkv = dot(spread, wcat_s[:, b * 384:(b + 1) * 384]).astype(BF)
                for s in range(2):
                    at = c * 8 + j * 2 + s
                    q_s[b, at] = qkv[s * PAD:(s + 1) * PAD, 0:128]
                    k_s[b, at] = qkv[s * PAD:(s + 1) * PAD, 128:256]
                    v_s[b, at] = qkv[s * PAD:(s + 1) * PAD, 256:384]

    masks = head_masks()

    @pl.loop(0, images * 2)
    def _(i):
        for b in range(2):
            pitch = 16 - 8 * b
            q, k, v = q_s[b, i], k_s[b, i], v_s[b, i]
            qb = head_blocks(q, masks)
            vt = jnp.transpose(v)
            ots = []
            for h in range(4):
                s = dot_nt(k, qb[h]) * (SCALE * LOG2E) + mask_ref[b]
                m = jnp.max(s, 0, keepdims=True)
                p = jnp.exp2(s - m)
                r = 1.0 / jnp.sum(p, 0, keepdims=True)
                pn = (p * r).astype(BF)
                p_s[b, i, :, h * 128:(h + 1) * 128] = pn
                ots.append(dot(vt[h * HD:(h + 1) * HD], pn))
            mixed = jnp.transpose(jnp.concatenate(ots, 0))[:PAD]
            taps = [lepe_s[n:n + 1, b * 128:(b + 1) * 128] for n in range(10)]
            local = window_sum(v.astype(F32), taps, pitch) + taps[9]
            a_s[b, i] = (mixed + local).astype(BF)

    def gather_rows(source, c, dest, lanes):
        for b in range(2):
            tail = None
            for j in range(4):
                both = jnp.concatenate([source(b, c * 8 + j * 2), source(b, c * 8 + j * 2 + 1)], 0)
                got = dot(outof_ref[b * 4 + j], both)
                head = got[0:16] if tail is None else got[0:16] + tail
                base = c * 784 + 192 * j
                cols = slice(b * lanes, (b + 1) * lanes)
                dest[pl.ds(pl.multiple_of(base, 16), 16), cols] = head.astype(BF)
                dest[pl.ds(pl.multiple_of(base + 16, 16), 176), cols] = got[16:192].astype(BF)
                tail = got[192:208]
                if j == 3:
                    dest[pl.ds(pl.multiple_of(base + 192, 16), 16), cols] = tail.astype(BF)

    @pl.loop(0, chunks)
    def _(c):
        gather_rows(lambda b, at: a_s[b, at], c, att_s, 128)

    @pl.loop(0, NT_TILES)
    def _(i):
        sl = pl.ds(pl.multiple_of(i * MT, 16), MT)
        one = dot_nt(att_s[sl, :], proj_s[...]) + norm_ref[2:3, :]
        middle = x_ref[sl, :].astype(F32) + one
        xhat, rate = norm_stats(middle)
        n2 = (xhat * norm_ref[3:4, :] + norm_ref[4:5, :]).astype(BF)
        n2_s[sl, :] = n2
        cot = cot_ref[sl, :]
        two = jnp.zeros((MT, D), F32)
        gn = jnp.zeros((MT, D), F32)
        for f in range(4):
            fs = slice(f * 256, (f + 1) * 256)
            hidden = dot(n2, fc1_s[:, fs]) + bias_ref[f:f + 1, :]
            gelu, slope = gelu_pair(hidden)
            act = gelu.astype(BF)
            act_s[sl, fs] = act
            two = two + dot_nt(act, fc2_s[:, fs])
            gh_f = dot(cot, fc2_s[:, fs]) * slope
            gh = gh_f.astype(BF)
            gh_s[sl, fs] = gh
            acc_s[10 + f] += fold8(gh.astype(F32))
            gn = gn + dot_nt(gh, fc1_s[:, fs])
        two = two + norm_ref[5:6, :]
        result = middle + two
        out_ref[sl, :] = result.astype(BF)
        acc_s[6] += fold8(one * one)
        acc_s[7] += fold8(middle * middle)
        acc_s[8] += fold8(two * two)
        acc_s[9] += fold8(result * result)
        cotf = cot.astype(F32)
        acc_s[5] += fold8(cotf)
        acc_s[3] += fold8(gn * xhat)
        acc_s[4] += fold8(gn)
        gm = cotf + norm_back(gn, norm_ref[3:4, :], xhat, rate)
        ig_ref[sl, :] = gm
        gb = gm.astype(BF)
        gb_s[sl, :] = gb
        acc_s[2] += fold8(gb.astype(F32))
        ga_s[sl, :] = dot(gb, proj_s[...]).astype(BF)

    def weight_grad(left, right):
        return lax.dot_general(left, right, (((0,), (0,)), ((), ())), preferred_element_type=F32)

    def put_rows(value, t, off):
        for n in range(parts):
            grad_ref[n, t, :, off:off + value.shape[1]] = value[n * depth:(n + 1) * depth]

    def put_mlp(left, right, off):
        for t in range(4):
            value = weight_grad(left[...], right[:, t * 256:(t + 1) * 256]).astype(BF)
            put_rows(value, t, off)

    put_mlp(n2_s, gh_s, 0)
    put_mlp(cot_ref, act_s, 256)

    @pl.loop(0, chunks)
    def _(c):
        for j in range(4):
            window = ga_s[pl.ds(pl.multiple_of(c * 784 + 192 * j, 16), 208), :]
            for b in range(2):
                spread = dot(into_ref[b * 4 + j], window[:, b * 128:(b + 1) * 128]).astype(BF)
                for s in range(2):
                    do_s[b, c * 8 + j * 2 + s] = spread[s * PAD:(s + 1) * PAD]

    @pl.loop(0, images * 2)
    def _(i):
        for b in range(2):
            pitch = 16 - 8 * b
            q, k, v, do = q_s[b, i], k_s[b, i], v_s[b, i], do_s[b, i]
            qb = head_blocks(q, masks)
            db = head_blocks(do, masks)
            kt = jnp.transpose(k)
            dqt = []
            dk = jnp.zeros((PAD, 128), F32)
            dv = jnp.zeros((PAD, 128), F32)
            for h in range(4):
                pn = p_s[b, i, :, h * 128:(h + 1) * 128]
                pf = pn.astype(F32)
                t = pf * dot_nt(v, db[h])
                ds = (t - pf * jnp.sum(t, 0, keepdims=True)).astype(BF)
                dv = dv + dot(pn, db[h])
                dk = dk + dot(ds, qb[h])
                dqt.append(dot(kt[h * HD:(h + 1) * HD], ds))
            dq = jnp.transpose(jnp.concatenate(dqt, 0))[:PAD]
            taps = [lepe_s[n:n + 1, b * 128:(b + 1) * 128] for n in range(10)]
            dof, vf = do.astype(F32), v.astype(F32)
            dv = dv + window_sum_back(dof, taps, pitch)
            for n, part in enumerate(tap_sums(dof, vf, pitch)):
                tacc_s[b, n] += part
            tacc_s[b, 9] += fold8(dof)
            q_s[b, i] = (dq * SCALE).astype(BF)
            k_s[b, i] = (dk * SCALE).astype(BF)
            v_s[b, i] = dv.astype(BF)

    @pl.loop(0, chunks)
    def _(c):
        gather_rows(lambda b, at: jnp.concatenate([q_s[b, at], k_s[b, at], v_s[b, at]], 1), c, dqkv_s, 384)

    @pl.loop(0, NT_TILES)
    def _(i):
        sl = pl.ds(pl.multiple_of(i * MT, 16), MT)
        gn = dot_nt(dqkv_s[sl, :], wcat_s[...])
        xhat, rate = norm_stats(x_ref[sl, :].astype(F32))
        acc_s[0] += fold8(gn * xhat)
        acc_s[1] += fold8(gn)
        ig_ref[sl, :] = ig_ref[sl, :] + norm_back(gn, norm_ref[0:1, :], xhat, rate)

    gw = weight_grad(n1_s[...], dqkv_s[...]).astype(BF)
    gp = weight_grad(gb_s[...], att_s[...]).astype(BF)
    work0 = jnp.concatenate([gw[:, 0:256], gw[:, 384:640]], 1)
    work1 = jnp.concatenate([gw[:, 256:384], gp[:, 0:128], gw[:, 640:768], gp[:, 128:256]], 1)
    for half, work in enumerate((work0, work1)):
        packed = dot_nt(work, lane_ref[...]).astype(BF)
        for t in range(4):
            put_rows(packed[:, t * 128:(t + 1) * 128], t, 512 + 128 * half)
    for n in range(14):
        small_ref[n:n + 1, :] = jnp.sum(acc_s[n], 0, keepdims=True)
    for n in range(10):
        row = jnp.concatenate([jnp.sum(tacc_s[b, n], 0, keepdims=True) for b in range(2)], 1)
        small_ref[14 + n:15 + n, :] = jnp.concatenate([row[:, b * 128 + h * 32:b * 128 + h * 32 + 32] for h in range(4) for b in range(2)], 1)


def compute_call(x, cot, w, norm, lepe, bias):
    rows = x.shape[0]
    n = rows // CELLS * 2
    into, outof = spread_tables()
    args = (x, cot, w, norm, lepe, bias.reshape(4, 256), jnp.asarray(into, BF), jnp.asarray(outof, BF), jnp.asarray(key_mask()), jnp.asarray(lane_table(4), BF))
    V = pltpu.VMEM
    return pl.pallas_call(
        compute_kernel,
        out_shape=(
            jax.ShapeDtypeStruct((rows, D), BF),
            jax.ShapeDtypeStruct((rows, D), F32),
            jax.ShapeDtypeStruct(w.shape, BF),
            jax.ShapeDtypeStruct((24, D), F32),
        ),
        in_specs=[pl.BlockSpec(memory_space=V)] * len(args),
        out_specs=tuple([pl.BlockSpec(memory_space=V)] * 4),
        scratch_shapes=[
            V((D, FF), BF), V((D, FF), BF), V((D, 768), BF), V((D, D), BF), V((16, D), F32),
            V((rows, D), BF),
            V((2, n, PAD, 128), BF), V((2, n, PAD, 128), BF), V((2, n, PAD, 128), BF), V((2, n, PAD, 128), BF),
            V((2, n, PAD, 512), BF),
            V((rows, D), BF), V((rows, D), BF), V((rows, FF), BF), V((rows, FF), BF), V((rows, D), BF), V((rows, D), BF),
            V((2, n, PAD, 128), BF), V((rows, 768), BF),
            V((14, 8, D), F32), V((2, 10, 8, 128), F32), V((2, D, 512), BF),
        ],
        compiler_params=pltpu.CompilerParams(vmem_limit_bytes=60 * 2**20),
    )(*args)


MESH = pl.DeviceIdType.MESH


def ring_peers(batch, tensor):
    me_b, me_t = lax.axis_index("batch"), lax.axis_index("tensor")
    along_b = [(lax.rem(me_b + k, batch), me_t) for k in range(1, batch)]
    along_t = [(me_b, lax.rem(me_t + k, tensor)) for k in range(1, tensor)]
    return me_b, me_t, along_b, along_t


def greet(peers):
    barrier = pltpu.get_barrier_semaphore()
    for peer in peers:
        pl.semaphore_signal(barrier, inc=1, device_id=peer, device_id_type=MESH)
    pl.semaphore_wait(barrier, len(peers))


def gather_kernel(batch, tensor, qkv_ref, proj_ref, fc1_ref, fc2_ref, full_ref, own_s, keep_sem, send_t, recv_t, send_b, recv_b):
    me_b, me_t, along_b, along_t = ring_peers(batch, tensor)
    own_s[:, 0:256] = fc1_ref[...].astype(BF)
    own_s[:, 256:512] = jnp.transpose(fc2_ref[...]).astype(BF)
    own_s[:, 512:640] = jnp.concatenate([qkv_ref[0], qkv_ref[1]], 1).astype(BF)
    own_s[:, 640:768] = jnp.concatenate([qkv_ref[2], jnp.transpose(proj_ref[...])], 1).astype(BF)
    greet(along_b + along_t)
    mine = full_ref.at[me_b, me_t]
    keep = pltpu.make_async_copy(own_s, mine, keep_sem)
    keep.start()
    across = []
    for k, peer in enumerate(along_t):
        copy = pltpu.make_async_remote_copy(src_ref=own_s, dst_ref=mine, send_sem=send_t.at[k], recv_sem=recv_t.at[k], device_id=peer, device_id_type=MESH)
        copy.start()
        across.append(copy)
    passed = []
    for n in range(tensor):
        if n == 0:
            source, slot = own_s, me_t
        else:
            across[n - 1].wait_recv()
            slot = lax.rem(me_t + tensor - n, tensor)
            source = full_ref.at[me_b, slot]
        for k, peer in enumerate(along_b):
            copy = pltpu.make_async_remote_copy(src_ref=source, dst_ref=full_ref.at[me_b, slot], send_sem=send_b.at[n, k], recv_sem=recv_b.at[n, k], device_id=peer, device_id_type=MESH)
            copy.start()
            passed.append(copy)
    keep.wait()
    for copy in across:
        copy.wait_send()
    for copy in passed:
        copy.wait()


def gather_call(batch, tensor, qkv, proj, fc1, fc2):
    rows = fc1.shape[0]
    V = pltpu.VMEM
    dma = pltpu.SemaphoreType.DMA
    return pl.pallas_call(
        functools.partial(gather_kernel, batch, tensor),
        out_shape=jax.ShapeDtypeStruct((batch, tensor, rows, 768), BF),
        in_specs=[pl.BlockSpec(memory_space=V)] * 4,
        out_specs=pl.BlockSpec(memory_space=V),
        scratch_shapes=[V((rows, 768), BF), dma, dma((tensor - 1,)), dma((tensor - 1,)), dma((tensor, batch - 1)), dma((tensor, batch - 1))],
        compiler_params=pltpu.CompilerParams(collective_id=0, has_side_effects=True, vmem_limit_bytes=32 * 2**20),
    )(qkv, proj, fc1, fc2)


def reduce_kernel(
    batch, tensor, grad_ref, small_ref, shard_ref, total_ref, norm_ref,
    in_b, mid_s, in_t, small_b, small_t, square_b, square_t,
    send_b, recv_b, send_t, recv_t, send_sb, recv_sb, send_st, recv_st, send_qb, recv_qb, send_qt, recv_qt,
):
    me_b, me_t, along_b, along_t = ring_peers(batch, tensor)
    greet(along_b + along_t)

    def push(source, dest, peer, send_sem, recv_sem):
        copy = pltpu.make_async_remote_copy(src_ref=source, dst_ref=dest, send_sem=send_sem, recv_sem=recv_sem, device_id=peer, device_id_type=MESH)
        copy.start()
        return copy

    first = [push(grad_ref.at[peer[0]], in_b.at[k], peer, send_b.at[k], recv_b.at[k]) for k, peer in enumerate(along_b)]
    small_b[me_b] = small_ref[...]
    small_first = [push(small_ref, small_b.at[me_b], peer, send_sb.at[k], recv_sb.at[k]) for k, peer in enumerate(along_b)]
    for copy in small_first:
        copy.wait()
    part = small_b[0]
    for n in range(1, batch):
        part = part + small_b[n]
    total_ref[...] = part
    small_t[me_t] = part
    small_second = [push(total_ref, small_t.at[me_t], peer, send_st.at[k], recv_st.at[k]) for k, peer in enumerate(along_t)]
    for copy in first:
        copy.wait()

    for n in range(tensor):
        value = grad_ref[me_b, n].astype(F32)
        for k in range(batch - 1):
            value = value + in_b[k, n].astype(F32)
        mid_s[n] = value.astype(mid_s.dtype)

    second = [push(mid_s.at[peer[1]], in_t.at[k], peer, send_t.at[k], recv_t.at[k]) for k, peer in enumerate(along_t)]
    for copy in small_second:
        copy.wait()
    part = small_t[0]
    for n in range(1, tensor):
        part = part + small_t[n]
    total_ref[...] = part
    for copy in second:
        copy.wait()
    shard = mid_s[me_t].astype(F32)
    for k in range(tensor - 1):
        shard = shard + in_t[k].astype(F32)
    shard_ref[...] = shard
    squares = fold8(shard * shard)
    lanes = squares[:, 0:128]
    for n in range(1, 6):
        lanes = lanes + squares[:, n * 128:(n + 1) * 128]
    square_b[me_b] = lanes
    norm_ref[...] = lanes
    last = [push(norm_ref, square_b.at[me_b], peer, send_qb.at[k], recv_qb.at[k]) for k, peer in enumerate(along_b)]
    for copy in last:
        copy.wait()
    lanes = square_b[0]
    for n in range(1, batch):
        lanes = lanes + square_b[n]
    square_t[me_t] = lanes
    norm_ref[...] = lanes
    last = [push(norm_ref, square_t.at[me_t], peer, send_qt.at[k], recv_qt.at[k]) for k, peer in enumerate(along_t)]
    for copy in last:
        copy.wait()
    lanes = square_t[0]
    for n in range(1, tensor):
        lanes = lanes + square_t[n]
    matrix = jnp.sum(jnp.sum(lanes, 0, keepdims=True), 1, keepdims=True)
    vectors = total_ref[...]
    row = lax.broadcasted_iota(jnp.int32, vectors.shape, 0)
    vectors = jnp.where((row < 6) | (row >= 10), vectors, 0.0)
    vector = jnp.sum(jnp.sum(vectors * vectors, 0, keepdims=True), 1, keepdims=True)
    norm_ref[...] = jnp.broadcast_to(jnp.sqrt(matrix + vector), (8, 128))


def reduce_call(batch, tensor, grad, small, mid=BF):
    rows = grad.shape[2]
    V = pltpu.VMEM
    dma = pltpu.SemaphoreType.DMA
    pair = lambda n: [dma((n - 1,)), dma((n - 1,))]
    return pl.pallas_call(
        functools.partial(reduce_kernel, batch, tensor),
        out_shape=(jax.ShapeDtypeStruct((rows, 768), F32), jax.ShapeDtypeStruct((24, 256), F32), jax.ShapeDtypeStruct((8, 128), F32)),
        in_specs=[pl.BlockSpec(memory_space=V)] * 2,
        out_specs=tuple([pl.BlockSpec(memory_space=V)] * 3),
        scratch_shapes=[
            V((batch - 1, tensor, rows, 768), BF), V((tensor, rows, 768), mid), V((tensor - 1, rows, 768), mid),
            V((batch, 24, 256), F32), V((tensor, 24, 256), F32), V((batch, 8, 128), F32), V((tensor, 8, 128), F32),
        ] + pair(batch) + pair(tensor) + pair(batch) + pair(tensor) + pair(batch) + pair(tensor),
        compiler_params=pltpu.CompilerParams(collective_id=1, has_side_effects=True, vmem_limit_bytes=32 * 2**20),
    )(grad, small)


def adam(master, first, second, clipped, rate, decay):
    first = BETA_ONE * first + (1.0 - BETA_ONE) * clipped
    second = BETA_TWO * second + (1.0 - BETA_TWO) * clipped * clipped
    hat = first * (1.0 / (1.0 - BETA_ONE**STEP))
    spread = second * (1.0 / (1.0 - BETA_TWO**STEP))
    return master - rate * (hat / (jnp.sqrt(spread) + ADAM_EPS) + decay * master), first, second


def update_kernel(
    all_tokens, shard_ref, total_ref, norm_ref,
    qkv_w, qkv_m, proj_w, proj_m, fc1_w, fc1_m, fc2_w, fc2_m, norm_w, norm_m, lepe_w, lepe_m, bias_w, bias_m,
    qkv_g, qkv_n, qkv_l, qkv_o, proj_g, proj_n, proj_l, proj_o, fc1_g, fc1_n, fc1_l, fc1_o, fc2_g, fc2_n, fc2_l, fc2_o,
    norm_g, norm_n, norm_o, lepe_g, lepe_n, lepe_o, bias_g, bias_n, bias_o, size_o, rms_o,
):
    size = norm_ref[0:1, 0:1]
    factor = jnp.minimum(1.0, CLIP_SCALE * math.sqrt(NPARAM) / (size + 1e-06))
    size_o[...] = size

    def one(grad, w, m, g_o, n_o, l_o, m_o, at, rate, decay):
        clipped = grad * factor
        new, first, second = adam(w[at], m[(0,) + at], m[(1,) + at], clipped, rate, decay)
        g_o[at] = clipped
        n_o[at] = new
        if l_o is not None:
            l_o[at] = new.astype(BF)
        m_o[(0,) + at] = first
        m_o[(1,) + at] = second

    every = (slice(None), slice(None))
    one(shard_ref[:, 0:256], fc1_w, fc1_m, fc1_g, fc1_n, fc1_l, fc1_o, every, RATE_MATRIX, DECAY_RATE)
    one(jnp.transpose(shard_ref[:, 256:512]), fc2_w, fc2_m, fc2_g, fc2_n, fc2_l, fc2_o, every, RATE_MATRIX, DECAY_RATE)
    for j in range(3):
        one(shard_ref[:, 512 + 64 * j:576 + 64 * j], qkv_w, qkv_m, qkv_g, qkv_n, qkv_l, qkv_o, (j,) + every, RATE_MATRIX, DECAY_RATE)
    one(jnp.transpose(shard_ref[:, 704:768]), proj_w, proj_m, proj_g, proj_n, proj_l, proj_o, every, RATE_MATRIX, DECAY_RATE)
    one(total_ref[0:6], norm_w, norm_m, norm_g, norm_n, None, norm_o, every, RATE_VECTOR, 0.0)
    one(total_ref[14:24], lepe_w, lepe_m, lepe_g, lepe_n, None, lepe_o, every, RATE_VECTOR, 0.0)
    one(total_ref[10:14], bias_w, bias_m, bias_g, bias_n, None, bias_o, every, RATE_VECTOR, 0.0)
    sums = jnp.sum(total_ref[6:10], 1, keepdims=True)
    rms_o[...] = jnp.sqrt(sums * (1.0 / (all_tokens * D)))


def update_call(all_tokens, shard, total, norm, arrays):
    arrays = list(arrays)
    arrays[12], arrays[13] = arrays[12].reshape(4, 256), arrays[13].reshape(2, 4, 256)
    V = pltpu.VMEM
    like = lambda a, dt=F32: jax.ShapeDtypeStruct(a.shape, dt)
    outs = []
    for n in range(4):
        w, m = arrays[2 * n], arrays[2 * n + 1]
        outs += [like(w), like(w), like(w, BF), like(m)]
    for n in range(4, 7):
        w, m = arrays[2 * n], arrays[2 * n + 1]
        outs += [like(w), like(w), like(m)]
    outs += [jax.ShapeDtypeStruct((1, 1), F32), jax.ShapeDtypeStruct((4, 1), F32)]
    got = list(pl.pallas_call(
        functools.partial(update_kernel, all_tokens),
        out_shape=tuple(outs),
        in_specs=[pl.BlockSpec(memory_space=V)] * (3 + len(arrays)),
        out_specs=tuple([pl.BlockSpec(memory_space=V)] * len(outs)),
    )(shard, total, norm, *arrays))
    got[22], got[23], got[24] = got[22].reshape(1024), got[23].reshape(1024), got[24].reshape(2, 1024)
    got[25], got[26] = got[25].reshape(()), got[26].reshape(4)
    return got


def shards(block_input, cotangent, *arrays):
    batch, tensor = lax.axis_size("batch"), lax.axis_size("tensor")
    qkv, _, proj, _, fc1, _, fc2, _, norm, _, lepe, _, bias, _ = arrays
    full = gather_call(batch, tensor, qkv, proj, fc1, fc2)
    output, input_grad, grads, small = compute_call(block_input, cotangent, full, norm, lepe, bias)
    shard, total, size = reduce_call(batch, tensor, grads, small)
    rest = update_call(block_input.shape[0] * batch * tensor, shard, total, size, arrays)
    return (output, input_grad, *rest)


def solution(mesh):
    token, matrix, moment = P(("batch", "tensor"), None), P("batch", "tensor"), P(None, "batch", "tensor")
    back, back_moment = P("tensor", "batch"), P(None, "tensor", "batch")
    stack, stack_moment = P(None, "batch", "tensor"), P(None, None, "batch", "tensor")
    return jax.shard_map(
        shards,
        mesh=mesh,
        in_specs=(token, token, stack, stack_moment, back, back_moment, matrix, moment, back, back_moment) + (P(),) * 6,
        out_specs=(token, token) + (stack,) * 3 + (stack_moment,) + (back,) * 3 + (back_moment,) + (matrix,) * 3 + (moment,) + (back,) * 3 + (back_moment,) + (P(),) * 11,
        check_vma=False,
    )
```

```python
import functools, math
import numpy as np
import jax, jax.numpy as jnp
from jax import lax
from jax.experimental import pallas as pl
from jax.experimental.pallas import tpu as pltpu
from jax.sharding import PartitionSpec as P

HD = 32
STEP = 10
NPARAM = 791552
CLIP_SCALE = 6.0
BETA_ONE = 0.9
BETA_TWO = 0.999
ADAM_EPS = 1e-08
DECAY_RATE = 0.05
RATE_MATRIX = 0.1
RATE_VECTOR = 0.6
GRID = 14
SPLIT = 7
CELLS = 196
PAD = 112
D = 256
FF = 1024
NORM_EPS = 1e-5
BF = jnp.bfloat16
F32 = jnp.float32
SCALE = HD ** -0.5
LOG2E = 1.4426950408889634


def slot_of(branch, cell):
    row, col = divmod(cell, GRID)
    if branch == 0:
        return row * 16 + col
    stripe, inner = divmod(col, SPLIT)
    return stripe * PAD + row * 8 + inner


def spread_tables():
    into = np.zeros((2, 4, 2 * PAD, 208), np.float32)
    for branch in range(2):
        for cell in range(CELLS):
            for j in range(4):
                into[branch, j, slot_of(branch, cell), cell + 4 * j] = 1.0
    return into.reshape(8, 2 * PAD, 208), into.transpose(0, 1, 3, 2).reshape(8, 208, 2 * PAD)


def key_mask():
    mask = np.full((2, PAD, 128), -1e30, np.float32)
    for branch in range(2):
        for cell in range(CELLS):
            slot = slot_of(branch, cell)
            if slot < PAD:
                mask[branch, slot] = 0.0
    return mask


def lane_table(tensor):
    heads = 4 // tensor
    assert heads == 1
    table = np.zeros((512, 512), np.float32)
    for t in range(4):
        for j in range(2):
            for b in range(2):
                for e in range(HD):
                    table[t * 128 + j * 64 + b * 32 + e, b * 256 + j * 128 + t * 32 + e] = 1.0
    return table


def dot(a, b):
    return lax.dot_general(a, b, (((1,), (0,)), ((), ())), preferred_element_type=F32)


def dot_nt(a, b):
    return lax.dot_general(a, b, (((1,), (1,)), ((), ())), preferred_element_type=F32)


def norm_stats(v):
    centre = jnp.mean(v, -1, keepdims=True)
    centred = v - centre
    spread = jnp.mean(centred * centred, -1, keepdims=True)
    rate = lax.rsqrt(spread + NORM_EPS)
    return centred * rate, rate


def norm_back(grad, gain, xhat, rate):
    gx = grad * gain
    first = jnp.mean(gx, -1, keepdims=True)
    second = jnp.mean(gx * xhat, -1, keepdims=True)
    return rate * (gx - first - xhat * second)


def fold8(v):
    return jnp.sum(v.reshape(v.shape[0] // 8, 8, v.shape[1]), axis=0)


def gelu_pair(h):
    e = jnp.exp2(h * h * (-0.5 * LOG2E))
    t = 1.0 / (1.0 + (0.3275911 * math.sqrt(0.5)) * jnp.abs(h))
    poly = t * (0.5 * 0.254829592 + t * (0.5 * -0.284496736 + t * (0.5 * 1.421413741 + t * (0.5 * -1.453152027 + t * (0.5 * 1.061405429)))))
    tail = poly * e
    phi = jnp.where(h < 0, tail, 1.0 - tail)
    return h * phi, phi + h * e * (1.0 / math.sqrt(2 * math.pi))


def head_masks():
    lane = lax.broadcasted_iota(jnp.int32, (128, 128), 1) // HD
    return [jnp.where(lane == h, 1.0, 0.0).astype(BF) for h in range(4)]


def head_blocks(z, masks):
    zp = jnp.concatenate([z, jnp.zeros((16, 128), BF)], 0)
    return [zp * masks[h] for h in range(4)]


def col_shift(v):
    return pltpu.roll(v, 1, 0), v, pltpu.roll(v, PAD - 1, 0)


def row_up(u, pitch):
    return jnp.concatenate([u[pitch:], jnp.zeros((pitch, 128), F32)], 0)


def row_down(u, pitch):
    return jnp.concatenate([jnp.zeros((pitch, 128), F32), u[:-pitch]], 0)


def window_sum(v, taps, pitch):
    cols = col_shift(v)
    rows = [sum(taps[3 * i + j] * cols[j] for j in range(3)) for i in range(3)]
    return row_down(rows[0], pitch) + rows[1] + row_up(rows[2], pitch)


def window_sum_back(d, taps, pitch):
    cols = col_shift(d)
    rows = [sum(taps[3 * i + j] * cols[2 - j] for j in range(3)) for i in range(3)]
    return row_up(rows[0], pitch) + rows[1] + row_down(rows[2], pitch)


def tap_sums(d, v, pitch):
    cols = col_shift(v)
    out = []
    for i in range(3):
        moved = row_up(d, pitch) if i == 0 else (d if i == 1 else row_down(d, pitch))
        for j in range(3):
            out.append(fold8(moved * cols[j]))
    return out


MT = 336
NT_TILES = 7


def compute_kernel(
    x_ref, cot_ref, w_ref, norm_ref, lepe_ref, bias_ref, into_ref, outof_ref, mask_ref, lane_ref,
    out_ref, ig_ref, grad_ref, small_ref,
    fc1_s, fc2_s, wcat_s, proj_s, lepe_s, n1_s, q_s, k_s, v_s, a_s, p_s, att_s, n2_s, act_s, gh_s, gb_s, ga_s, do_s, dqkv_s, acc_s, tacc_s, pack_s,
):
    rows = x_ref.shape[0]
    images = rows // CELLS
    chunks = images // 4

    parts, depth = w_ref.shape[0], w_ref.shape[2]
    for t in range(4):
        for n in range(parts):
            at = slice(n * depth, (n + 1) * depth)
            fc1_s[at, t * 256:(t + 1) * 256] = w_ref[n, t, :, 0:256]
            fc2_s[at, t * 256:(t + 1) * 256] = w_ref[n, t, :, 256:512]
            pack_s[0, at, t * 128:(t + 1) * 128] = w_ref[n, t, :, 512:640]
            pack_s[1, at, t * 128:(t + 1) * 128] = w_ref[n, t, :, 640:768]
    for half in range(2):
        work = dot(pack_s[half], lane_ref[...]).astype(BF)
        for b in range(2):
            if half == 0:
                wcat_s[:, b * 384:b * 384 + 256] = work[:, b * 256:b * 256 + 256]
            else:
                wcat_s[:, b * 384 + 256:b * 384 + 384] = work[:, b * 256:b * 256 + 128]
                proj_s[:, b * 128:b * 128 + 128] = work[:, b * 256 + 128:b * 256 + 256]
    lp = lepe_ref[...]
    lepe_s[0:10, :] = jnp.concatenate([lp[:, h * 64 + b * 32:h * 64 + b * 32 + 32] for b in range(2) for h in range(4)], 1)
    acc_s[...] = jnp.zeros_like(acc_s)
    tacc_s[...] = jnp.zeros_like(tacc_s)

    @pl.loop(0, NT_TILES)
    def _(i):
        sl = pl.ds(pl.multiple_of(i * MT, 16), MT)
        xhat, rate = norm_stats(x_ref[sl, :].astype(F32))
        n1_s[sl, :] = (xhat * norm_ref[0:1, :] + norm_ref[1:2, :]).astype(BF)

    @pl.loop(0, chunks)
    def _(c):
        for j in range(4):
            window = n1_s[pl.ds(pl.multiple_of(c * 784 + 192 * j, 16), 208), :]
            for b in range(2):
                spread = dot(into_ref[b * 4 + j], window).astype(BF)
                qkv = dot(spread, wcat_s[:, b * 384:(b + 1) * 384]).astype(BF)
                for s in range(2):
                    at = c * 8 + j * 2 + s
                    q_s[b, at] = qkv[s * PAD:(s + 1) * PAD, 0:128]
                    k_s[b, at] = qkv[s * PAD:(s + 1) * PAD, 128:256]
                    v_s[b, at] = qkv[s * PAD:(s + 1) * PAD, 256:384]

    masks = head_masks()

    @pl.loop(0, images * 2)
    def _(i):
        for b in range(2):
            pitch = 16 - 8 * b
            q, k, v = q_s[b, i], k_s[b, i], v_s[b, i]
            qb = head_blocks(q, masks)
            vt = jnp.transpose(v)
            ots = []
            for h in range(4):
                s = dot_nt(k, qb[h]) * (SCALE * LOG2E) + mask_ref[b]
                m = jnp.max(s, 0, keepdims=True)
                p = jnp.exp2(s - m)
                r = 1.0 / jnp.sum(p, 0, keepdims=True)
                pn = (p * r).astype(BF)
                p_s[b, i, :, h * 128:(h + 1) * 128] = pn
                ots.append(dot(vt[h * HD:(h + 1) * HD], pn))
            mixed = jnp.transpose(jnp.concatenate(ots, 0))[:PAD]
            taps = [lepe_s[n:n + 1, b * 128:(b + 1) * 128] for n in range(10)]
            local = window_sum(v.astype(F32), taps, pitch) + taps[9]
            a_s[b, i] = (mixed + local).astype(BF)

    def gather_rows(source, c, dest, lanes):
        for b in range(2):
            tail = None
            for j in range(4):
                both = jnp.concatenate([source(b, c * 8 + j * 2), source(b, c * 8 + j * 2 + 1)], 0)
                got = dot(outof_ref[b * 4 + j], both)
                head = got[0:16] if tail is None else got[0:16] + tail
                base = c * 784 + 192 * j
                cols = slice(b * lanes, (b + 1) * lanes)
                dest[pl.ds(pl.multiple_of(base, 16), 16), cols] = head.astype(BF)
                dest[pl.ds(pl.multiple_of(base + 16, 16), 176), cols] = got[16:192].astype(BF)
                tail = got[192:208]
                if j == 3:
                    dest[pl.ds(pl.multiple_of(base + 192, 16), 16), cols] = tail.astype(BF)

    @pl.loop(0, chunks)
    def _(c):
        gather_rows(lambda b, at: a_s[b, at], c, att_s, 128)

    @pl.loop(0, NT_TILES)
    def _(i):
        sl = pl.ds(pl.multiple_of(i * MT, 16), MT)
        one = dot_nt(att_s[sl, :], proj_s[...]) + norm_ref[2:3, :]
        middle = x_ref[sl, :].astype(F32) + one
        xhat, rate = norm_stats(middle)
        n2 = (xhat * norm_ref[3:4, :] + norm_ref[4:5, :]).astype(BF)
        n2_s[sl, :] = n2
        cot = cot_ref[sl, :]
        two = jnp.zeros((MT, D), F32)
        gn = jnp.zeros((MT, D), F32)
        for f in range(4):
            fs = slice(f * 256, (f + 1) * 256)
            hidden = dot(n2, fc1_s[:, fs]) + jnp.concatenate([bias_ref[2 * f:2 * f + 1, :], bias_ref[2 * f + 1:2 * f + 2, :]], 1)
            gelu, slope = gelu_pair(hidden)
            act = gelu.astype(BF)
            act_s[sl, fs] = act
            two = two + dot_nt(act, fc2_s[:, fs])
            gh_f = dot(cot, fc2_s[:, fs]) * slope
            gh = gh_f.astype(BF)
            gh_s[sl, fs] = gh
            acc_s[10 + f] += fold8(gh.astype(F32))
            gn = gn + dot_nt(gh, fc1_s[:, fs])
        two = two + norm_ref[5:6, :]
        result = middle + two
        out_ref[sl, :] = result.astype(BF)
        acc_s[6] += fold8(one * one)
        acc_s[7] += fold8(middle * middle)
        acc_s[8] += fold8(two * two)
        acc_s[9] += fold8(result * result)
        cotf = cot.astype(F32)
        acc_s[5] += fold8(cotf)
        acc_s[3] += fold8(gn * xhat)
        acc_s[4] += fold8(gn)
        gm = cotf + norm_back(gn, norm_ref[3:4, :], xhat, rate)
        ig_ref[sl, :] = gm
        gb = gm.astype(BF)
        gb_s[sl, :] = gb
        acc_s[2] += fold8(gb.astype(F32))
        ga_s[sl, :] = dot(gb, proj_s[...]).astype(BF)

    def weight_grad(left, right):
        return lax.dot_general(left, right, (((0,), (0,)), ((), ())), preferred_element_type=F32)

    def put_rows(value, t, off):
        for n in range(parts):
            grad_ref[n, t, :, off:off + value.shape[1]] = value[n * depth:(n + 1) * depth]

    def put_mlp(left, right, off):
        for t in range(4):
            value = weight_grad(left[...], right[:, t * 256:(t + 1) * 256]).astype(BF)
            put_rows(value, t, off)

    put_mlp(n2_s, gh_s, 0)
    put_mlp(cot_ref, act_s, 256)

    @pl.loop(0, chunks)
    def _(c):
        for j in range(4):
            window = ga_s[pl.ds(pl.multiple_of(c * 784 + 192 * j, 16), 208), :]
            for b in range(2):
                spread = dot(into_ref[b * 4 + j], window[:, b * 128:(b + 1) * 128]).astype(BF)
                for s in range(2):
                    do_s[b, c * 8 + j * 2 + s] = spread[s * PAD:(s + 1) * PAD]

    @pl.loop(0, images * 2)
    def _(i):
        for b in range(2):
            pitch = 16 - 8 * b
            q, k, v, do = q_s[b, i], k_s[b, i], v_s[b, i], do_s[b, i]
            qb = head_blocks(q, masks)
            db = head_blocks(do, masks)
            kt = jnp.transpose(k)
            dqt = []
            dk = jnp.zeros((PAD, 128), F32)
            dv = jnp.zeros((PAD, 128), F32)
            for h in range(4):
                pn = p_s[b, i, :, h * 128:(h + 1) * 128]
                pf = pn.astype(F32)
                t = pf * dot_nt(v, db[h])
                ds = (t - pf * jnp.sum(t, 0, keepdims=True)).astype(BF)
                dv = dv + dot(pn, db[h])
                dk = dk + dot(ds, qb[h])
                dqt.append(dot(kt[h * HD:(h + 1) * HD], ds))
            dq = jnp.transpose(jnp.concatenate(dqt, 0))[:PAD]
            taps = [lepe_s[n:n + 1, b * 128:(b + 1) * 128] for n in range(10)]
            dof, vf = do.astype(F32), v.astype(F32)
            dv = dv + window_sum_back(dof, taps, pitch)
            for n, part in enumerate(tap_sums(dof, vf, pitch)):
                tacc_s[b, n] += part
            tacc_s[b, 9] += fold8(dof)
            q_s[b, i] = (dq * SCALE).astype(BF)
            k_s[b, i] = (dk * SCALE).astype(BF)
            v_s[b, i] = dv.astype(BF)

    @pl.loop(0, chunks)
    def _(c):
        gather_rows(lambda b, at: jnp.concatenate([q_s[b, at], k_s[b, at], v_s[b, at]], 1), c, dqkv_s, 384)

    @pl.loop(0, NT_TILES)
    def _(i):
        sl = pl.ds(pl.multiple_of(i * MT, 16), MT)
        gn = dot_nt(dqkv_s[sl, :], wcat_s[...])
        xhat, rate = norm_stats(x_ref[sl, :].astype(F32))
        acc_s[0] += fold8(gn * xhat)
        acc_s[1] += fold8(gn)
        ig_ref[sl, :] = ig_ref[sl, :] + norm_back(gn, norm_ref[0:1, :], xhat, rate)

    gw = weight_grad(n1_s[...], dqkv_s[...]).astype(BF)
    gp = weight_grad(gb_s[...], att_s[...]).astype(BF)
    work0 = jnp.concatenate([gw[:, 0:256], gw[:, 384:640]], 1)
    work1 = jnp.concatenate([gw[:, 256:384], gp[:, 0:128], gw[:, 640:768], gp[:, 128:256]], 1)
    for half, work in enumerate((work0, work1)):
        packed = dot_nt(work, lane_ref[...]).astype(BF)
        for t in range(4):
            put_rows(packed[:, t * 128:(t + 1) * 128], t, 512 + 128 * half)
    for n in range(14):
        small_ref[n:n + 1, :] = jnp.sum(acc_s[n], 0, keepdims=True)
    for n in range(10):
        row = jnp.concatenate([jnp.sum(tacc_s[b, n], 0, keepdims=True) for b in range(2)], 1)
        small_ref[14 + n:15 + n, :] = jnp.concatenate([row[:, b * 128 + h * 32:b * 128 + h * 32 + 32] for h in range(4) for b in range(2)], 1)


def compute_call(x, cot, w, norm, lepe, bias):
    rows = x.shape[0]
    n = rows // CELLS * 2
    into, outof = spread_tables()
    args = (x, cot, w, norm, lepe, bias, jnp.asarray(into, BF), jnp.asarray(outof, BF), jnp.asarray(key_mask()), jnp.asarray(lane_table(4), BF))
    V = pltpu.VMEM
    return pl.pallas_call(
        compute_kernel,
        out_shape=(
            jax.ShapeDtypeStruct((rows, D), BF),
            jax.ShapeDtypeStruct((rows, D), F32),
            jax.ShapeDtypeStruct(w.shape, BF),
            jax.ShapeDtypeStruct((24, D), F32),
        ),
        in_specs=[pl.BlockSpec(memory_space=V)] * len(args),
        out_specs=tuple([pl.BlockSpec(memory_space=V)] * 4),
        scratch_shapes=[
            V((D, FF), BF), V((D, FF), BF), V((D, 768), BF), V((D, D), BF), V((16, D), F32),
            V((rows, D), BF),
            V((2, n, PAD, 128), BF), V((2, n, PAD, 128), BF), V((2, n, PAD, 128), BF), V((2, n, PAD, 128), BF),
            V((2, n, PAD, 512), BF),
            V((rows, D), BF), V((rows, D), BF), V((rows, FF), BF), V((rows, FF), BF), V((rows, D), BF), V((rows, D), BF),
            V((2, n, PAD, 128), BF), V((rows, 768), BF),
            V((14, 8, D), F32), V((2, 10, 8, 128), F32), V((2, D, 512), BF),
        ],
        compiler_params=pltpu.CompilerParams(vmem_limit_bytes=60 * 2**20),
    )(*args)


MESH = pl.DeviceIdType.MESH


def ring_peers(batch, tensor):
    me_b, me_t = lax.axis_index("batch"), lax.axis_index("tensor")
    along_b = [(lax.rem(me_b + k, batch), me_t) for k in range(1, batch)]
    along_t = [(me_b, lax.rem(me_t + k, tensor)) for k in range(1, tensor)]
    return me_b, me_t, along_b, along_t


def greet(peers):
    barrier = pltpu.get_barrier_semaphore()
    for peer in peers:
        pl.semaphore_signal(barrier, inc=1, device_id=peer, device_id_type=MESH)
    pl.semaphore_wait(barrier, len(peers))


def gather_kernel(batch, tensor, qkv_ref, proj_ref, fc1_ref, fc2_ref, full_ref, own_s, keep_sem, send_t, recv_t, send_b, recv_b):
    me_b, me_t, along_b, along_t = ring_peers(batch, tensor)
    own_s[:, 0:256] = fc1_ref[...].astype(BF)
    own_s[:, 256:512] = fc2_ref[...].astype(BF)
    own_s[:, 512:640] = jnp.concatenate([qkv_ref[0], qkv_ref[1]], 1).astype(BF)
    own_s[:, 640:768] = jnp.concatenate([qkv_ref[2], proj_ref[...]], 1).astype(BF)
    greet(along_b + along_t)
    mine = full_ref.at[me_b, me_t]
    keep = pltpu.make_async_copy(own_s, mine, keep_sem)
    keep.start()
    across = []
    for k, peer in enumerate(along_t):
        copy = pltpu.make_async_remote_copy(src_ref=own_s, dst_ref=mine, send_sem=send_t.at[k], recv_sem=recv_t.at[k], device_id=peer, device_id_type=MESH)
        copy.start()
        across.append(copy)
    passed = []
    for n in range(tensor):
        if n == 0:
            source, slot = own_s, me_t
        else:
            across[n - 1].wait_recv()
            slot = lax.rem(me_t + tensor - n, tensor)
            source = full_ref.at[me_b, slot]
        for k, peer in enumerate(along_b):
            copy = pltpu.make_async_remote_copy(src_ref=source, dst_ref=full_ref.at[me_b, slot], send_sem=send_b.at[n, k], recv_sem=recv_b.at[n, k], device_id=peer, device_id_type=MESH)
            copy.start()
            passed.append(copy)
    keep.wait()
    for copy in across:
        copy.wait_send()
    for copy in passed:
        copy.wait()


def gather_call(batch, tensor, qkv, proj, fc1, fc2):
    rows = fc1.shape[0]
    V = pltpu.VMEM
    dma = pltpu.SemaphoreType.DMA
    return pl.pallas_call(
        functools.partial(gather_kernel, batch, tensor),
        out_shape=jax.ShapeDtypeStruct((batch, tensor, rows, 768), BF),
        in_specs=[pl.BlockSpec(memory_space=V)] * 4,
        out_specs=pl.BlockSpec(memory_space=V),
        scratch_shapes=[V((rows, 768), BF), dma, dma((tensor - 1,)), dma((tensor - 1,)), dma((tensor, batch - 1)), dma((tensor, batch - 1))],
        compiler_params=pltpu.CompilerParams(collective_id=0, has_side_effects=True, vmem_limit_bytes=60 * 2**20),
    )(qkv, proj, fc1, fc2)


def reduce_kernel(
    batch, tensor, grad_ref, small_ref, shard_ref, total_ref, norm_ref,
    in_b, mid_s, in_t, small_b, small_t, square_b, square_t,
    send_b, recv_b, send_t, recv_t, send_sb, recv_sb, send_st, recv_st, send_qb, recv_qb, send_qt, recv_qt,
):
    me_b, me_t, along_b, along_t = ring_peers(batch, tensor)
    greet(along_b + along_t)

    def push(source, dest, peer, send_sem, recv_sem):
        copy = pltpu.make_async_remote_copy(src_ref=source, dst_ref=dest, send_sem=send_sem, recv_sem=recv_sem, device_id=peer, device_id_type=MESH)
        copy.start()
        return copy

    first = [push(grad_ref.at[peer[0]], in_b.at[k], peer, send_b.at[k], recv_b.at[k]) for k, peer in enumerate(along_b)]
    small_b[me_b] = small_ref[...]
    small_first = [push(small_ref, small_b.at[me_b], peer, send_sb.at[k], recv_sb.at[k]) for k, peer in enumerate(along_b)]
    for copy in small_first:
        copy.wait()
    part = small_b[0]
    for n in range(1, batch):
        part = part + small_b[n]
    total_ref[...] = part
    small_t[me_t] = part
    small_second = [push(total_ref, small_t.at[me_t], peer, send_st.at[k], recv_st.at[k]) for k, peer in enumerate(along_t)]
    for copy in first:
        copy.wait()

    for n in range(tensor):
        value = grad_ref[me_b, n].astype(F32)
        for k in range(batch - 1):
            value = value + in_b[k, n].astype(F32)
        mid_s[n] = value.astype(mid_s.dtype)

    second = [push(mid_s.at[peer[1]], in_t.at[k], peer, send_t.at[k], recv_t.at[k]) for k, peer in enumerate(along_t)]
    for copy in small_second:
        copy.wait()
    part = small_t[0]
    for n in range(1, tensor):
        part = part + small_t[n]
    total_ref[...] = part
    for copy in second:
        copy.wait()
    shard = mid_s[me_t].astype(F32)
    for k in range(tensor - 1):
        shard = shard + in_t[k].astype(F32)
    shard_ref[...] = shard
    squares = fold8(shard * shard)
    lanes = squares[:, 0:128]
    for n in range(1, 6):
        lanes = lanes + squares[:, n * 128:(n + 1) * 128]
    square_b[me_b] = lanes
    norm_ref[...] = lanes
    last = [push(norm_ref, square_b.at[me_b], peer, send_qb.at[k], recv_qb.at[k]) for k, peer in enumerate(along_b)]
    for copy in last:
        copy.wait()
    lanes = square_b[0]
    for n in range(1, batch):
        lanes = lanes + square_b[n]
    square_t[me_t] = lanes
    norm_ref[...] = lanes
    last = [push(norm_ref, square_t.at[me_t], peer, send_qt.at[k], recv_qt.at[k]) for k, peer in enumerate(along_t)]
    for copy in last:
        copy.wait()
    lanes = square_t[0]
    for n in range(1, tensor):
        lanes = lanes + square_t[n]
    matrix = jnp.sum(jnp.sum(lanes, 0, keepdims=True), 1, keepdims=True)
    vectors = total_ref[...]
    row = lax.broadcasted_iota(jnp.int32, vectors.shape, 0)
    vectors = jnp.where((row < 6) | (row >= 10), vectors, 0.0)
    vector = jnp.sum(jnp.sum(vectors * vectors, 0, keepdims=True), 1, keepdims=True)
    norm_ref[...] = jnp.broadcast_to(jnp.sqrt(matrix + vector), (8, 128))


def reduce_call(batch, tensor, grad, small, mid=BF):
    rows = grad.shape[2]
    V = pltpu.VMEM
    dma = pltpu.SemaphoreType.DMA
    pair = lambda n: [dma((n - 1,)), dma((n - 1,))]
    return pl.pallas_call(
        functools.partial(reduce_kernel, batch, tensor),
        out_shape=(jax.ShapeDtypeStruct((rows, 768), F32), jax.ShapeDtypeStruct((24, 256), F32), jax.ShapeDtypeStruct((8, 128), F32)),
        in_specs=[pl.BlockSpec(memory_space=V)] * 2,
        out_specs=tuple([pl.BlockSpec(memory_space=V)] * 3),
        scratch_shapes=[
            V((batch - 1, tensor, rows, 768), BF), V((tensor, rows, 768), mid), V((tensor - 1, rows, 768), mid),
            V((batch, 24, 256), F32), V((tensor, 24, 256), F32), V((batch, 8, 128), F32), V((tensor, 8, 128), F32),
        ] + pair(batch) + pair(tensor) + pair(batch) + pair(tensor) + pair(batch) + pair(tensor),
        compiler_params=pltpu.CompilerParams(collective_id=1, has_side_effects=True, vmem_limit_bytes=60 * 2**20),
    )(grad, small)


def adam(master, first, second, clipped, rate, decay):
    first = BETA_ONE * first + (1.0 - BETA_ONE) * clipped
    second = BETA_TWO * second + (1.0 - BETA_TWO) * clipped * clipped
    hat = first * (1.0 / (1.0 - BETA_ONE**STEP))
    spread = second * (1.0 / (1.0 - BETA_TWO**STEP))
    return master - rate * (hat / (jnp.sqrt(spread) + ADAM_EPS) + decay * master), first, second


def update_kernel(
    all_tokens, shard_ref, total_ref, norm_ref,
    qkv_w, qkv_m, proj_w, proj_m, fc1_w, fc1_m, fc2_w, fc2_m, norm_w, norm_m, lepe_w, lepe_m, bias_w, bias_m,
    qkv_g, qkv_n, qkv_l, qkv_o, proj_g, proj_n, proj_l, proj_o, fc1_g, fc1_n, fc1_l, fc1_o, fc2_g, fc2_n, fc2_l, fc2_o,
    norm_g, norm_n, norm_o, lepe_g, lepe_n, lepe_o, bias_g, bias_n, bias_o, size_o, rms_o,
):
    size = norm_ref[0:1, 0:1]
    factor = jnp.minimum(1.0, CLIP_SCALE * math.sqrt(NPARAM) / (size + 1e-06))
    size_o[...] = size

    def one(grad, w, m, g_o, n_o, l_o, m_o, at, rate, decay, pair=lambda n, at: (n,) + at):
        clipped = grad * factor
        new, first, second = adam(w[at], m[pair(0, at)], m[pair(1, at)], clipped, rate, decay)
        g_o[at] = clipped
        n_o[at] = new
        if l_o is not None:
            l_o[at] = new.astype(BF)
        m_o[pair(0, at)] = first
        m_o[pair(1, at)] = second

    every = (slice(None), slice(None))
    middle = lambda n, at: (at[0], n, at[1])
    one(shard_ref[:, 0:256], fc1_w, fc1_m, fc1_g, fc1_n, fc1_l, fc1_o, every, RATE_MATRIX, DECAY_RATE)
    one(shard_ref[:, 256:512], fc2_w, fc2_m, fc2_g, fc2_n, fc2_l, fc2_o, every, RATE_MATRIX, DECAY_RATE)
    for j in range(3):
        one(shard_ref[:, 512 + 64 * j:576 + 64 * j], qkv_w, qkv_m, qkv_g, qkv_n, qkv_l, qkv_o, (j,) + every, RATE_MATRIX, DECAY_RATE)
    one(shard_ref[:, 704:768], proj_w, proj_m, proj_g, proj_n, proj_l, proj_o, every, RATE_MATRIX, DECAY_RATE)
    one(total_ref[0:6], norm_w, norm_m, norm_g, norm_n, None, norm_o, every, RATE_VECTOR, 0.0, middle)
    one(total_ref[14:24], lepe_w, lepe_m, lepe_g, lepe_n, None, lepe_o, every, RATE_VECTOR, 0.0, middle)
    for f in range(8):
        at = (slice(f, f + 1), slice(None))
        part = total_ref[10 + f // 2:11 + f // 2, 128 * (f % 2):128 * (f % 2) + 128]
        one(part, bias_w, bias_m, bias_g, bias_n, None, bias_o, at, RATE_VECTOR, 0.0, middle)
    lane = lax.broadcasted_iota(jnp.int32, (1, 4), 1)
    sums = jnp.zeros((1, 4), F32)
    for n in range(4):
        sums = jnp.where(lane == n, jnp.sum(total_ref[6 + n:7 + n], 1, keepdims=True), sums)
    rms_o[...] = jnp.sqrt(sums * (1.0 / (all_tokens * D)))


def update_call(all_tokens, shard, total, norm, arrays):
    V = pltpu.VMEM
    like = lambda a, dt=F32: jax.ShapeDtypeStruct(a.shape, dt)
    outs = []
    for n in range(4):
        w, m = arrays[2 * n], arrays[2 * n + 1]
        outs += [like(w), like(w), like(w, BF), like(m)]
    for n in range(4, 7):
        w, m = arrays[2 * n], arrays[2 * n + 1]
        outs += [like(w), like(w), like(m)]
    outs += [jax.ShapeDtypeStruct((1, 1), F32), jax.ShapeDtypeStruct((1, 4), F32)]
    return list(pl.pallas_call(
        functools.partial(update_kernel, all_tokens),
        out_shape=tuple(outs),
        in_specs=[pl.BlockSpec(memory_space=V)] * (3 + len(arrays)),
        out_specs=tuple([pl.BlockSpec(memory_space=V)] * len(outs)),
        compiler_params=pltpu.CompilerParams(vmem_limit_bytes=60 * 2**20),
    )(shard, total, norm, *arrays))


def flip(a):
    return jnp.swapaxes(a, -1, -2)


def shards(block_input, cotangent, *arrays):
    batch, tensor = lax.axis_size("batch"), lax.axis_size("tensor")
    arrays = list(arrays)
    for n in (2, 3, 6, 7):
        arrays[n] = flip(arrays[n])
    arrays[9], arrays[11] = jnp.swapaxes(arrays[9], 0, 1), jnp.swapaxes(arrays[11], 0, 1)
    arrays[12], arrays[13] = arrays[12].reshape(8, 128), jnp.swapaxes(arrays[13].reshape(2, 8, 128), 0, 1)
    qkv, _, proj, _, fc1, _, fc2, _, norm, _, lepe, _, bias, _ = arrays
    full = gather_call(batch, tensor, qkv, proj, fc1, fc2)
    output, input_grad, grads, small = compute_call(block_input, cotangent, full, norm, lepe, bias)
    shard, total, size = reduce_call(batch, tensor, grads, small)
    got = update_call(block_input.shape[0] * batch * tensor, shard, total, size, arrays)
    for n in (4, 5, 6, 7, 12, 13, 14, 15):
        got[n] = flip(got[n])
    got[18], got[21] = jnp.swapaxes(got[18], 0, 1), jnp.swapaxes(got[21], 0, 1)
    got[22], got[23], got[24] = got[22].reshape(1024), got[23].reshape(1024), jnp.swapaxes(got[24], 0, 1).reshape(2, 1024)
    got[25], got[26] = got[25].reshape(()), got[26].reshape(4)
    return (output, input_grad, *got)


def solution(mesh):
    token, matrix, moment = P(("batch", "tensor"), None), P("batch", "tensor"), P(None, "batch", "tensor")
    back, back_moment = P("tensor", "batch"), P(None, "tensor", "batch")
    stack, stack_moment = P(None, "batch", "tensor"), P(None, None, "batch", "tensor")
    return jax.shard_map(
        shards,
        mesh=mesh,
        in_specs=(token, token, stack, stack_moment, back, back_moment, matrix, moment, back, back_moment) + (P(),) * 6,
        out_specs=(token, token) + (stack,) * 3 + (stack_moment,) + (back,) * 3 + (back_moment,) + (matrix,) * 3 + (moment,) + (back,) * 3 + (back_moment,) + (P(),) * 11,
        check_vma=False,
    )
```

```python
import functools, math
import numpy as np
import jax, jax.numpy as jnp
from jax import lax
from jax.experimental import pallas as pl
from jax.experimental.pallas import tpu as pltpu
from jax.sharding import PartitionSpec as P

HD = 32
STEP = 10
NPARAM = 791552
CLIP_SCALE = 6.0
BETA_ONE = 0.9
BETA_TWO = 0.999
ADAM_EPS = 1e-08
DECAY_RATE = 0.05
RATE_MATRIX = 0.1
RATE_VECTOR = 0.6
GRID = 14
SPLIT = 7
CELLS = 196
PAD = 112
D = 256
FF = 1024
NORM_EPS = 1e-5
BF = jnp.bfloat16
F32 = jnp.float32
SCALE = HD ** -0.5
LOG2E = 1.4426950408889634


def slot_of(branch, cell):
    row, col = divmod(cell, GRID)
    if branch == 0:
        return row * 16 + col
    stripe, inner = divmod(col, SPLIT)
    return stripe * PAD + row * 8 + inner


def spread_tables():
    into = np.zeros((2, 4, 2 * PAD, 208), np.float32)
    for branch in range(2):
        for cell in range(CELLS):
            for j in range(4):
                into[branch, j, slot_of(branch, cell), cell + 4 * j] = 1.0
    return into.reshape(8, 2 * PAD, 208), into.transpose(0, 1, 3, 2).reshape(8, 208, 2 * PAD)


def key_mask():
    mask = np.full((2, PAD, 128), -1e30, np.float32)
    for branch in range(2):
        for cell in range(CELLS):
            slot = slot_of(branch, cell)
            if slot < PAD:
                mask[branch, slot] = 0.0
    return mask


def lane_table(tensor):
    heads = 4 // tensor
    assert heads == 1
    table = np.zeros((512, 512), np.float32)
    for t in range(4):
        for j in range(2):
            for b in range(2):
                for e in range(HD):
                    table[t * 128 + j * 64 + b * 32 + e, b * 256 + j * 128 + t * 32 + e] = 1.0
    return table


def dot(a, b):
    return lax.dot_general(a, b, (((1,), (0,)), ((), ())), preferred_element_type=F32)


def dot_nt(a, b):
    return lax.dot_general(a, b, (((1,), (1,)), ((), ())), preferred_element_type=F32)


def norm_stats(v):
    centre = jnp.mean(v, -1, keepdims=True)
    centred = v - centre
    spread = jnp.mean(centred * centred, -1, keepdims=True)
    rate = lax.rsqrt(spread + NORM_EPS)
    return centred * rate, rate


def norm_back(grad, gain, xhat, rate):
    gx = grad * gain
    first = jnp.mean(gx, -1, keepdims=True)
    second = jnp.mean(gx * xhat, -1, keepdims=True)
    return rate * (gx - first - xhat * second)


def fold8(v):
    return jnp.sum(v.reshape(v.shape[0] // 8, 8, v.shape[1]), axis=0)


def gelu_pair(h):
    e = jnp.exp2(h * h * (-0.5 * LOG2E))
    t = 1.0 / (1.0 + (0.3275911 * math.sqrt(0.5)) * jnp.abs(h))
    poly = t * (0.5 * 0.254829592 + t * (0.5 * -0.284496736 + t * (0.5 * 1.421413741 + t * (0.5 * -1.453152027 + t * (0.5 * 1.061405429)))))
    tail = poly * e
    phi = jnp.where(h < 0, tail, 1.0 - tail)
    return h * phi, phi + h * e * (1.0 / math.sqrt(2 * math.pi))


def head_masks():
    lane = lax.broadcasted_iota(jnp.int32, (128, 128), 1) // HD
    return [jnp.where(lane == h, 1.0, 0.0).astype(BF) for h in range(4)]


def head_blocks(z, masks):
    zp = jnp.concatenate([z, jnp.zeros((16, 128), BF)], 0)
    return [zp * masks[h] for h in range(4)]


def col_shift(v):
    return pltpu.roll(v, 1, 0), v, pltpu.roll(v, PAD - 1, 0)


def row_up(u, pitch):
    return jnp.concatenate([u[pitch:], jnp.zeros((pitch, 128), F32)], 0)


def row_down(u, pitch):
    return jnp.concatenate([jnp.zeros((pitch, 128), F32), u[:-pitch]], 0)


def window_sum(v, taps, pitch):
    cols = col_shift(v)
    rows = [sum(taps[3 * i + j] * cols[j] for j in range(3)) for i in range(3)]
    return row_down(rows[0], pitch) + rows[1] + row_up(rows[2], pitch)


def window_sum_back(d, taps, pitch):
    cols = col_shift(d)
    rows = [sum(taps[3 * i + j] * cols[2 - j] for j in range(3)) for i in range(3)]
    return row_up(rows[0], pitch) + rows[1] + row_down(rows[2], pitch)


def tap_sums(d, v, pitch):
    cols = col_shift(v)
    out = []
    for i in range(3):
        moved = row_up(d, pitch) if i == 0 else (d if i == 1 else row_down(d, pitch))
        for j in range(3):
            out.append(fold8(moved * cols[j]))
    return out


MT = 336
NT_TILES = 7
MESH = pl.DeviceIdType.MESH


def block_kernel(
    batch, tensor, linked, *refs,
):
    names = NAMES_IN + NAMES_OUT + NAMES_SCRATCH
    r = dict(zip(names, refs))
    (x_hbm, cot_hbm, qkv_ref, proj_ref, m1_ref, m2_ref, norm_ref, lepe_ref, bias_ref, into_hbm, outof_hbm, mask_ref, lane_hbm) = [r[n] for n in NAMES_IN]
    (out_hbm, ig_hbm, shard_ref, total_ref, size_ref) = [r[n] for n in NAMES_OUT]
    (x_ref, cot_ref, out_ref, ig_ref, into_ref, outof_ref, lane_ref,
     gq_s, gm_s, hq_s, hm_s, inq_s, inm_s, midq_s, midm_s, zq_s, zm_s, small_ref, smallb_s, smallt_s, sqb_s, sqt_s,
     fc1_s, fc2_s, wcat_s, proj_s, lepe_s, n1_s, q_s, k_s, v_s, a_s, p_s, att_s, n2_s, act_s, gh_s, gb_s, ga_s, do_s,
     acc_s, tacc_s, s_s, ds_s, dk_s, dv_s) = [r[n] for n in NAMES_SCRATCH[:46]]
    dq_s, dqkv_s = a_s, gh_s
    load_sem, store_sem = r["load_sem"], r["store_sem"]

    rows = x_ref.shape[0]
    images = rows // CELLS
    chunks = images // 4
    depth = m1_ref.shape[0]

    loads = []
    for n, (source, dest) in enumerate(((x_hbm, x_ref), (into_hbm, into_ref), (lane_hbm, lane_ref), (outof_hbm, outof_ref), (cot_hbm, cot_ref))):
        copy = pltpu.make_async_copy(source, dest, load_sem.at[n])
        copy.start()
        loads.append(copy)

    if linked:
        me_b, me_t = lax.axis_index("batch"), lax.axis_index("tensor")
    else:
        me_b, me_t = 0, 0
    along_b = [(lax.rem(me_b + k, batch), me_t) for k in range(1, batch)]
    along_t = [(me_b, lax.rem(me_t + k, tensor)) for k in range(1, tensor)]

    class Push:
        def __init__(self, source, dest, peer, send, recv):
            self.copy = None
            if linked:
                self.copy = pltpu.make_async_remote_copy(src_ref=source, dst_ref=dest, send_sem=send, recv_sem=recv, device_id=peer, device_id_type=MESH)
                self.copy.start()

        def wait_recv(self):
            if self.copy is not None:
                self.copy.wait_recv()

        def wait_send(self):
            if self.copy is not None:
                self.copy.wait_send()

    sent = []

    def push(source, dest, peer, sems, *at):
        got = Push(source, dest, peer, r[sems + "_s"].at[at], r[sems + "_r"].at[at])
        sent.append(got)
        return got

    def arrive(copies):
        for copy in copies:
            copy.wait_recv()

    gq_s[me_b, me_t] = jnp.concatenate([qkv_ref[0], qkv_ref[1], qkv_ref[2], proj_ref[...]], 1).astype(BF)
    gm_s[me_b, me_t, :, 0:256] = m1_ref[...].astype(BF)
    gm_s[me_b, me_t, :, 256:512] = m2_ref[...].astype(BF)
    if linked:
        barrier = pltpu.get_barrier_semaphore()
        for peer in along_b + along_t:
            pl.semaphore_signal(barrier, inc=1, device_id=peer, device_id_type=MESH)
        pl.semaphore_wait(barrier, len(along_b) + len(along_t))
    got_q, got_m = [], []
    over = {}
    for name, ref in (("zq", gq_s), ("zm", gm_s)):
        mine = ref.at[me_b, me_t]
        over[name] = [push(mine, mine, peer, name, k) for k, peer in enumerate(along_t)]
        if name == "zq":
            got_q += [push(mine, mine, peer, "bq", 0, k) for k, peer in enumerate(along_b)]
    acc_s[...] = jnp.zeros_like(acc_s)
    lp = lepe_ref[...]
    lepe_s[0:10, :] = jnp.concatenate([lp[:, h * 64 + b * 32:h * 64 + b * 32 + 32] for b in range(2) for h in range(4)], 1)
    for n in range(1, tensor):
        over["zq"][n - 1].wait_recv()
        slot = gq_s.at[me_b, lax.rem(me_t + tensor - n, tensor)]
        got_q += [push(slot, slot, peer, "bq", n, k) for k, peer in enumerate(along_b)]
    for n in range(tensor):
        if n > 0:
            over["zm"][n - 1].wait_recv()
        slot = gm_s.at[me_b, lax.rem(me_t + tensor - n, tensor)]
        got_m += [push(slot, slot, peer, "bm", n, k) for k, peer in enumerate(along_b)]
    loads[0].wait()

    @pl.loop(0, NT_TILES)
    def _(i):
        sl = pl.ds(pl.multiple_of(i * MT, 16), MT)
        xhat, rate = norm_stats(x_ref[sl, :].astype(F32))
        n1_s[sl, :] = (xhat * norm_ref[0:1, :] + norm_ref[1:2, :]).astype(BF)

    loads[1].wait()
    loads[2].wait()
    arrive(got_q)
    for half in range(2):
        lanes = slice(half * 128, half * 128 + 128)
        packed = jnp.concatenate([jnp.concatenate([gq_s[n, t, :, lanes] for n in range(batch)], 0) for t in range(4)], 1)
        work = dot(packed, lane_ref[...]).astype(BF)
        for b in range(2):
            if half == 0:
                wcat_s[:, b * 384:b * 384 + 256] = work[:, b * 256:b * 256 + 256]
            else:
                wcat_s[:, b * 384 + 256:b * 384 + 384] = work[:, b * 256:b * 256 + 128]
                proj_s[:, b * 128:b * 128 + 128] = work[:, b * 256 + 128:b * 256 + 256]

    @pl.loop(0, chunks)
    def _(c):
        for j in range(4):
            window = n1_s[pl.ds(pl.multiple_of(c * 784 + 192 * j, 16), 208), :]
            for b in range(2):
                spread = dot(into_ref[b * 4 + j], window).astype(BF)
                qkv = dot(spread, wcat_s[:, b * 384:(b + 1) * 384]).astype(BF)
                for s in range(2):
                    at = c * 8 + j * 2 + s
                    q_s[b, at] = qkv[s * PAD:(s + 1) * PAD, 0:128]
                    k_s[b, at] = qkv[s * PAD:(s + 1) * PAD, 128:256]
                    v_s[b, at] = qkv[s * PAD:(s + 1) * PAD, 256:384]

    masks = head_masks()

    stripes = images * 2

    def scores_stage(b, at):
        s_s[b] = dot_nt(k_s[b, at], jnp.concatenate(head_blocks(q_s[b, at], masks), 0))

    def soft_stage(b, at):
        for h in range(4):
            lanes = slice(h * 128, (h + 1) * 128)
            s = s_s[b, :, lanes] * (SCALE * LOG2E) + mask_ref[b]
            p = jnp.exp2(s - jnp.max(s, 0, keepdims=True))
            p_s[b, at, :, lanes] = (p * (1.0 / jnp.sum(p, 0, keepdims=True))).astype(BF)

    def mix_stage(b, at):
        pitch = 16 - 8 * b
        v = v_s[b, at]
        vt = jnp.transpose(v)
        ots = [dot(vt[h * HD:(h + 1) * HD], p_s[b, at, :, h * 128:(h + 1) * 128]) for h in range(4)]
        mixed = jnp.transpose(jnp.concatenate(ots, 0))[:PAD]
        taps = [lepe_s[n:n + 1, b * 128:(b + 1) * 128] for n in range(10)]
        local = window_sum(v.astype(F32), taps, pitch) + taps[9]
        a_s[b, at] = (mixed + local).astype(BF)

    @pl.loop(0, stripes + 2)
    def _(i):
        first, second, third = jnp.minimum(i, stripes - 1), jnp.clip(i - 1, 0, stripes - 1), jnp.maximum(i - 2, 0)
        for b in range(2):
            mix_stage(b, third)
            soft_stage(b, second)
            scores_stage(b, first)

    def gather_rows(source, c, dest, lanes):
        for b in range(2):
            tail = None
            for j in range(4):
                both = jnp.concatenate([source(b, c * 8 + j * 2), source(b, c * 8 + j * 2 + 1)], 0)
                got = dot(outof_ref[b * 4 + j], both)
                head = got[0:16] if tail is None else got[0:16] + tail
                base = c * 784 + 192 * j
                cols = slice(b * lanes, (b + 1) * lanes)
                dest[pl.ds(pl.multiple_of(base, 16), 16), cols] = head.astype(BF)
                dest[pl.ds(pl.multiple_of(base + 16, 16), 176), cols] = got[16:192].astype(BF)
                tail = got[192:208]
                if j == 3:
                    dest[pl.ds(pl.multiple_of(base + 192, 16), 16), cols] = tail.astype(BF)

    loads[3].wait()
    loads[4].wait()

    @pl.loop(0, chunks)
    def _(c):
        gather_rows(lambda b, at: a_s[b, at], c, att_s, 128)

    arrive(got_m)
    for t in range(4):
        for n in range(batch):
            at = slice(n * depth, (n + 1) * depth)
            fc1_s[at, t * 256:(t + 1) * 256] = gm_s[n, t, :, 0:256]
            fc2_s[at, t * 256:(t + 1) * 256] = gm_s[n, t, :, 256:512]

    @pl.loop(0, NT_TILES)
    def _(i):
        sl = pl.ds(pl.multiple_of(i * MT, 16), MT)
        one = dot_nt(att_s[sl, :], proj_s[...]) + norm_ref[2:3, :]
        middle = x_ref[sl, :].astype(F32) + one
        xhat, rate = norm_stats(middle)
        n2 = (xhat * norm_ref[3:4, :] + norm_ref[4:5, :]).astype(BF)
        n2_s[sl, :] = n2
        cot = cot_ref[sl, :]
        two = jnp.zeros((MT, D), F32)
        gn = jnp.zeros((MT, D), F32)
        for f in range(4):
            fs = slice(f * 256, (f + 1) * 256)
            hidden = dot(n2, fc1_s[:, fs]) + jnp.concatenate([bias_ref[2 * f:2 * f + 1, :], bias_ref[2 * f + 1:2 * f + 2, :]], 1)
            gelu, slope = gelu_pair(hidden)
            act = gelu.astype(BF)
            act_s[sl, fs] = act
            two = two + dot_nt(act, fc2_s[:, fs])
            gh_f = dot(cot, fc2_s[:, fs]) * slope
            gh = gh_f.astype(BF)
            gh_s[sl, fs] = gh
            acc_s[10 + f] += fold8(gh.astype(F32))
            gn = gn + dot_nt(gh, fc1_s[:, fs])
        two = two + norm_ref[5:6, :]
        result = middle + two
        out_ref[sl, :] = result.astype(BF)
        acc_s[6] += fold8(one * one)
        acc_s[7] += fold8(middle * middle)
        acc_s[8] += fold8(two * two)
        acc_s[9] += fold8(result * result)
        cotf = cot.astype(F32)
        acc_s[5] += fold8(cotf)
        acc_s[3] += fold8(gn * xhat)
        acc_s[4] += fold8(gn)
        gm = cotf + norm_back(gn, norm_ref[3:4, :], xhat, rate)
        ig_ref[sl, :] = gm
        gb = gm.astype(BF)
        gb_s[sl, :] = gb
        acc_s[2] += fold8(gb.astype(F32))
        ga_s[sl, :] = dot(gb, proj_s[...]).astype(BF)

    stores = [pltpu.make_async_copy(out_ref, out_hbm, store_sem.at[0])]
    stores[0].start()

    def weight_grad(left, right):
        return lax.dot_general(left, right, (((0,), (0,)), ((), ())), preferred_element_type=F32)

    def put_rows(ref, value, t, off):
        for n in range(batch):
            ref[n, t, :, off:off + value.shape[1]] = value[n * depth:(n + 1) * depth]

    for left, right, off in ((n2_s, gh_s, 0), (cot_ref, act_s, 256)):
        for t in range(4):
            put_rows(hm_s, weight_grad(left[...], right[:, t * 256:(t + 1) * 256]).astype(BF), t, off)
    gp = weight_grad(gb_s[...], att_s[...]).astype(BF)
    sums_m = [push(hm_s.at[peer[0]], inm_s.at[k], peer, "rm", k) for k, peer in enumerate(along_b)]

    @pl.loop(0, chunks)
    def _(c):
        for j in range(4):
            window = ga_s[pl.ds(pl.multiple_of(c * 784 + 192 * j, 16), 208), :]
            for b in range(2):
                spread = dot(into_ref[b * 4 + j], window[:, b * 128:(b + 1) * 128]).astype(BF)
                for s in range(2):
                    do_s[b, c * 8 + j * 2 + s] = spread[s * PAD:(s + 1) * PAD]

    def dprobs_stage(b, at):
        s_s[b] = dot_nt(v_s[b, at], jnp.concatenate(head_blocks(do_s[b, at], masks), 0))

    def dscores_stage(b, at):
        for h in range(4):
            lanes = slice(h * 128, (h + 1) * 128)
            pf = p_s[b, at, :, lanes].astype(F32)
            t = pf * s_s[b, :, lanes]
            ds_s[b, :, lanes] = (t - pf * jnp.sum(t, 0, keepdims=True)).astype(BF)

    def dqkv_stage(b, at):
        pitch = 16 - 8 * b
        q, k, v, do = q_s[b, at], k_s[b, at], v_s[b, at], do_s[b, at]
        kt = jnp.transpose(k)
        dqt = [dot(kt[h * HD:(h + 1) * HD], ds_s[b, :, h * 128:(h + 1) * 128]) for h in range(4)]
        dv = dot(p_s[b, at], jnp.concatenate(head_blocks(do, masks), 0))
        dk = dot(ds_s[b], jnp.concatenate(head_blocks(q, masks), 0))
        dq = jnp.transpose(jnp.concatenate(dqt, 0))[:PAD]
        taps = [lepe_s[n:n + 1, b * 128:(b + 1) * 128] for n in range(10)]
        dof, vf = do.astype(F32), v.astype(F32)
        dv = dv + window_sum_back(dof, taps, pitch)
        for n, part in enumerate(tap_sums(dof, vf, pitch)):
            tacc_s[b, n] += part
        tacc_s[b, 9] += fold8(dof)
        dq_s[b, at] = (dq * SCALE).astype(BF)
        dk_s[b, at] = (dk * SCALE).astype(BF)
        dv_s[b, at] = dv.astype(BF)

    @pl.loop(0, stripes + 2)
    def _(i):
        first, second, third = jnp.minimum(i, stripes - 1), jnp.clip(i - 1, 0, stripes - 1), jnp.maximum(i - 2, 0)
        for b in range(2):
            @pl.when(i == 2)
            def _():
                tacc_s[b] = jnp.zeros((10, 8, 128), F32)
            dqkv_stage(b, third)
            dscores_stage(b, second)
            dprobs_stage(b, first)

    def add_up(own, into, mid):
        for n in range(tensor):
            value = own[me_b, n].astype(F32)
            for k in range(batch - 1):
                value = value + into[k, n].astype(F32)
            mid[n] = value.astype(BF)

    arrive(sums_m)
    add_up(hm_s, inm_s, midm_s)
    last_m = [push(midm_s.at[peer[1]], zm_s.at[k], peer, "tm", k) for k, peer in enumerate(along_t)]

    @pl.loop(0, chunks)
    def _(c):
        gather_rows(lambda b, at: jnp.concatenate([dq_s[b, at], dk_s[b, at], dv_s[b, at]], 1), c, dqkv_s, 384)

    gw = weight_grad(n1_s[...], dqkv_s[:, 0:768]).astype(BF)
    work0 = jnp.concatenate([gw[:, 0:256], gw[:, 384:640]], 1)
    work1 = jnp.concatenate([gw[:, 256:384], gp[:, 0:128], gw[:, 640:768], gp[:, 128:256]], 1)
    for half, work in enumerate((work0, work1)):
        packed = dot_nt(work, lane_ref[...]).astype(BF)
        for t in range(4):
            put_rows(hq_s, packed[:, t * 128:(t + 1) * 128], t, 128 * half)
    sums_q = [push(hq_s.at[peer[0]], inq_s.at[k], peer, "rq", k) for k, peer in enumerate(along_b)]

    @pl.loop(0, NT_TILES)
    def _(i):
        sl = pl.ds(pl.multiple_of(i * MT, 16), MT)
        gn = dot_nt(dqkv_s[sl, 0:768], wcat_s[...])
        xhat, rate = norm_stats(x_ref[sl, :].astype(F32))
        acc_s[0] += fold8(gn * xhat)
        acc_s[1] += fold8(gn)
        ig_ref[sl, :] = ig_ref[sl, :] + norm_back(gn, norm_ref[0:1, :], xhat, rate)

    stores.append(pltpu.make_async_copy(ig_ref, ig_hbm, store_sem.at[1]))
    stores[1].start()
    for n in range(14):
        small_ref[n:n + 1, :] = jnp.sum(acc_s[n], 0, keepdims=True)
    for n in range(10):
        row = jnp.concatenate([jnp.sum(tacc_s[b, n], 0, keepdims=True) for b in range(2)], 1)
        small_ref[14 + n:15 + n, :] = jnp.concatenate([row[:, b * 128 + h * 32:b * 128 + h * 32 + 32] for h in range(4) for b in range(2)], 1)


    smallb_s[me_b] = small_ref[...]
    small_b = [push(small_ref, smallb_s.at[me_b], peer, "sb", k) for k, peer in enumerate(along_b)]
    arrive(sums_q)
    add_up(hq_s, inq_s, midq_s)
    last_q = [push(midq_s.at[peer[1]], zq_s.at[k], peer, "tq", k) for k, peer in enumerate(along_t)]
    arrive(small_b)

    def in_order(ref, count):
        part = ref[0]
        for n in range(1, count):
            part = part + ref[n]
        return part

    part = in_order(smallb_s, batch)
    total_ref[...] = part
    smallt_s[me_t] = part
    small_t = [push(total_ref, smallt_s.at[me_t], peer, "st", k) for k, peer in enumerate(along_t)]
    arrive(last_m)
    arrive(last_q)
    lanes = jnp.zeros((8, 128), F32)
    for mid, into, off in ((midm_s, zm_s, 0), (midq_s, zq_s, 512)):
        shard = mid[me_t].astype(F32)
        for k in range(tensor - 1):
            shard = shard + into[k].astype(F32)
        shard_ref[:, off:off + shard.shape[1]] = shard
        squares = fold8(shard * shard)
        for n in range(shard.shape[1] // 128):
            lanes = lanes + squares[:, n * 128:(n + 1) * 128]
    sqb_s[me_b] = lanes
    size_ref[...] = lanes
    square_b = [push(size_ref, sqb_s.at[me_b], peer, "qb", k) for k, peer in enumerate(along_b)]
    arrive(square_b)
    lanes = in_order(sqb_s, batch)
    sqt_s[me_t] = lanes
    for copy in square_b:
        copy.wait_send()
        sent.remove(copy)
    size_ref[...] = lanes
    square_t = [push(size_ref, sqt_s.at[me_t], peer, "qt", k) for k, peer in enumerate(along_t)]
    arrive(small_t)
    for copy in small_t:
        copy.wait_send()
        sent.remove(copy)
    vectors = in_order(smallt_s, tensor)
    total_ref[...] = vectors
    row = lax.broadcasted_iota(jnp.int32, vectors.shape, 0)
    vectors = jnp.where((row < 6) | (row >= 10), vectors, 0.0)
    vector = jnp.sum(jnp.sum(vectors * vectors, 0, keepdims=True), 1, keepdims=True)
    arrive(square_t)
    for copy in sent:
        copy.wait_send()
    matrix = jnp.sum(jnp.sum(in_order(sqt_s, tensor), 0, keepdims=True), 1, keepdims=True)
    size_ref[...] = jnp.broadcast_to(jnp.sqrt(matrix + vector), (8, 128))
    for copy in stores:
        copy.wait()


NAMES_IN = ["x_hbm", "cot_hbm", "qkv", "proj", "m1", "m2", "norm", "lepe", "bias", "into_hbm", "outof_hbm", "mask", "lane_hbm"]
NAMES_OUT = ["out_hbm", "ig_hbm", "shard", "total", "size"]


def scratch_list(batch, tensor, rows, depth):
    n = rows // CELLS * 2
    V = pltpu.VMEM
    dma = pltpu.SemaphoreType.DMA
    stripe = (2, n, PAD, 128)
    items = [
        ("x", V((rows, D), BF)), ("cot", V((rows, D), BF)), ("out", V((rows, D), BF)), ("ig", V((rows, D), F32)),
        ("into", V((8, 2 * PAD, 208), BF)), ("outof", V((8, 208, 2 * PAD), BF)), ("lane", V((512, 512), BF)),
        ("gq", V((batch, tensor, depth, 256), BF)), ("gm", V((batch, tensor, depth, 512), BF)),
        ("hq", V((batch, tensor, depth, 256), BF)), ("hm", V((batch, tensor, depth, 512), BF)),
        ("inq", V((batch - 1, tensor, depth, 256), BF)), ("inm", V((batch - 1, tensor, depth, 512), BF)),
        ("midq", V((tensor, depth, 256), BF)), ("midm", V((tensor, depth, 512), BF)),
        ("zqb", V((tensor - 1, depth, 256), BF)), ("zmb", V((tensor - 1, depth, 512), BF)),
        ("small", V((24, D), F32)), ("smallb", V((batch, 24, D), F32)), ("smallt", V((tensor, 24, D), F32)),
        ("sqb", V((batch, 8, 128), F32)), ("sqt", V((tensor, 8, 128), F32)),
        ("fc1", V((D, FF), BF)), ("fc2", V((D, FF), BF)), ("wcat", V((D, 768), BF)), ("proj_w", V((D, D), BF)), ("lepe_w", V((16, D), F32)),
        ("n1", V((rows, D), BF)), ("q", V(stripe, BF)), ("k", V(stripe, BF)), ("v", V(stripe, BF)), ("a", V(stripe, BF)),
        ("p", V((2, n, PAD, 512), BF)), ("att", V((rows, D), BF)), ("n2", V((rows, D), BF)), ("act", V((rows, FF), BF)), ("gh", V((rows, FF), BF)),
        ("gb", V((rows, D), BF)), ("ga", V((rows, D), BF)), ("do", V(stripe, BF)),
        ("acc", V((14, 8, D), F32)), ("tacc", V((2, 10, 8, 128), F32)),
        ("s", V((2, PAD, 512), F32)), ("ds", V((2, PAD, 512), BF)), ("dk", V(stripe, BF)), ("dv", V(stripe, BF)),
        ("load_sem", dma((5,))), ("store_sem", dma((2,))),
    ]
    b, t = batch - 1, tensor - 1
    for name, shape in (("zq", (t,)), ("zm", (t,)), ("bq", (tensor, b)), ("bm", (tensor, b)), ("rm", (b,)), ("rq", (b,)), ("tm", (t,)), ("tq", (t,)), ("sb", (b,)), ("st", (t,)), ("qb", (b,)), ("qt", (t,))):
        items += [(name + "_s", dma(shape)), (name + "_r", dma(shape))]
    return items


NAMES_SCRATCH = [name for name, _ in scratch_list(8, 4, 2352, 32)]


def block_call(batch, tensor, linked, x, cot, qkv, proj, fc1, fc2, norm, lepe, bias):
    rows, depth = x.shape[0], fc1.shape[0]
    into, outof = spread_tables()
    args = (x, cot, qkv, proj, fc1, fc2, norm, lepe, bias, jnp.asarray(into, BF), jnp.asarray(outof, BF), jnp.asarray(key_mask()), jnp.asarray(lane_table(4), BF))
    V = pl.BlockSpec(memory_space=pltpu.VMEM)
    H = pl.BlockSpec(memory_space=pl.ANY)
    extra = dict(collective_id=0, has_side_effects=True) if linked else {}
    return pl.pallas_call(
        functools.partial(block_kernel, batch, tensor, linked),
        out_shape=(
            jax.ShapeDtypeStruct((rows, D), BF),
            jax.ShapeDtypeStruct((rows, D), F32),
            jax.ShapeDtypeStruct((depth, 768), F32),
            jax.ShapeDtypeStruct((24, D), F32),
            jax.ShapeDtypeStruct((8, 128), F32),
        ),
        in_specs=[H, H] + [V] * 7 + [H, H, V, H],
        out_specs=(H, H, V, V, V),
        scratch_shapes=[shape for _, shape in scratch_list(batch, tensor, rows, depth)],
        compiler_params=pltpu.CompilerParams(vmem_limit_bytes=62 * 2**20, **extra),
    )(*args)


def adam(master, first, second, clipped, rate, decay):
    first = BETA_ONE * first + (1.0 - BETA_ONE) * clipped
    second = BETA_TWO * second + (1.0 - BETA_TWO) * clipped * clipped
    hat = first * (1.0 / (1.0 - BETA_ONE**STEP))
    spread = second * (1.0 / (1.0 - BETA_TWO**STEP))
    return master - rate * (hat / (jnp.sqrt(spread) + ADAM_EPS) + decay * master), first, second


def update_kernel(
    all_tokens, out_in, ig_in, shard_ref, total_ref, norm_ref,
    qkv_w, qkv_m, proj_w, proj_m, fc1_w, fc1_m, fc2_w, fc2_m, norm_w, norm_m, lepe_w, lepe_m, bias_w, bias_m,
    out_o, ig_o, qkv_g, qkv_n, qkv_l, qkv_o, proj_g, proj_n, proj_l, proj_o, fc1_g, fc1_n, fc1_l, fc1_o, fc2_g, fc2_n, fc2_l, fc2_o,
    norm_g, norm_n, norm_o, lepe_g, lepe_n, lepe_o, bias_g, bias_n, bias_o, size_o, rms_o, sems,
):
    copies = [pltpu.make_async_copy(out_in, out_o, sems.at[0]), pltpu.make_async_copy(ig_in, ig_o, sems.at[1])]
    for copy in copies:
        copy.start()
    size = norm_ref[0:1, 0:1]
    factor = jnp.minimum(1.0, CLIP_SCALE * math.sqrt(NPARAM) / (size + 1e-06))
    size_o[...] = size

    def one(grad, w, m, g_o, n_o, l_o, m_o, at, rate, decay, pair=lambda n, at: (n,) + at):
        clipped = grad * factor
        new, first, second = adam(w[at], m[pair(0, at)], m[pair(1, at)], clipped, rate, decay)
        g_o[at] = clipped
        n_o[at] = new
        if l_o is not None:
            l_o[at] = new.astype(BF)
        m_o[pair(0, at)] = first
        m_o[pair(1, at)] = second

    every = (slice(None), slice(None))
    middle = lambda n, at: (at[0], n, at[1])
    one(shard_ref[:, 0:256], fc1_w, fc1_m, fc1_g, fc1_n, fc1_l, fc1_o, every, RATE_MATRIX, DECAY_RATE)
    one(shard_ref[:, 256:512], fc2_w, fc2_m, fc2_g, fc2_n, fc2_l, fc2_o, every, RATE_MATRIX, DECAY_RATE)
    for j in range(3):
        one(shard_ref[:, 512 + 64 * j:576 + 64 * j], qkv_w, qkv_m, qkv_g, qkv_n, qkv_l, qkv_o, (j,) + every, RATE_MATRIX, DECAY_RATE)
    one(shard_ref[:, 704:768], proj_w, proj_m, proj_g, proj_n, proj_l, proj_o, every, RATE_MATRIX, DECAY_RATE)
    one(total_ref[0:6], norm_w, norm_m, norm_g, norm_n, None, norm_o, every, RATE_VECTOR, 0.0, middle)
    one(total_ref[14:24], lepe_w, lepe_m, lepe_g, lepe_n, None, lepe_o, every, RATE_VECTOR, 0.0, middle)
    for f in range(8):
        at = (slice(f, f + 1), slice(None))
        part = total_ref[10 + f // 2:11 + f // 2, 128 * (f % 2):128 * (f % 2) + 128]
        one(part, bias_w, bias_m, bias_g, bias_n, None, bias_o, at, RATE_VECTOR, 0.0, middle)
    lane = lax.broadcasted_iota(jnp.int32, (1, 4), 1)
    sums = jnp.zeros((1, 4), F32)
    for n in range(4):
        sums = jnp.where(lane == n, jnp.sum(total_ref[6 + n:7 + n], 1, keepdims=True), sums)
    rms_o[...] = jnp.sqrt(sums * (1.0 / (all_tokens * D)))
    for copy in copies:
        copy.wait()


def update_call(all_tokens, out, ig, shard, total, norm, arrays):
    V = pltpu.VMEM
    like = lambda a, dt=F32: jax.ShapeDtypeStruct(a.shape, dt)
    outs = [like(out, BF), like(ig)]
    H = pl.BlockSpec(memory_space=pl.ANY)
    for n in range(4):
        w, m = arrays[2 * n], arrays[2 * n + 1]
        outs += [like(w), like(w), like(w, BF), like(m)]
    for n in range(4, 7):
        w, m = arrays[2 * n], arrays[2 * n + 1]
        outs += [like(w), like(w), like(m)]
    outs += [jax.ShapeDtypeStruct((1, 1), F32), jax.ShapeDtypeStruct((1, 4), F32)]
    return list(pl.pallas_call(
        functools.partial(update_kernel, all_tokens),
        out_shape=tuple(outs),
        in_specs=[H, H] + [pl.BlockSpec(memory_space=V)] * (3 + len(arrays)),
        out_specs=tuple([H, H] + [pl.BlockSpec(memory_space=V)] * (len(outs) - 2)),
        scratch_shapes=[pltpu.SemaphoreType.DMA((2,))],
        compiler_params=pltpu.CompilerParams(vmem_limit_bytes=60 * 2**20),
    )(out, ig, shard, total, norm, *arrays))


def flip(a):
    return jnp.swapaxes(a, -1, -2)


def shards(block_input, cotangent, *arrays):
    batch, tensor = lax.axis_size("batch"), lax.axis_size("tensor")
    arrays = list(arrays)
    for n in (2, 3, 6, 7):
        arrays[n] = flip(arrays[n])
    arrays[9], arrays[11] = jnp.swapaxes(arrays[9], 0, 1), jnp.swapaxes(arrays[11], 0, 1)
    arrays[12], arrays[13] = arrays[12].reshape(8, 128), jnp.swapaxes(arrays[13].reshape(2, 8, 128), 0, 1)
    qkv, _, proj, _, fc1, _, fc2, _, norm, _, lepe, _, bias, _ = arrays
    output, input_grad, shard, total, size = block_call(batch, tensor, True, block_input, cotangent, qkv, proj, fc1, fc2, norm, lepe, bias)
    output, input_grad, *got = update_call(block_input.shape[0] * batch * tensor, output, input_grad, shard, total, size, arrays)
    for n in (4, 5, 6, 7, 12, 13, 14, 15):
        got[n] = flip(got[n])
    got[18], got[21] = jnp.swapaxes(got[18], 0, 1), jnp.swapaxes(got[21], 0, 1)
    got[22], got[23], got[24] = got[22].reshape(1024), got[23].reshape(1024), jnp.swapaxes(got[24], 0, 1).reshape(2, 1024)
    got[25], got[26] = got[25].reshape(()), got[26].reshape(4)
    return (output, input_grad, *got)


def solution(mesh):
    token, matrix, moment = P(("batch", "tensor"), None), P("batch", "tensor"), P(None, "batch", "tensor")
    back, back_moment = P("tensor", "batch"), P(None, "tensor", "batch")
    stack, stack_moment = P(None, "batch", "tensor"), P(None, None, "batch", "tensor")
    return jax.shard_map(
        shards,
        mesh=mesh,
        in_specs=(token, token, stack, stack_moment, back, back_moment, matrix, moment, back, back_moment) + (P(),) * 6,
        out_specs=(token, token) + (stack,) * 3 + (stack_moment,) + (back,) * 3 + (back_moment,) + (matrix,) * 3 + (moment,) + (back,) * 3 + (back_moment,) + (P(),) * 11,
        check_vma=False,
    )
```

```python
import functools, math
import numpy as np
import jax, jax.numpy as jnp
from jax import lax
from jax.experimental import pallas as pl
from jax.experimental.pallas import tpu as pltpu
from jax.sharding import PartitionSpec as P

HD = 32
STEP = 10
NPARAM = 791552
CLIP_SCALE = 6.0
BETA_ONE = 0.9
BETA_TWO = 0.999
ADAM_EPS = 1e-08
DECAY_RATE = 0.05
RATE_MATRIX = 0.1
RATE_VECTOR = 0.6
GRID = 14
SPLIT = 7
CELLS = 196
PAD = 112
D = 256
FF = 1024
NORM_EPS = 1e-5
BF = jnp.bfloat16
F32 = jnp.float32
SCALE = HD ** -0.5
LOG2E = 1.4426950408889634


def slot_of(branch, cell):
    row, col = divmod(cell, GRID)
    if branch == 0:
        return row * 16 + col
    stripe, inner = divmod(col, SPLIT)
    return stripe * PAD + row * 8 + inner


def spread_tables():
    into = np.zeros((2, 4, 2 * PAD, 208), np.float32)
    for branch in range(2):
        for cell in range(CELLS):
            for j in range(4):
                into[branch, j, slot_of(branch, cell), cell + 4 * j] = 1.0
    return into.reshape(8, 2 * PAD, 208), into.transpose(0, 1, 3, 2).reshape(8, 208, 2 * PAD)


def key_mask():
    mask = np.full((2, PAD, 128), -1e30, np.float32)
    for branch in range(2):
        for cell in range(CELLS):
            slot = slot_of(branch, cell)
            if slot < PAD:
                mask[branch, slot] = 0.0
    return mask


def lane_table(tensor):
    heads = 4 // tensor
    assert heads == 1
    table = np.zeros((512, 512), np.float32)
    for t in range(4):
        for j in range(2):
            for b in range(2):
                for e in range(HD):
                    table[t * 128 + j * 64 + b * 32 + e, b * 256 + j * 128 + t * 32 + e] = 1.0
    return table


def dot(a, b):
    return lax.dot_general(a, b, (((1,), (0,)), ((), ())), preferred_element_type=F32)


def dot_nt(a, b):
    return lax.dot_general(a, b, (((1,), (1,)), ((), ())), preferred_element_type=F32)


def norm_stats(v):
    centre = jnp.mean(v, -1, keepdims=True)
    centred = v - centre
    spread = jnp.mean(centred * centred, -1, keepdims=True)
    rate = lax.rsqrt(spread + NORM_EPS)
    return centred * rate, rate


def norm_back(grad, gain, xhat, rate):
    gx = grad * gain
    first = jnp.mean(gx, -1, keepdims=True)
    second = jnp.mean(gx * xhat, -1, keepdims=True)
    return rate * (gx - first - xhat * second)


def fold8(v):
    return jnp.sum(v.reshape(v.shape[0] // 8, 8, v.shape[1]), axis=0)


def gelu_pair(h):
    e = jnp.exp2(h * h * (-0.5 * LOG2E))
    t = 1.0 / (1.0 + (0.3275911 * math.sqrt(0.5)) * jnp.abs(h))
    poly = t * (0.5 * 0.254829592 + t * (0.5 * -0.284496736 + t * (0.5 * 1.421413741 + t * (0.5 * -1.453152027 + t * (0.5 * 1.061405429)))))
    tail = poly * e
    phi = jnp.where(h < 0, tail, 1.0 - tail)
    return h * phi, phi + h * e * (1.0 / math.sqrt(2 * math.pi))


def head_masks():
    lane = lax.broadcasted_iota(jnp.int32, (128, 128), 1) // HD
    return [jnp.where(lane == h, 1.0, 0.0).astype(BF) for h in range(4)]


def head_blocks(z, masks):
    zp = jnp.concatenate([z, jnp.zeros((16, 128), BF)], 0)
    return [zp * masks[h] for h in range(4)]


def col_shift(v):
    return pltpu.roll(v, 1, 0), v, pltpu.roll(v, PAD - 1, 0)


def row_up(u, pitch):
    return jnp.concatenate([u[pitch:], jnp.zeros((pitch, 128), F32)], 0)


def row_down(u, pitch):
    return jnp.concatenate([jnp.zeros((pitch, 128), F32), u[:-pitch]], 0)


def window_sum(v, taps, pitch):
    cols = col_shift(v)
    rows = [sum(taps[3 * i + j] * cols[j] for j in range(3)) for i in range(3)]
    return row_down(rows[0], pitch) + rows[1] + row_up(rows[2], pitch)


def window_sum_back(d, taps, pitch):
    cols = col_shift(d)
    rows = [sum(taps[3 * i + j] * cols[2 - j] for j in range(3)) for i in range(3)]
    return row_up(rows[0], pitch) + rows[1] + row_down(rows[2], pitch)


def tap_sums(d, v, pitch):
    cols = col_shift(v)
    out = []
    for i in range(3):
        moved = row_up(d, pitch) if i == 0 else (d if i == 1 else row_down(d, pitch))
        for j in range(3):
            out.append(fold8(moved * cols[j]))
    return out


MT = 336
NT_TILES = 7
MESH = pl.DeviceIdType.MESH


def block_kernel(
    batch, tensor, linked, *refs,
):
    names = NAMES_IN + NAMES_OUT + NAMES_SCRATCH
    r = dict(zip(names, refs))
    (x_hbm, cot_hbm, qkv_ref, proj_ref, m1_ref, m2_ref, norm_ref, lepe_ref, bias_ref, into_hbm, outof_hbm, mask_ref, lane_hbm) = [r[n] for n in NAMES_IN]
    (out_hbm, ig_hbm, shard_ref, total_ref, size_ref) = [r[n] for n in NAMES_OUT]
    (x_ref, cot_ref, out_ref, ig_ref, into_ref, outof_ref, lane_ref,
     gq_s, gm_s, hq_s, hm_s, inq_s, inm_s, midq_s, midm_s, zq_s, zm_s, small_ref, smallb_s, smallt_s, sqb_s, sqt_s,
     fc1_s, fc2_s, wcat_s, proj_s, lepe_s, n1_s, q_s, k_s, v_s, a_s, p_s, att_s, n2_s, act_s, gh_s, gb_s, ga_s, do_s,
     acc_s, tacc_s, s_s, ds_s, dk_s, dv_s) = [r[n] for n in NAMES_SCRATCH[:46]]
    dq_s, dqkv_s = a_s, gh_s
    load_sem, store_sem = r["load_sem"], r["store_sem"]

    rows = x_ref.shape[0]
    images = rows // CELLS
    chunks = images // 4
    depth = m1_ref.shape[0]

    loads = []
    for n, (source, dest) in enumerate(((x_hbm, x_ref), (into_hbm, into_ref), (lane_hbm, lane_ref), (outof_hbm, outof_ref), (cot_hbm, cot_ref))):
        copy = pltpu.make_async_copy(source, dest, load_sem.at[n])
        copy.start()
        loads.append(copy)

    if linked:
        me_b, me_t = lax.axis_index("batch"), lax.axis_index("tensor")
    else:
        me_b, me_t = 0, 0
    along_b = [(lax.rem(me_b + k, batch), me_t) for k in range(1, batch)]
    along_t = [(me_b, lax.rem(me_t + k, tensor)) for k in range(1, tensor)]

    class Push:
        def __init__(self, source, dest, peer, send, recv):
            self.copy = None
            if linked:
                self.copy = pltpu.make_async_remote_copy(src_ref=source, dst_ref=dest, send_sem=send, recv_sem=recv, device_id=peer, device_id_type=MESH)
                self.copy.start()

        def wait_recv(self):
            if self.copy is not None:
                self.copy.wait_recv()

        def wait_send(self):
            if self.copy is not None:
                self.copy.wait_send()

    sent = []

    def push(source, dest, peer, sems, *at):
        got = Push(source, dest, peer, r[sems + "_s"].at[at], r[sems + "_r"].at[at])
        sent.append(got)
        return got

    def arrive(copies):
        for copy in copies:
            copy.wait_recv()

    gq_s[me_b, me_t] = jnp.concatenate([qkv_ref[0], qkv_ref[1], qkv_ref[2], proj_ref[...]], 1).astype(BF)
    gm_s[me_b, me_t, :, 0:256] = m1_ref[...].astype(BF)
    gm_s[me_b, me_t, :, 256:512] = m2_ref[...].astype(BF)
    if linked:
        barrier = pltpu.get_barrier_semaphore()
        for peer in along_b + along_t:
            pl.semaphore_signal(barrier, inc=1, device_id=peer, device_id_type=MESH)
        pl.semaphore_wait(barrier, len(along_b) + len(along_t))
    got_q, got_m = [], []
    over = {}
    for name, ref in (("zq", gq_s), ("zm", gm_s)):
        mine = ref.at[me_b, me_t]
        over[name] = [push(mine, mine, peer, name, k) for k, peer in enumerate(along_t)]
        if name == "zq":
            got_q += [push(mine, mine, peer, "bq", 0, k) for k, peer in enumerate(along_b)]
    acc_s[...] = jnp.zeros_like(acc_s)
    lp = lepe_ref[...]
    lepe_s[0:10, :] = jnp.concatenate([lp[:, h * 64 + b * 32:h * 64 + b * 32 + 32] for b in range(2) for h in range(4)], 1)
    for n in range(1, tensor):
        over["zq"][n - 1].wait_recv()
        slot = gq_s.at[me_b, lax.rem(me_t + tensor - n, tensor)]
        got_q += [push(slot, slot, peer, "bq", n, k) for k, peer in enumerate(along_b)]
    for n in range(tensor):
        if n > 0:
            over["zm"][n - 1].wait_recv()
        slot = gm_s.at[me_b, lax.rem(me_t + tensor - n, tensor)]
        got_m += [push(slot, slot, peer, "bm", n, k) for k, peer in enumerate(along_b)]
    loads[0].wait()

    @pl.loop(0, NT_TILES)
    def _(i):
        sl = pl.ds(pl.multiple_of(i * MT, 16), MT)
        xhat, rate = norm_stats(x_ref[sl, :].astype(F32))
        n1_s[sl, :] = (xhat * norm_ref[0:1, :] + norm_ref[1:2, :]).astype(BF)

    loads[1].wait()
    loads[2].wait()
    arrive(got_q)
    for half in range(2):
        lanes = slice(half * 128, half * 128 + 128)
        packed = jnp.concatenate([jnp.concatenate([gq_s[n, t, :, lanes] for n in range(batch)], 0) for t in range(4)], 1)
        work = dot(packed, lane_ref[...]).astype(BF)
        for b in range(2):
            if half == 0:
                wcat_s[:, b * 384:b * 384 + 256] = work[:, b * 256:b * 256 + 256]
            else:
                wcat_s[:, b * 384 + 256:b * 384 + 384] = work[:, b * 256:b * 256 + 128]
                proj_s[:, b * 128:b * 128 + 128] = work[:, b * 256 + 128:b * 256 + 256]

    @pl.loop(0, chunks)
    def _(c):
        for j in range(4):
            window = n1_s[pl.ds(pl.multiple_of(c * 784 + 192 * j, 16), 208), :]
            for b in range(2):
                spread = dot(into_ref[b * 4 + j], window).astype(BF)
                qkv = dot(spread, wcat_s[:, b * 384:(b + 1) * 384]).astype(BF)
                for s in range(2):
                    at = c * 8 + j * 2 + s
                    q_s[b, at] = qkv[s * PAD:(s + 1) * PAD, 0:128]
                    k_s[b, at] = qkv[s * PAD:(s + 1) * PAD, 128:256]
                    v_s[b, at] = qkv[s * PAD:(s + 1) * PAD, 256:384]

    masks = head_masks()

    stripes = images * 2

    def scores_stage(b, at):
        s_s[b] = dot_nt(k_s[b, at], jnp.concatenate(head_blocks(q_s[b, at], masks), 0))

    def soft_stage(b, at):
        for h in range(4):
            lanes = slice(h * 128, (h + 1) * 128)
            s = s_s[b, :, lanes] * (SCALE * LOG2E) + mask_ref[b]
            p = jnp.exp2(s - jnp.max(s, 0, keepdims=True))
            p_s[b, at, :, lanes] = (p * (1.0 / jnp.sum(p, 0, keepdims=True))).astype(BF)

    def mix_stage(b, at):
        pitch = 16 - 8 * b
        v = v_s[b, at]
        vt = jnp.transpose(v)
        ots = [dot(vt[h * HD:(h + 1) * HD], p_s[b, at, :, h * 128:(h + 1) * 128]) for h in range(4)]
        mixed = jnp.transpose(jnp.concatenate(ots, 0))[:PAD]
        taps = [lepe_s[n:n + 1, b * 128:(b + 1) * 128] for n in range(10)]
        local = window_sum(v.astype(F32), taps, pitch) + taps[9]
        a_s[b, at] = (mixed + local).astype(BF)

    @pl.loop(0, stripes + 2)
    def _(i):
        first, second, third = jnp.minimum(i, stripes - 1), jnp.clip(i - 1, 0, stripes - 1), jnp.maximum(i - 2, 0)
        for b in range(2):
            mix_stage(b, third)
            soft_stage(b, second)
            scores_stage(b, first)

    def gather_rows(source, c, dest, lanes):
        for b in range(2):
            tail = None
            for j in range(4):
                both = jnp.concatenate([source(b, c * 8 + j * 2), source(b, c * 8 + j * 2 + 1)], 0)
                got = dot(outof_ref[b * 4 + j], both)
                head = got[0:16] if tail is None else got[0:16] + tail
                base = c * 784 + 192 * j
                cols = slice(b * lanes, (b + 1) * lanes)
                dest[pl.ds(pl.multiple_of(base, 16), 16), cols] = head.astype(BF)
                dest[pl.ds(pl.multiple_of(base + 16, 16), 176), cols] = got[16:192].astype(BF)
                tail = got[192:208]
                if j == 3:
                    dest[pl.ds(pl.multiple_of(base + 192, 16), 16), cols] = tail.astype(BF)

    loads[3].wait()
    loads[4].wait()

    @pl.loop(0, chunks)
    def _(c):
        gather_rows(lambda b, at: a_s[b, at], c, att_s, 128)

    arrive(got_m)
    for t in range(4):
        for n in range(batch):
            at = slice(n * depth, (n + 1) * depth)
            fc1_s[at, t * 256:(t + 1) * 256] = gm_s[n, t, :, 0:256]
            fc2_s[at, t * 256:(t + 1) * 256] = gm_s[n, t, :, 256:512]

    @pl.loop(0, NT_TILES)
    def _(i):
        sl = pl.ds(pl.multiple_of(i * MT, 16), MT)
        one = dot_nt(att_s[sl, :], proj_s[...]) + norm_ref[2:3, :]
        middle = x_ref[sl, :].astype(F32) + one
        xhat, rate = norm_stats(middle)
        n2 = (xhat * norm_ref[3:4, :] + norm_ref[4:5, :]).astype(BF)
        n2_s[sl, :] = n2
        cot = cot_ref[sl, :]
        two = jnp.zeros((MT, D), F32)
        gn = jnp.zeros((MT, D), F32)
        for f in range(4):
            fs = slice(f * 256, (f + 1) * 256)
            hidden = dot(n2, fc1_s[:, fs]) + jnp.concatenate([bias_ref[2 * f:2 * f + 1, :], bias_ref[2 * f + 1:2 * f + 2, :]], 1)
            gelu, slope = gelu_pair(hidden)
            act = gelu.astype(BF)
            act_s[sl, fs] = act
            two = two + dot_nt(act, fc2_s[:, fs])
            gh_f = dot(cot, fc2_s[:, fs]) * slope
            gh = gh_f.astype(BF)
            gh_s[sl, fs] = gh
            acc_s[10 + f] += fold8(gh.astype(F32))
            gn = gn + dot_nt(gh, fc1_s[:, fs])
        two = two + norm_ref[5:6, :]
        result = middle + two
        out_ref[sl, :] = result.astype(BF)
        acc_s[6] += fold8(one * one)
        acc_s[7] += fold8(middle * middle)
        acc_s[8] += fold8(two * two)
        acc_s[9] += fold8(result * result)
        cotf = cot.astype(F32)
        acc_s[5] += fold8(cotf)
        acc_s[3] += fold8(gn * xhat)
        acc_s[4] += fold8(gn)
        gm = cotf + norm_back(gn, norm_ref[3:4, :], xhat, rate)
        ig_ref[sl, :] = gm
        gb = gm.astype(BF)
        gb_s[sl, :] = gb
        acc_s[2] += fold8(gb.astype(F32))
        ga_s[sl, :] = dot(gb, proj_s[...]).astype(BF)

    stores = [pltpu.make_async_copy(out_ref, out_hbm, store_sem.at[0])]
    stores[0].start()

    def weight_grad(left, right):
        return lax.dot_general(left, right, (((0,), (0,)), ((), ())), preferred_element_type=F32)

    def put_rows(ref, value, t, off):
        for n in range(batch):
            ref[n, t, :, off:off + value.shape[1]] = value[n * depth:(n + 1) * depth]

    for left, right, off in ((n2_s, gh_s, 0), (cot_ref, act_s, 256)):
        for t in range(4):
            put_rows(hm_s, weight_grad(left[...], right[:, t * 256:(t + 1) * 256]).astype(BF), t, off)
    gp = weight_grad(gb_s[...], att_s[...]).astype(BF)
    sums_m = [push(hm_s.at[peer[0]], inm_s.at[k], peer, "rm", k) for k, peer in enumerate(along_b)]

    @pl.loop(0, chunks)
    def _(c):
        for j in range(4):
            window = ga_s[pl.ds(pl.multiple_of(c * 784 + 192 * j, 16), 208), :]
            for b in range(2):
                spread = dot(into_ref[b * 4 + j], window[:, b * 128:(b + 1) * 128]).astype(BF)
                for s in range(2):
                    do_s[b, c * 8 + j * 2 + s] = spread[s * PAD:(s + 1) * PAD]

    def dprobs_stage(b, at):
        s_s[b] = dot_nt(v_s[b, at], jnp.concatenate(head_blocks(do_s[b, at], masks), 0))

    def dscores_stage(b, at):
        for h in range(4):
            lanes = slice(h * 128, (h + 1) * 128)
            pf = p_s[b, at, :, lanes].astype(F32)
            t = pf * s_s[b, :, lanes]
            ds_s[b, :, lanes] = (t - pf * jnp.sum(t, 0, keepdims=True)).astype(BF)

    def dqkv_stage(b, at):
        pitch = 16 - 8 * b
        q, k, v, do = q_s[b, at], k_s[b, at], v_s[b, at], do_s[b, at]
        kt = jnp.transpose(k)
        dqt = [dot(kt[h * HD:(h + 1) * HD], ds_s[b, :, h * 128:(h + 1) * 128]) for h in range(4)]
        dv = dot(p_s[b, at], jnp.concatenate(head_blocks(do, masks), 0))
        dk = dot(ds_s[b], jnp.concatenate(head_blocks(q, masks), 0))
        dq = jnp.transpose(jnp.concatenate(dqt, 0))[:PAD]
        taps = [lepe_s[n:n + 1, b * 128:(b + 1) * 128] for n in range(10)]
        dof, vf = do.astype(F32), v.astype(F32)
        dv = dv + window_sum_back(dof, taps, pitch)
        for n, part in enumerate(tap_sums(dof, vf, pitch)):
            tacc_s[b, n] += part
        tacc_s[b, 9] += fold8(dof)
        dq_s[b, at] = (dq * SCALE).astype(BF)
        dk_s[b, at] = (dk * SCALE).astype(BF)
        dv_s[b, at] = dv.astype(BF)

    @pl.loop(0, stripes + 2)
    def _(i):
        first, second, third = jnp.minimum(i, stripes - 1), jnp.clip(i - 1, 0, stripes - 1), jnp.maximum(i - 2, 0)
        for b in range(2):
            @pl.when(i == 2)
            def _():
                tacc_s[b] = jnp.zeros((10, 8, 128), F32)
            dqkv_stage(b, third)
            dscores_stage(b, second)
            dprobs_stage(b, first)

    def add_up(own, into, mid):
        for n in range(tensor):
            value = own[me_b, n].astype(F32)
            for k in range(batch - 1):
                value = value + into[k, n].astype(F32)
            mid[n] = value.astype(BF)

    arrive(sums_m)
    add_up(hm_s, inm_s, midm_s)
    last_m = [push(midm_s.at[peer[1]], zm_s.at[k], peer, "tm", k) for k, peer in enumerate(along_t)]

    @pl.loop(0, chunks)
    def _(c):
        gather_rows(lambda b, at: jnp.concatenate([dq_s[b, at], dk_s[b, at], dv_s[b, at]], 1), c, dqkv_s, 384)

    gw = weight_grad(n1_s[...], dqkv_s[:, 0:768]).astype(BF)
    work0 = jnp.concatenate([gw[:, 0:256], gw[:, 384:640]], 1)
    work1 = jnp.concatenate([gw[:, 256:384], gp[:, 0:128], gw[:, 640:768], gp[:, 128:256]], 1)
    for half, work in enumerate((work0, work1)):
        packed = dot_nt(work, lane_ref[...]).astype(BF)
        for t in range(4):
            put_rows(hq_s, packed[:, t * 128:(t + 1) * 128], t, 128 * half)
    sums_q = [push(hq_s.at[peer[0]], inq_s.at[k], peer, "rq", k) for k, peer in enumerate(along_b)]

    @pl.loop(0, NT_TILES)
    def _(i):
        sl = pl.ds(pl.multiple_of(i * MT, 16), MT)
        gn = dot_nt(dqkv_s[sl, 0:768], wcat_s[...])
        xhat, rate = norm_stats(x_ref[sl, :].astype(F32))
        acc_s[0] += fold8(gn * xhat)
        acc_s[1] += fold8(gn)
        ig_ref[sl, :] = ig_ref[sl, :] + norm_back(gn, norm_ref[0:1, :], xhat, rate)

    stores.append(pltpu.make_async_copy(ig_ref, ig_hbm, store_sem.at[1]))
    stores[1].start()
    for n in range(14):
        small_ref[n:n + 1, :] = jnp.sum(acc_s[n], 0, keepdims=True)
    for n in range(10):
        row = jnp.concatenate([jnp.sum(tacc_s[b, n], 0, keepdims=True) for b in range(2)], 1)
        small_ref[14 + n:15 + n, :] = jnp.concatenate([row[:, b * 128 + h * 32:b * 128 + h * 32 + 32] for h in range(4) for b in range(2)], 1)


    smallb_s[me_b] = small_ref[...]
    small_b = [push(small_ref, smallb_s.at[me_b], peer, "sb", k) for k, peer in enumerate(along_b)]
    arrive(sums_q)
    add_up(hq_s, inq_s, midq_s)
    last_q = [push(midq_s.at[peer[1]], zq_s.at[k], peer, "tq", k) for k, peer in enumerate(along_t)]
    arrive(small_b)

    def in_order(ref, count):
        part = ref[0]
        for n in range(1, count):
            part = part + ref[n]
        return part

    part = in_order(smallb_s, batch)
    total_ref[...] = part
    smallt_s[me_t] = part
    small_t = [push(total_ref, smallt_s.at[me_t], peer, "st", k) for k, peer in enumerate(along_t)]
    arrive(last_m)
    arrive(last_q)
    lanes = jnp.zeros((8, 128), F32)
    for mid, into, off in ((midm_s, zm_s, 0), (midq_s, zq_s, 512)):
        shard = mid[me_t].astype(F32)
        for k in range(tensor - 1):
            shard = shard + into[k].astype(F32)
        shard_ref[:, off:off + shard.shape[1]] = shard
        squares = fold8(shard * shard)
        for n in range(shard.shape[1] // 128):
            lanes = lanes + squares[:, n * 128:(n + 1) * 128]
    sqb_s[me_b] = lanes
    size_ref[...] = lanes
    square_b = [push(size_ref, sqb_s.at[me_b], peer, "qb", k) for k, peer in enumerate(along_b)]
    arrive(square_b)
    lanes = in_order(sqb_s, batch)
    sqt_s[me_t] = lanes
    for copy in square_b:
        copy.wait_send()
        sent.remove(copy)
    size_ref[...] = lanes
    square_t = [push(size_ref, sqt_s.at[me_t], peer, "qt", k) for k, peer in enumerate(along_t)]
    arrive(small_t)
    for copy in small_t:
        copy.wait_send()
        sent.remove(copy)
    vectors = in_order(smallt_s, tensor)
    total_ref[...] = vectors
    row = lax.broadcasted_iota(jnp.int32, vectors.shape, 0)
    vectors = jnp.where((row < 6) | (row >= 10), vectors, 0.0)
    vector = jnp.sum(jnp.sum(vectors * vectors, 0, keepdims=True), 1, keepdims=True)
    arrive(square_t)
    for copy in sent:
        copy.wait_send()
    matrix = jnp.sum(jnp.sum(in_order(sqt_s, tensor), 0, keepdims=True), 1, keepdims=True)
    size_ref[...] = jnp.broadcast_to(jnp.sqrt(matrix + vector), (8, 128))
    for copy in stores:
        copy.wait()


NAMES_IN = ["x_hbm", "cot_hbm", "qkv", "proj", "m1", "m2", "norm", "lepe", "bias", "into_hbm", "outof_hbm", "mask", "lane_hbm"]
NAMES_OUT = ["out_hbm", "ig_hbm", "shard", "total", "size"]


def scratch_list(batch, tensor, rows, depth):
    n = rows // CELLS * 2
    V = pltpu.VMEM
    dma = pltpu.SemaphoreType.DMA
    stripe = (2, n, PAD, 128)
    items = [
        ("x", V((rows, D), BF)), ("cot", V((rows, D), BF)), ("out", V((rows, D), BF)), ("ig", V((rows, D), F32)),
        ("into", V((8, 2 * PAD, 208), BF)), ("outof", V((8, 208, 2 * PAD), BF)), ("lane", V((512, 512), BF)),
        ("gq", V((batch, tensor, depth, 256), BF)), ("gm", V((batch, tensor, depth, 512), BF)),
        ("hq", V((batch, tensor, depth, 256), BF)), ("hm", V((batch, tensor, depth, 512), BF)),
        ("inq", V((batch - 1, tensor, depth, 256), BF)), ("inm", V((batch - 1, tensor, depth, 512), BF)),
        ("midq", V((tensor, depth, 256), BF)), ("midm", V((tensor, depth, 512), BF)),
        ("zqb", V((tensor - 1, depth, 256), BF)), ("zmb", V((tensor - 1, depth, 512), BF)),
        ("small", V((24, D), F32)), ("smallb", V((batch, 24, D), F32)), ("smallt", V((tensor, 24, D), F32)),
        ("sqb", V((batch, 8, 128), F32)), ("sqt", V((tensor, 8, 128), F32)),
        ("fc1", V((D, FF), BF)), ("fc2", V((D, FF), BF)), ("wcat", V((D, 768), BF)), ("proj_w", V((D, D), BF)), ("lepe_w", V((16, D), F32)),
        ("n1", V((rows, D), BF)), ("q", V(stripe, BF)), ("k", V(stripe, BF)), ("v", V(stripe, BF)), ("a", V(stripe, BF)),
        ("p", V((2, n, PAD, 512), BF)), ("att", V((rows, D), BF)), ("n2", V((rows, D), BF)), ("act", V((rows, FF), BF)), ("gh", V((rows, FF), BF)),
        ("gb", V((rows, D), BF)), ("ga", V((rows, D), BF)), ("do", V(stripe, BF)),
        ("acc", V((14, 8, D), F32)), ("tacc", V((2, 10, 8, 128), F32)),
        ("s", V((2, PAD, 512), F32)), ("ds", V((2, PAD, 512), BF)), ("dk", V(stripe, BF)), ("dv", V(stripe, BF)),
        ("load_sem", dma((5,))), ("store_sem", dma((2,))),
    ]
    b, t = batch - 1, tensor - 1
    for name, shape in (("zq", (t,)), ("zm", (t,)), ("bq", (tensor, b)), ("bm", (tensor, b)), ("rm", (b,)), ("rq", (b,)), ("tm", (t,)), ("tq", (t,)), ("sb", (b,)), ("st", (t,)), ("qb", (b,)), ("qt", (t,))):
        items += [(name + "_s", dma(shape)), (name + "_r", dma(shape))]
    return items


NAMES_SCRATCH = [name for name, _ in scratch_list(8, 4, 2352, 32)]


def block_call(batch, tensor, linked, x, cot, qkv, proj, fc1, fc2, norm, lepe, bias):
    rows, depth = x.shape[0], fc1.shape[0]
    into, outof = spread_tables()
    args = (x, cot, qkv, proj, fc1, fc2, norm, lepe, bias, jnp.asarray(into, BF), jnp.asarray(outof, BF), jnp.asarray(key_mask()), jnp.asarray(lane_table(4), BF))
    V = pl.BlockSpec(memory_space=pltpu.VMEM)
    H = pl.BlockSpec(memory_space=pl.ANY)
    extra = dict(collective_id=0, has_side_effects=True) if linked else {}
    return pl.pallas_call(
        functools.partial(block_kernel, batch, tensor, linked),
        out_shape=(
            jax.ShapeDtypeStruct((rows, D), BF),
            jax.ShapeDtypeStruct((rows, D), F32),
            jax.ShapeDtypeStruct((depth, 768), F32),
            jax.ShapeDtypeStruct((24, D), F32),
            jax.ShapeDtypeStruct((8, 128), F32),
        ),
        in_specs=[H, H] + [V] * 7 + [H, H, V, H],
        out_specs=(H, H, V, V, V),
        scratch_shapes=[shape for _, shape in scratch_list(batch, tensor, rows, depth)],
        compiler_params=pltpu.CompilerParams(vmem_limit_bytes=62 * 2**20, **extra),
    )(*args)


def adam(master, first, second, clipped, rate, decay):
    first = BETA_ONE * first + (1.0 - BETA_ONE) * clipped
    second = BETA_TWO * second + (1.0 - BETA_TWO) * clipped * clipped
    hat = first * (1.0 / (1.0 - BETA_ONE**STEP))
    spread = second * (1.0 / (1.0 - BETA_TWO**STEP))
    return master - rate * (hat / (jnp.sqrt(spread) + ADAM_EPS) + decay * master), first, second


def update_kernel(
    all_tokens, out_in, ig_in, shard_ref, total_ref, norm_ref,
    qkv_w, qkv_m, proj_w, proj_m, fc1_w, fc1_m, fc2_w, fc2_m, norm_w, norm_m, lepe_w, lepe_m, bias_w, bias_m,
    out_o, ig_o, qkv_g, qkv_n, qkv_l, qkv_o, proj_g, proj_n, proj_l, proj_o, fc1_g, fc1_n, fc1_l, fc1_o, fc2_g, fc2_n, fc2_l, fc2_o,
    norm_g, norm_n, norm_o, lepe_g, lepe_n, lepe_o, bias_g, bias_n, bias_o, size_o, rms_o, out_s, ig_s, sems,
):
    moves = []
    for source, held, dest in ((out_in, out_s, out_o), (ig_in, ig_s, ig_o)):
        step = held.shape[0] // 3
        for n in range(3):
            at = pl.ds(n * step, step)
            moves.append([pltpu.make_async_copy(source.at[at], held.at[at], sems.at[0, len(moves)]), pltpu.make_async_copy(held.at[at], dest.at[at], sems.at[1, len(moves)])])
    for into, _ in moves:
        into.start()
    size = norm_ref[0:1, 0:1]
    factor = jnp.minimum(1.0, CLIP_SCALE * math.sqrt(NPARAM) / (size + 1e-06))
    size_o[...] = size

    def one(grad, w, m, g_o, n_o, l_o, m_o, at, rate, decay, pair=lambda n, at: (n,) + at):
        clipped = grad * factor
        new, first, second = adam(w[at], m[pair(0, at)], m[pair(1, at)], clipped, rate, decay)
        g_o[at] = clipped
        n_o[at] = new
        if l_o is not None:
            l_o[at] = new.astype(BF)
        m_o[pair(0, at)] = first
        m_o[pair(1, at)] = second

    for into, away in moves:
        into.wait()
        away.start()
    every = (slice(None), slice(None))
    middle = lambda n, at: (at[0], n, at[1])
    one(shard_ref[:, 0:256], fc1_w, fc1_m, fc1_g, fc1_n, fc1_l, fc1_o, every, RATE_MATRIX, DECAY_RATE)
    one(shard_ref[:, 256:512], fc2_w, fc2_m, fc2_g, fc2_n, fc2_l, fc2_o, every, RATE_MATRIX, DECAY_RATE)
    for j in range(3):
        one(shard_ref[:, 512 + 64 * j:576 + 64 * j], qkv_w, qkv_m, qkv_g, qkv_n, qkv_l, qkv_o, (j,) + every, RATE_MATRIX, DECAY_RATE)
    one(shard_ref[:, 704:768], proj_w, proj_m, proj_g, proj_n, proj_l, proj_o, every, RATE_MATRIX, DECAY_RATE)
    one(total_ref[0:6], norm_w, norm_m, norm_g, norm_n, None, norm_o, every, RATE_VECTOR, 0.0, middle)
    one(total_ref[14:24], lepe_w, lepe_m, lepe_g, lepe_n, None, lepe_o, every, RATE_VECTOR, 0.0, middle)
    for f in range(8):
        at = (slice(f, f + 1), slice(None))
        part = total_ref[10 + f // 2:11 + f // 2, 128 * (f % 2):128 * (f % 2) + 128]
        one(part, bias_w, bias_m, bias_g, bias_n, None, bias_o, at, RATE_VECTOR, 0.0, middle)
    lane = lax.broadcasted_iota(jnp.int32, (1, 4), 1)
    sums = jnp.zeros((1, 4), F32)
    for n in range(4):
        sums = jnp.where(lane == n, jnp.sum(total_ref[6 + n:7 + n], 1, keepdims=True), sums)
    rms_o[...] = jnp.sqrt(sums * (1.0 / (all_tokens * D)))
    for _, away in moves:
        away.wait()


def update_call(all_tokens, out, ig, shard, total, norm, arrays):
    V = pltpu.VMEM
    like = lambda a, dt=F32: jax.ShapeDtypeStruct(a.shape, dt)
    outs = [like(out, BF), like(ig)]
    H = pl.BlockSpec(memory_space=pl.ANY)
    for n in range(4):
        w, m = arrays[2 * n], arrays[2 * n + 1]
        outs += [like(w), like(w), like(w, BF), like(m)]
    for n in range(4, 7):
        w, m = arrays[2 * n], arrays[2 * n + 1]
        outs += [like(w), like(w), like(m)]
    outs += [jax.ShapeDtypeStruct((1, 1), F32), jax.ShapeDtypeStruct((1, 4), F32)]
    return list(pl.pallas_call(
        functools.partial(update_kernel, all_tokens),
        out_shape=tuple(outs),
        in_specs=[H, H] + [pl.BlockSpec(memory_space=V)] * (3 + len(arrays)),
        out_specs=tuple([H, H] + [pl.BlockSpec(memory_space=V)] * (len(outs) - 2)),
        scratch_shapes=[V(out.shape, BF), V(ig.shape, F32), pltpu.SemaphoreType.DMA((2, 6))],
        compiler_params=pltpu.CompilerParams(vmem_limit_bytes=60 * 2**20),
    )(out, ig, shard, total, norm, *arrays))


def flip(a):
    return jnp.swapaxes(a, -1, -2)


def shards(block_input, cotangent, *arrays):
    batch, tensor = lax.axis_size("batch"), lax.axis_size("tensor")
    arrays = list(arrays)
    for n in (2, 3, 6, 7):
        arrays[n] = flip(arrays[n])
    arrays[9], arrays[11] = jnp.swapaxes(arrays[9], 0, 1), jnp.swapaxes(arrays[11], 0, 1)
    arrays[12], arrays[13] = arrays[12].reshape(8, 128), jnp.swapaxes(arrays[13].reshape(2, 8, 128), 0, 1)
    qkv, _, proj, _, fc1, _, fc2, _, norm, _, lepe, _, bias, _ = arrays
    output, input_grad, shard, total, size = block_call(batch, tensor, True, block_input, cotangent, qkv, proj, fc1, fc2, norm, lepe, bias)
    output, input_grad, *got = update_call(block_input.shape[0] * batch * tensor, output, input_grad, shard, total, size, arrays)
    for n in (4, 5, 6, 7, 12, 13, 14, 15):
        got[n] = flip(got[n])
    got[18], got[21] = jnp.swapaxes(got[18], 0, 1), jnp.swapaxes(got[21], 0, 1)
    got[22], got[23], got[24] = got[22].reshape(1024), got[23].reshape(1024), jnp.swapaxes(got[24], 0, 1).reshape(2, 1024)
    got[25], got[26] = got[25].reshape(()), got[26].reshape(4)
    return (output, input_grad, *got)


def solution(mesh):
    token, matrix, moment = P(("batch", "tensor"), None), P("batch", "tensor"), P(None, "batch", "tensor")
    back, back_moment = P("tensor", "batch"), P(None, "tensor", "batch")
    stack, stack_moment = P(None, "batch", "tensor"), P(None, None, "batch", "tensor")
    return jax.shard_map(
        shards,
        mesh=mesh,
        in_specs=(token, token, stack, stack_moment, back, back_moment, matrix, moment, back, back_moment) + (P(),) * 6,
        out_specs=(token, token) + (stack,) * 3 + (stack_moment,) + (back,) * 3 + (back_moment,) + (matrix,) * 3 + (moment,) + (back,) * 3 + (back_moment,) + (P(),) * 11,
        check_vma=False,
    )
```

```python
import functools, math
import numpy as np
import jax, jax.numpy as jnp
from jax import lax
from jax.experimental import pallas as pl
from jax.experimental.pallas import tpu as pltpu
from jax.sharding import PartitionSpec as P

HD = 32
STEP = 10
NPARAM = 791552
CLIP_SCALE = 6.0
BETA_ONE = 0.9
BETA_TWO = 0.999
ADAM_EPS = 1e-08
DECAY_RATE = 0.05
RATE_MATRIX = 0.1
RATE_VECTOR = 0.6
GRID = 14
SPLIT = 7
CELLS = 196
PAD = 112
D = 256
FF = 1024
NORM_EPS = 1e-5
BF = jnp.bfloat16
F32 = jnp.float32
SCALE = HD ** -0.5
LOG2E = 1.4426950408889634


def slot_of(branch, cell):
    row, col = divmod(cell, GRID)
    if branch == 0:
        return row * 16 + col
    stripe, inner = divmod(col, SPLIT)
    return stripe * PAD + row * 8 + inner


def spread_tables():
    into = np.zeros((2, 4, 2 * PAD, 208), np.float32)
    for branch in range(2):
        for cell in range(CELLS):
            for j in range(4):
                into[branch, j, slot_of(branch, cell), cell + 4 * j] = 1.0
    return into.reshape(8, 2 * PAD, 208), into.transpose(0, 1, 3, 2).reshape(8, 208, 2 * PAD)


def key_mask():
    mask = np.full((2, PAD, 128), -1e30, np.float32)
    for branch in range(2):
        for cell in range(CELLS):
            slot = slot_of(branch, cell)
            if slot < PAD:
                mask[branch, slot] = 0.0
    return mask


def lane_table():
    table = np.zeros((512, 512), np.float32)
    for t in range(4):
        for j in range(4):
            for e in range(HD):
                table[t * 128 + j * 32 + e, j * 128 + t * 32 + e] = 1.0
    return table


def dot(a, b):
    return lax.dot_general(a, b, (((1,), (0,)), ((), ())), preferred_element_type=F32)


def dot_nt(a, b):
    return lax.dot_general(a, b, (((1,), (1,)), ((), ())), preferred_element_type=F32)


def norm_stats(v):
    centre = jnp.mean(v, -1, keepdims=True)
    centred = v - centre
    spread = jnp.mean(centred * centred, -1, keepdims=True)
    rate = lax.rsqrt(spread + NORM_EPS)
    return centred * rate, rate


def norm_back(grad, gain, xhat, rate):
    gx = grad * gain
    first = jnp.mean(gx, -1, keepdims=True)
    second = jnp.mean(gx * xhat, -1, keepdims=True)
    return rate * (gx - first - xhat * second)


def fold8(v):
    return jnp.sum(v.reshape(v.shape[0] // 8, 8, v.shape[1]), axis=0)


def gelu_pair(h):
    e = jnp.exp2(h * h * (-0.5 * LOG2E))
    t = 1.0 / (1.0 + (0.3275911 * math.sqrt(0.5)) * jnp.abs(h))
    poly = t * (0.5 * 0.254829592 + t * (0.5 * -0.284496736 + t * (0.5 * 1.421413741 + t * (0.5 * -1.453152027 + t * (0.5 * 1.061405429)))))
    tail = poly * e
    phi = jnp.where(h < 0, tail, 1.0 - tail)
    return h * phi, phi + h * e * (1.0 / math.sqrt(2 * math.pi))


def head_masks():
    lane = lax.broadcasted_iota(jnp.int32, (128, 128), 1) // HD
    return [jnp.where(lane == h, 1.0, 0.0).astype(BF) for h in range(4)]


def head_blocks(z, masks):
    zp = jnp.concatenate([z, jnp.zeros((16, 128), BF)], 0)
    return [zp * masks[h] for h in range(4)]


def col_shift(v):
    return pltpu.roll(v, 1, 0), v, pltpu.roll(v, PAD - 1, 0)


def row_up(u, pitch):
    return jnp.concatenate([u[pitch:], jnp.zeros((pitch, 128), F32)], 0)


def row_down(u, pitch):
    return jnp.concatenate([jnp.zeros((pitch, 128), F32), u[:-pitch]], 0)


def window_sum(v, taps, pitch):
    cols = col_shift(v)
    rows = [sum(taps[3 * i + j] * cols[j] for j in range(3)) for i in range(3)]
    return row_down(rows[0], pitch) + rows[1] + row_up(rows[2], pitch)


def window_sum_back(d, taps, pitch):
    cols = col_shift(d)
    rows = [sum(taps[3 * i + j] * cols[2 - j] for j in range(3)) for i in range(3)]
    return row_up(rows[0], pitch) + rows[1] + row_down(rows[2], pitch)


def tap_sums(d, v, pitch):
    cols = col_shift(v)
    out = []
    for i in range(3):
        moved = row_up(d, pitch) if i == 0 else (d if i == 1 else row_down(d, pitch))
        for j in range(3):
            out.append(fold8(moved * cols[j]))
    return out


MT = 784
NT_TILES = 3
MESH = pl.DeviceIdType.MESH


def block_kernel(batch, tensor, linked, *refs):
    r = dict(zip(NAMES, refs))
    x_ref, cot_ref, out_ref, ig_ref = r["x"], r["cot"], r["out"], r["ig"]
    into_ref, outof_ref, lane_ref, mask_ref = r["into"], r["outof"], r["lane"], r["mask"]
    norm_ref, lepe_ref, bias_ref = r["norm"], r["lepe"], r["bias"]
    gather_s = [r["g0"], r["g1"], r["gm"]]
    wire_s = [r["h0"], r["h1"], r["hm"]]
    in_s = [r["in0"], r["in1"], r["inm"]]
    mid_s = [r["mid0"], r["mid1"], r["midm"]]
    last_s = [r["last0"], r["last1"], r["lastm"]]
    fc1_s, fc2_s, wcat_s, proj_s, lepe_s = r["fc1"], r["fc2"], r["wcat"], r["projw"], r["lepew"]
    n1_s, n1t_s, cott_s, q_s, k_s, v_s, a_s, p_s = r["n1"], r["n1t"], r["cott"], r["q"], r["k"], r["v"], r["a"], r["p"]
    att_s, n2_s, act_s, gh_s, gb_s, ga_s, do_s = r["att"], r["n2"], r["act"], r["gh"], r["gb"], r["ga"], r["do"]
    acc_s, tacc_s, s_s, ds_s, dk_s, dv_s = r["acc"], r["tacc"], r["s"], r["ds"], r["dk"], r["dv"]
    sq_s, rows_s = r["sq"], r["rows"]
    shard_ref, total_ref, size_ref = r["shard"], r["total"], r["size"]
    dq_s, dqkv_s = a_s, gh_s

    rows = x_ref.shape[0]
    images = rows // CELLS
    chunks = images // 4
    depth = r["m1"].shape[0]

    loads = []
    for n, name in enumerate(("x", "cot", "into", "lane", "outof")):
        copy = pltpu.make_async_copy(r[name + "_hbm"], r[name], r["load_sem"].at[n])
        copy.start()
        loads.append(copy)

    if linked:
        me_b, me_t = lax.axis_index("batch"), lax.axis_index("tensor")
    else:
        me_b, me_t = 0, 0
    along_b = [(lax.rem(me_b + k, batch), me_t) for k in range(1, batch)]
    along_t = [(me_b, lax.rem(me_t + k, tensor)) for k in range(1, tensor)]
    beyond = [(lax.rem(me_b + k, batch), lax.rem(me_t + n, tensor)) for n in range(1, tensor) for k in range(1, batch)]
    sent = []

    class Push:
        def __init__(self, source, dest, peer, send, recv):
            self.copy = None
            if linked:
                self.copy = pltpu.make_async_remote_copy(src_ref=source, dst_ref=dest, send_sem=send, recv_sem=recv, device_id=peer, device_id_type=MESH)
                self.copy.start()

        def wait_recv(self):
            if self.copy is not None:
                self.copy.wait_recv()

        def wait_send(self):
            if self.copy is not None:
                self.copy.wait_send()

    def push(source, dest, peer, sems, *at):
        got = Push(source, dest, peer, r[sems + "_s"].at[at], r[sems + "_r"].at[at])
        sent.append(got)
        return got

    def arrive(copies):
        for copy in copies:
            copy.wait_recv()

    q, k, v, p = r["qkv"][0], r["qkv"][1], r["qkv"][2], r["proj"][...]
    for b in range(2):
        at = slice(b * HD, (b + 1) * HD)
        gather_s[b][me_b, me_t] = jnp.concatenate([q[:, at], k[:, at], v[:, at], p[:, at]], 1).astype(BF)
    gather_s[2][me_b, me_t, :, 0:256] = r["m1"][...].astype(BF)
    gather_s[2][me_b, me_t, :, 256:512] = r["m2"][...].astype(BF)
    if linked:
        barrier = pltpu.get_barrier_semaphore()
        everyone = along_b + along_t + beyond
        for peer in everyone:
            pl.semaphore_signal(barrier, inc=1, device_id=peer, device_id_type=MESH)
        pl.semaphore_wait(barrier, len(everyone))

    plane = [(2 * k, n) for n in range(tensor) for k in range(batch // 2) if k + n > 0]
    pair = (me_b + 1 - 2 * lax.rem(me_b, 2), me_t)
    mine = gather_s[0].at[me_b, me_t]
    first = [push(mine, mine, (lax.rem(me_b + k, batch), lax.rem(me_t + n, tensor)), "gp", at) for at, (k, n) in enumerate(plane)]
    paired = [push(mine, mine, pair, "gc", 0)]

    acc_s[...] = jnp.zeros_like(acc_s)
    lp = lepe_ref[...]
    lepe_s[0:10, :] = jnp.concatenate([lp[:, h * 64 + b * 32:h * 64 + b * 32 + 32] for b in range(2) for h in range(4)], 1)
    loads[0].wait()

    @pl.loop(0, NT_TILES, unroll=NT_TILES)
    def _(i):
        sl = pl.ds(pl.multiple_of(i * MT, 16), MT)
        xhat, rate = norm_stats(x_ref[sl, :].astype(F32))
        n1_s[sl, :] = (xhat * norm_ref[0:1, :] + norm_ref[1:2, :]).astype(BF)

    masks = head_masks()

    def spread_rows(b, c, j, source, lanes):
        return dot(into_ref[b * 4 + j], source[pl.ds(pl.multiple_of(c * 784 + 192 * j, 16), 208), lanes]).astype(BF)

    for copy in loads[1:]:
        copy.wait()
    n1t_s[...] = jnp.transpose(n1_s[...])

    for c in range(chunks):
        for j in range(4):
            for b in range(2):
                rows_s[b, c * 4 + j] = spread_rows(b, c, j, n1_s, slice(None))

    for at, (k, n) in enumerate(plane):
        first[at].wait_recv()
        slot = gather_s[0].at[lax.rem(me_b + batch - k, batch), lax.rem(me_t + tensor - n, tensor)]
        paired.append(push(slot, slot, pair, "gc", at + 1))
    got = {0: paired}
    over = [[push(gather_s[n].at[me_b, me_t], gather_s[n].at[me_b, me_t], peer, "gt", n - 1, k) for k, peer in enumerate(along_t)] for n in (1, 2)]
    cott_s[...] = jnp.transpose(cot_ref[...])

    def onward():
        for n in (1, 2):
            arrive(over[n - 1])
            row = gather_s[n].at[me_b]
            got[n] = [push(row, row, peer, "gb", n - 1, k) for k, peer in enumerate(along_b)]

    def dense_rows(b, source, dest, width):
        lanes = slice(b * width, (b + 1) * width)

        for c in range(chunks):
            tail = None
            for j in range(4):
                both = jnp.concatenate([source(c * 8 + j * 2), source(c * 8 + j * 2 + 1)], 0)
                got = dot(outof_ref[b * 4 + j], both)
                head = got[0:16] if tail is None else got[0:16] + tail
                base = c * 784 + 192 * j
                dest[pl.ds(pl.multiple_of(base, 16), 16), lanes] = head.astype(BF)
                dest[pl.ds(pl.multiple_of(base + 16, 16), 176), lanes] = got[16:192].astype(BF)
                tail = got[192:208]
                if j == 3:
                    dest[pl.ds(pl.multiple_of(base + 192, 16), 16), lanes] = tail.astype(BF)

    def scores_stage(b, s, at):
        s_s[s] = dot_nt(k_s[b, at], jnp.concatenate(head_blocks(q_s[b, at], masks), 0))

    def soft_stage(b, s, at):
        for h in range(4):
            lanes = slice(h * 128, (h + 1) * 128)
            score = s_s[s, :, lanes] * (SCALE * LOG2E) + mask_ref[b]
            e = jnp.exp2(score - jnp.max(score, 0, keepdims=True))
            p_s[b, at, :, lanes] = (e * (1.0 / jnp.sum(e, 0, keepdims=True))).astype(BF)

    def mix_stage(b, s, at):
        pitch = 16 - 8 * b
        v = v_s[b, at]
        vt = jnp.transpose(v)
        ots = [dot(vt[h * HD:(h + 1) * HD], p_s[b, at, :, h * 128:(h + 1) * 128]) for h in range(4)]
        mixed = jnp.transpose(jnp.concatenate(ots, 0))[:PAD]
        taps = [lepe_s[n:n + 1, b * 128:(b + 1) * 128] for n in range(10)]
        local = window_sum(v.astype(F32), taps, pitch) + taps[9]
        a_s[b, at] = (mixed + local).astype(BF)

    def qkv_stage(b):
        for c in range(images // 4):
            flat = jnp.concatenate([rows_s[b, c * 4 + j] for j in range(4)], 0)
            value = dot(flat, wcat_s[:, b * 384:b * 384 + 384]).astype(BF)
            for dest, at in ((q_s, 0), (k_s, 128), (v_s, 256)):
                for n in range(8):
                    dest[b, c * 8 + n] = value[n * PAD:(n + 1) * PAD, at:at + 128]

    for b in range(2):
        arrive(got[b])
        packed = jnp.concatenate([jnp.concatenate([gather_s[b][n, t] for n in range(batch)], 0) for t in range(4)], 1)
        work = dot(packed, lane_ref[...]).astype(BF)
        wcat_s[:, b * 384:(b + 1) * 384] = work[:, 0:384]
        proj_s[:, b * 128:(b + 1) * 128] = work[:, 384:512]
        qkv_stage(b)
        if b == 0:
            onward()
        for s in range(2):
            scores_stage(b, s, s)

        @pl.loop(0, images, unroll=2)
        def _(i):
            before, after = jnp.maximum(i - 1, 0), jnp.minimum(i + 1, images - 1)
            for s in range(2):
                mix_stage(b, s, before * 2 + s)
                soft_stage(b, s, i * 2 + s)
                scores_stage(b, s, after * 2 + s)

        for s in range(2):
            mix_stage(b, s, images * 2 - 2 + s)
        dense_rows(b, lambda at: a_s[b, at], att_s, 128)

    arrive(got[2])
    for t in range(4):
        for n in range(batch):
            at = slice(n * depth, (n + 1) * depth)
            fc1_s[at, t * 256:(t + 1) * 256] = gather_s[2][n, t, :, 0:256]
            fc2_s[at, t * 256:(t + 1) * 256] = gather_s[2][n, t, :, 256:512]

    @pl.loop(0, NT_TILES, unroll=NT_TILES)
    def _(i):
        sl = pl.ds(pl.multiple_of(i * MT, 16), MT)
        one = dot_nt(att_s[sl, :], proj_s[...]) + norm_ref[2:3, :]
        middle = x_ref[sl, :].astype(F32) + one
        xhat, rate = norm_stats(middle)
        n2 = (xhat * norm_ref[3:4, :] + norm_ref[4:5, :]).astype(BF)
        n2_s[sl, :] = n2
        cot = cot_ref[sl, :]
        two = jnp.zeros((MT, D), F32)
        gn = jnp.zeros((MT, D), F32)
        for f in range(4):
            fs = slice(f * 256, (f + 1) * 256)
            hidden = dot(n2, fc1_s[:, fs]) + jnp.concatenate([bias_ref[2 * f:2 * f + 1, :], bias_ref[2 * f + 1:2 * f + 2, :]], 1)
            gelu, slope = gelu_pair(hidden)
            act = gelu.astype(BF)
            act_s[sl, fs] = act
            two = two + dot_nt(act, fc2_s[:, fs])
            gh_f = dot(cot, fc2_s[:, fs]) * slope
            gh = gh_f.astype(BF)
            gh_s[sl, fs] = gh
            acc_s[10 + f] += fold8(gh.astype(F32))
            gn = gn + dot_nt(gh, fc1_s[:, fs])
        two = two + norm_ref[5:6, :]
        result = middle + two
        out_ref[sl, :] = result.astype(BF)
        acc_s[6] += fold8(one * one)
        acc_s[7] += fold8(middle * middle)
        acc_s[8] += fold8(two * two)
        acc_s[9] += fold8(result * result)
        cotf = cot.astype(F32)
        acc_s[5] += fold8(cotf)
        acc_s[3] += fold8(gn * xhat)
        acc_s[4] += fold8(gn)
        gm = cotf + norm_back(gn, norm_ref[3:4, :], xhat, rate)
        ig_ref[sl, :] = gm
        gb = gm.astype(BF)
        gb_s[sl, :] = gb
        acc_s[2] += fold8(gb.astype(F32))
        ga_s[sl, :] = dot(gb, proj_s[...]).astype(BF)

    stores = [pltpu.make_async_copy(out_ref, r["out_hbm"], r["store_sem"].at[0])]
    stores[0].start()

    def put_rows(ref, value, t, off):
        for n in range(batch):
            ref[n, t, :, off:off + value.shape[1]] = value[n * depth:(n + 1) * depth]

    def scatter_sum(n):
        return [push(wire_s[n].at[peer[0]], in_s[n].at[k], peer, "rb", n, k) for k, peer in enumerate(along_b)]

    def add_up(n, copies):
        arrive(copies)
        for t in range(tensor):
            value = wire_s[n][me_b, t].astype(F32)
            for k in range(batch - 1):
                value = value + in_s[n][k, t].astype(F32)
            mid_s[n][t] = value.astype(BF)
        return [push(mid_s[n].at[peer[1]], last_s[n].at[k], peer, "rt", n, k) for k, peer in enumerate(along_t)]

    def finish(n, copies, off):
        arrive(copies)
        shard = mid_s[n][me_t].astype(F32)
        for k in range(tensor - 1):
            shard = shard + last_s[n][k].astype(F32)
        shard_ref[:, off:off + shard.shape[1]] = shard
        squares = fold8(shard * shard)
        return sum(squares[:, m * 128:(m + 1) * 128] for m in range(shard.shape[1] // 128))

    n2t = jnp.transpose(n2_s[...])
    n1_s_t = r["n2t"]
    n1_s_t[...] = n2t
    for left, right, off in ((n1_s_t, gh_s, 0), (cott_s, act_s, 256)):
        for t in range(4):
            put_rows(wire_s[2], dot(left[...], right[:, t * 256:(t + 1) * 256]).astype(BF), t, off)
    sums_m = scatter_sum(2)
    gp = dot(jnp.transpose(gb_s[...]), att_s[...]).astype(BF)
    r["gp"][...] = gp

    def spread_do(b):
        for c in range(chunks):
            for j in range(4):
                rows_in = spread_rows(b, c, j, ga_s, slice(b * 128, (b + 1) * 128))
                for s in range(2):
                    do_s[b, c * 8 + j * 2 + s] = rows_in[s * PAD:(s + 1) * PAD]

    def dprobs_stage(b, s, at):
        s_s[s] = dot_nt(v_s[b, at], jnp.concatenate(head_blocks(do_s[b, at], masks), 0))

    def dscores_stage(b, s, at):
        for h in range(4):
            lanes = slice(h * 128, (h + 1) * 128)
            pf = p_s[b, at, :, lanes].astype(F32)
            t = pf * s_s[s, :, lanes]
            ds_s[s, :, lanes] = (t - pf * jnp.sum(t, 0, keepdims=True)).astype(BF)

    def dqkv_stage(b, s, at):
        pitch = 16 - 8 * b
        q, k, v, do = q_s[b, at], k_s[b, at], v_s[b, at], do_s[b, at]
        kt = jnp.transpose(k)
        dqt = [dot(kt[h * HD:(h + 1) * HD], ds_s[s, :, h * 128:(h + 1) * 128]) for h in range(4)]
        dv = dot(p_s[b, at], jnp.concatenate(head_blocks(do, masks), 0))
        dk = dot(ds_s[s], jnp.concatenate(head_blocks(q, masks), 0))
        dq = jnp.transpose(jnp.concatenate(dqt, 0))[:PAD]
        taps = [lepe_s[n:n + 1, b * 128:(b + 1) * 128] for n in range(10)]
        dof, vf = do.astype(F32), v.astype(F32)
        dv = dv + window_sum_back(dof, taps, pitch)
        for n, part in enumerate(tap_sums(dof, vf, pitch)):
            tacc_s[b, n] += part
        tacc_s[b, 9] += fold8(dof)
        dq_s[b, at] = (dq * SCALE).astype(BF)
        dk_s[b, at] = (dk * SCALE).astype(BF)
        dv_s[b, at] = dv.astype(BF)

    def branch_back(b):
        spread_do(b)
        for s in range(2):
            dprobs_stage(b, s, s)

        @pl.loop(0, images, unroll=2)
        def _(i):
            before, after = jnp.maximum(i - 1, 0), jnp.minimum(i + 1, images - 1)

            @pl.when(i == 1)
            def _():
                tacc_s[b] = jnp.zeros((10, 8, 128), F32)

            for s in range(2):
                dqkv_stage(b, s, before * 2 + s)
                dscores_stage(b, s, i * 2 + s)
                dprobs_stage(b, s, after * 2 + s)

        for s in range(2):
            dqkv_stage(b, s, images * 2 - 2 + s)
        if b == 1:
            smalls.append(small_out("l", pairs_of_taps(1)))
        dense_rows(b, lambda at: jnp.concatenate([dq_s[b, at], dk_s[b, at], dv_s[b, at]], 1), dqkv_s, 384)
        gw = dot(n1t_s[...], dqkv_s[:, b * 384:(b + 1) * 384]).astype(BF)
        packed = dot_nt(jnp.concatenate([gw, r["gp"][:, b * 128:(b + 1) * 128]], 1), lane_ref[...]).astype(BF)
        for t in range(4):
            for n in range(batch):
                part = packed[n * depth:(n + 1) * depth, t * 128:(t + 1) * 128]
                if b == 0:
                    wire_s[0][n, t] = part
                else:
                    wire_s[1][n % 2, n // 2, t] = part

    def pairs_of_taps(b):
        taps = jnp.sum(tacc_s[b], axis=1)
        return [jnp.concatenate([taps[2 * n:2 * n + 1], taps[2 * n + 1:2 * n + 2]], 1) for n in range(5)]

    def small_out(g, parts):
        own = r["small" + g]
        own[...] = jnp.zeros_like(own)
        for n, part in enumerate(parts):
            own[n:n + 1, :] = part
        r["smallb" + g][me_b] = own[...]
        return [push(own, r["smallb" + g].at[me_b], peer, "sb" + g, k) for k, peer in enumerate(along_b)]

    def in_order(ref, count):
        part = ref[0]
        for n in range(1, count):
            part = part + ref[n]
        return part

    def small_on(g, copies):
        arrive(copies)
        part = in_order(r["smallb" + g], batch)
        own = r["smalln" + g]
        own[...] = part
        r["smallt" + g][me_t] = part
        return [push(own, r["smallt" + g].at[me_t], peer, "st" + g, k) for k, peer in enumerate(along_t)]

    smalls = []
    branch_back(0)
    sums_0 = scatter_sum(0)
    sums = jnp.sum(acc_s[2:14], axis=1)
    smalls.append(small_out("e", [sums[n:n + 1] for n in range(12)] + pairs_of_taps(0)))
    branch_back(1)
    side = lax.rem(me_b, 2)
    across = push(wire_s[1].at[1 - side], in_s[1], pair, "rc", 0)
    last_m = add_up(2, sums_m)
    across.wait_recv()
    for n in range(batch // 2):
        mid_s[1][n] = (wire_s[1][side, n].astype(F32) + in_s[1][n].astype(F32)).astype(BF)
    half = lax.div(me_b, 2)
    last_1 = []
    for at, (k, n) in enumerate(plane):
        to_b, to_t = lax.rem(half + k // 2, batch // 2), lax.rem(me_t + n, tensor)
        last_1.append(push(mid_s[1].at[to_b, to_t], last_s[1].at[at], (2 * to_b + side, to_t), "rp", at))
    last_0 = add_up(0, sums_0)
    early, late = small_on("e", smalls[0]), small_on("l", smalls[1])

    @pl.loop(0, NT_TILES, unroll=NT_TILES)
    def _(i):
        sl = pl.ds(pl.multiple_of(i * MT, 16), MT)
        gn = dot_nt(dqkv_s[sl, 0:768], wcat_s[...])
        xhat, rate = norm_stats(x_ref[sl, :].astype(F32))
        acc_s[0] += fold8(gn * xhat)
        acc_s[1] += fold8(gn)
        ig_ref[sl, :] = ig_ref[sl, :] + norm_back(gn, norm_ref[0:1, :], xhat, rate)

    stores.append(pltpu.make_async_copy(ig_ref, r["ig_hbm"], r["store_sem"].at[1]))
    stores[1].start()
    lanes = finish(2, last_m, 0) + finish(0, last_0, 512)
    sums = jnp.sum(acc_s[0:2], axis=1)
    arrive(last_1)
    shard = mid_s[1][half, me_t].astype(F32)
    for at in range(len(plane)):
        shard = shard + last_s[1][at].astype(F32)
    shard_ref[:, 640:768] = shard
    lanes = jnp.sum(lanes + fold8(shard * shard), 0, keepdims=True)
    own = r["all"]
    own[...] = jnp.concatenate([lanes, sums[0:1], sums[1:2]], 1)
    me = me_b * tensor + me_t
    sq_s[me] = own[...]
    everyone = along_b + along_t + beyond
    square = [push(own, sq_s.at[me], peer, "sq", k) for k, peer in enumerate(everyone)]
    arrive(early)
    arrive(late)
    first_sums, last_sums = in_order(r["smallte"], tensor), in_order(r["smalltl"], tensor)
    total_ref[2:14, :] = first_sums[0:12]
    for n in range(10):
        halves = [part[:, n % 2 * 128:n % 2 * 128 + 128] for part in (first_sums[12 + n // 2:13 + n // 2], last_sums[n // 2:1 + n // 2])]
        total_ref[14 + n:15 + n, :] = jnp.concatenate([halves[b][:, h * HD:(h + 1) * HD] for h in range(4) for b in range(2)], 1)
    row = lax.broadcasted_iota(jnp.int32, first_sums.shape, 0)
    first_sums = jnp.where((row < 4) | (row >= 8), first_sums, 0.0)
    vector = jnp.sum(first_sums * first_sums, 0, keepdims=True) + jnp.sum(last_sums * last_sums, 0, keepdims=True)
    vector = jnp.sum(vector, 1, keepdims=True)
    arrive(square)
    for copy in sent:
        copy.wait_send()
    whole = in_order(sq_s, batch * tensor)
    total_ref[0:1, :] = whole[:, 128:384]
    total_ref[1:2, :] = whole[:, 384:640]
    lane = lax.broadcasted_iota(jnp.int32, whole.shape, 1)
    matrix = jnp.sum(jnp.where(lane < 128, whole, whole * whole), 1, keepdims=True)
    size_ref[...] = jnp.broadcast_to(jnp.sqrt(matrix + vector), (8, 128))
    for copy in stores:
        copy.wait()


NAMES_IN = ["x_hbm", "cot_hbm", "qkv", "proj", "m1", "m2", "norm", "lepe", "bias", "into_hbm", "outof_hbm", "mask", "lane_hbm"]
NAMES_OUT = ["out_hbm", "ig_hbm", "shard", "total", "size"]


def scratch_list(batch, tensor, rows, depth):
    n = rows // CELLS * 2
    V = pltpu.VMEM
    dma = pltpu.SemaphoreType.DMA
    stripe = (2, n, PAD, 128)
    items = [
        ("x", V((rows, D), BF)), ("cot", V((rows, D), BF)), ("out", V((rows, D), BF)), ("ig", V((rows, D), F32)),
        ("into", V((8, 2 * PAD, 208), BF)), ("outof", V((8, 208, 2 * PAD), BF)), ("lane", V((512, 512), BF)),
    ]
    for name, width in (("0", 128), ("m", 512)):
        items += [
            ("g" + name, V((batch, tensor, depth, width), BF)), ("h" + name, V((batch, tensor, depth, width), BF)), ("in" + name, V((batch - 1, tensor, depth, width), BF)),
            ("mid" + name, V((tensor, depth, width), BF)), ("last" + name, V((tensor - 1, depth, width), BF)),
        ]
    half = (batch // 2, tensor, depth, 128)
    items += [("g1", V((batch, tensor, depth, 128), BF)), ("h1", V((2,) + half, BF)), ("in1", V(half, BF)), ("mid1", V(half, BF)), ("last1", V((batch // 2 * tensor - 1, depth, 128), BF))]
    for name, count in (("e", 24), ("l", 8)):
        items += [("small" + name, V((count, D), F32)), ("smallb" + name, V((batch, count, D), F32)), ("smalln" + name, V((count, D), F32)), ("smallt" + name, V((tensor, count, D), F32))]
    items += [
        ("sq", V((batch * tensor, 1, 640), F32)), ("all", V((1, 640), F32)), ("rows", V((2, n // 2, 2 * PAD, D), BF)),
        ("fc1", V((D, FF), BF)), ("fc2", V((D, FF), BF)), ("wcat", V((D, 768), BF)), ("projw", V((D, D), BF)), ("lepew", V((16, D), F32)), ("gp", V((D, D), BF)),
        ("n1", V((rows, D), BF)), ("n1t", V((D, rows), BF)), ("cott", V((D, rows), BF)), ("n2t", V((D, rows), BF)),
        ("q", V(stripe, BF)), ("k", V(stripe, BF)), ("v", V(stripe, BF)), ("a", V(stripe, BF)),
        ("p", V((2, n, PAD, 512), BF)), ("att", V((rows, D), BF)), ("n2", V((rows, D), BF)), ("act", V((rows, FF), BF)), ("gh", V((rows, FF), BF)),
        ("gb", V((rows, D), BF)), ("ga", V((rows, D), BF)), ("do", V(stripe, BF)),
        ("acc", V((14, 8, D), F32)), ("tacc", V((2, 10, 8, 128), F32)),
        ("s", V((2, PAD, 512), F32)), ("ds", V((2, PAD, 512), BF)), ("dk", V(stripe, BF)), ("dv", V(stripe, BF)),
        ("load_sem", dma((5,))), ("store_sem", dma((2,))),
    ]
    b, t = batch - 1, tensor - 1
    for name, shape in (("gp", (batch // 2 * tensor - 1,)), ("gc", (batch // 2 * tensor,)), ("gt", (2, t)), ("gb", (2, b)), ("rb", (3, b)), ("rt", (3, t)), ("rc", (1,)), ("rp", (batch // 2 * tensor - 1,)), ("sbe", (b,)), ("ste", (t,)), ("sbl", (b,)), ("stl", (t,)), ("sq", (batch * tensor - 1,))):
        items += [(name + "_s", dma(shape)), (name + "_r", dma(shape))]
    return items


NAMES = NAMES_IN + NAMES_OUT + [name for name, _ in scratch_list(8, 4, 2352, 32)]


def block_call(batch, tensor, linked, x, cot, qkv, proj, fc1, fc2, norm, lepe, bias):
    rows, depth = x.shape[0], fc1.shape[0]
    into, outof = spread_tables()
    args = (x, cot, qkv, proj, fc1, fc2, norm, lepe, bias, jnp.asarray(into, BF), jnp.asarray(outof, BF), jnp.asarray(key_mask()), jnp.asarray(lane_table(), BF))
    V = pl.BlockSpec(memory_space=pltpu.VMEM)
    H = pl.BlockSpec(memory_space=pl.ANY)
    extra = dict(collective_id=0, has_side_effects=True) if linked else {}
    return pl.pallas_call(
        functools.partial(block_kernel, batch, tensor, linked),
        out_shape=(
            jax.ShapeDtypeStruct((rows, D), BF),
            jax.ShapeDtypeStruct((rows, D), F32),
            jax.ShapeDtypeStruct((depth, 768), F32),
            jax.ShapeDtypeStruct((24, D), F32),
            jax.ShapeDtypeStruct((8, 128), F32),
        ),
        in_specs=[H, H] + [V] * 7 + [H, H, V, H],
        out_specs=(H, H, V, V, V),
        scratch_shapes=[shape for _, shape in scratch_list(batch, tensor, rows, depth)],
        compiler_params=pltpu.CompilerParams(vmem_limit_bytes=62 * 2**20, **extra),
    )(*args)


def adam(master, first, second, clipped, rate, decay):
    first = BETA_ONE * first + (1.0 - BETA_ONE) * clipped
    second = BETA_TWO * second + (1.0 - BETA_TWO) * clipped * clipped
    hat = first * (1.0 / (1.0 - BETA_ONE**STEP))
    spread = second * (1.0 / (1.0 - BETA_TWO**STEP))
    return master - rate * (hat / (jnp.sqrt(spread) + ADAM_EPS) + decay * master), first, second


def update_kernel(
    all_tokens, out_in, ig_in, shard_ref, total_ref, norm_ref,
    qkv_w, qkv_m, proj_w, proj_m, fc1_w, fc1_m, fc2_w, fc2_m, norm_w, norm_m, lepe_w, lepe_m, bias_w, bias_m,
    out_o, ig_o, qkv_g, qkv_n, qkv_l, qkv_o, proj_g, proj_n, proj_l, proj_o, fc1_g, fc1_n, fc1_l, fc1_o, fc2_g, fc2_n, fc2_l, fc2_o,
    norm_g, norm_n, norm_o, lepe_g, lepe_n, lepe_o, bias_g, bias_n, bias_o, size_o, rms_o, out_s, ig_s, sems,
):
    moves = []
    for source, held, dest in ((out_in, out_s, out_o), (ig_in, ig_s, ig_o)):
        step = held.shape[0] // 3
        for n in range(3):
            at = pl.ds(n * step, step)
            moves.append([pltpu.make_async_copy(source.at[at], held.at[at], sems.at[0, len(moves)]), pltpu.make_async_copy(held.at[at], dest.at[at], sems.at[1, len(moves)])])
    for into, _ in moves:
        into.start()
    size = norm_ref[0:1, 0:1]
    factor = jnp.minimum(1.0, CLIP_SCALE * math.sqrt(NPARAM) / (size + 1e-06))
    size_o[...] = size

    def one(grad, w, m, g_o, n_o, l_o, m_o, at, rate, decay, pair=lambda n, at: (n,) + at):
        clipped = grad * factor
        new, first, second = adam(w[at], m[pair(0, at)], m[pair(1, at)], clipped, rate, decay)
        g_o[at] = clipped
        n_o[at] = new
        if l_o is not None:
            l_o[at] = new.astype(BF)
        m_o[pair(0, at)] = first
        m_o[pair(1, at)] = second

    for into, away in moves:
        into.wait()
        away.start()
    every = (slice(None), slice(None))
    middle = lambda n, at: (at[0], n, at[1])
    one(shard_ref[:, 0:256], fc1_w, fc1_m, fc1_g, fc1_n, fc1_l, fc1_o, every, RATE_MATRIX, DECAY_RATE)
    one(shard_ref[:, 256:512], fc2_w, fc2_m, fc2_g, fc2_n, fc2_l, fc2_o, every, RATE_MATRIX, DECAY_RATE)
    lanes = lambda j: jnp.concatenate([shard_ref[:, 512 + 32 * j:544 + 32 * j], shard_ref[:, 640 + 32 * j:672 + 32 * j]], 1)
    for j in range(3):
        one(lanes(j), qkv_w, qkv_m, qkv_g, qkv_n, qkv_l, qkv_o, (j,) + every, RATE_MATRIX, DECAY_RATE)
    one(lanes(3), proj_w, proj_m, proj_g, proj_n, proj_l, proj_o, every, RATE_MATRIX, DECAY_RATE)
    one(total_ref[0:6], norm_w, norm_m, norm_g, norm_n, None, norm_o, every, RATE_VECTOR, 0.0, middle)
    one(total_ref[14:24], lepe_w, lepe_m, lepe_g, lepe_n, None, lepe_o, every, RATE_VECTOR, 0.0, middle)
    for f in range(8):
        at = (slice(f, f + 1), slice(None))
        part = total_ref[10 + f // 2:11 + f // 2, 128 * (f % 2):128 * (f % 2) + 128]
        one(part, bias_w, bias_m, bias_g, bias_n, None, bias_o, at, RATE_VECTOR, 0.0, middle)
    lane = lax.broadcasted_iota(jnp.int32, (1, 4), 1)
    sums = jnp.zeros((1, 4), F32)
    for n in range(4):
        sums = jnp.where(lane == n, jnp.sum(total_ref[6 + n:7 + n], 1, keepdims=True), sums)
    rms_o[...] = jnp.sqrt(sums * (1.0 / (all_tokens * D)))
    for _, away in moves:
        away.wait()


def update_call(all_tokens, out, ig, shard, total, norm, arrays):
    V = pltpu.VMEM
    like = lambda a, dt=F32: jax.ShapeDtypeStruct(a.shape, dt)
    outs = [like(out, BF), like(ig)]
    H = pl.BlockSpec(memory_space=pl.ANY)
    for n in range(4):
        w, m = arrays[2 * n], arrays[2 * n + 1]
        outs += [like(w), like(w), like(w, BF), like(m)]
    for n in range(4, 7):
        w, m = arrays[2 * n], arrays[2 * n + 1]
        outs += [like(w), like(w), like(m)]
    outs += [jax.ShapeDtypeStruct((1, 1), F32), jax.ShapeDtypeStruct((1, 4), F32)]
    return list(pl.pallas_call(
        functools.partial(update_kernel, all_tokens),
        out_shape=tuple(outs),
        in_specs=[H, H] + [pl.BlockSpec(memory_space=V)] * (3 + len(arrays)),
        out_specs=tuple([H, H] + [pl.BlockSpec(memory_space=V)] * (len(outs) - 2)),
        scratch_shapes=[V(out.shape, BF), V(ig.shape, F32), pltpu.SemaphoreType.DMA((2, 6))],
        compiler_params=pltpu.CompilerParams(vmem_limit_bytes=60 * 2**20),
    )(out, ig, shard, total, norm, *arrays))


def flip(a):
    return jnp.swapaxes(a, -1, -2)


def shards(block_input, cotangent, *arrays):
    batch, tensor = lax.axis_size("batch"), lax.axis_size("tensor")
    arrays = list(arrays)
    for n in (2, 3, 6, 7):
        arrays[n] = flip(arrays[n])
    arrays[9], arrays[11] = jnp.swapaxes(arrays[9], 0, 1), jnp.swapaxes(arrays[11], 0, 1)
    arrays[12], arrays[13] = arrays[12].reshape(8, 128), jnp.swapaxes(arrays[13].reshape(2, 8, 128), 0, 1)
    qkv, _, proj, _, fc1, _, fc2, _, norm, _, lepe, _, bias, _ = arrays
    output, input_grad, shard, total, size = block_call(batch, tensor, True, block_input, cotangent, qkv, proj, fc1, fc2, norm, lepe, bias)
    output, input_grad, *got = update_call(block_input.shape[0] * batch * tensor, output, input_grad, shard, total, size, arrays)
    for n in (4, 5, 6, 7, 12, 13, 14, 15):
        got[n] = flip(got[n])
    got[18], got[21] = jnp.swapaxes(got[18], 0, 1), jnp.swapaxes(got[21], 0, 1)
    got[22], got[23], got[24] = got[22].reshape(1024), got[23].reshape(1024), jnp.swapaxes(got[24], 0, 1).reshape(2, 1024)
    got[25], got[26] = got[25].reshape(()), got[26].reshape(4)
    return (output, input_grad, *got)


def solution(mesh):
    token, matrix, moment = P(("batch", "tensor"), None), P("batch", "tensor"), P(None, "batch", "tensor")
    back, back_moment = P("tensor", "batch"), P(None, "tensor", "batch")
    stack, stack_moment = P(None, "batch", "tensor"), P(None, None, "batch", "tensor")
    return jax.shard_map(
        shards,
        mesh=mesh,
        in_specs=(token, token, stack, stack_moment, back, back_moment, matrix, moment, back, back_moment) + (P(),) * 6,
        out_specs=(token, token) + (stack,) * 3 + (stack_moment,) + (back,) * 3 + (back_moment,) + (matrix,) * 3 + (moment,) + (back,) * 3 + (back_moment,) + (P(),) * 11,
        check_vma=False,
    )
```

```python
import functools, math
import numpy as np
import jax, jax.numpy as jnp
from jax import lax
from jax.experimental import pallas as pl
from jax.experimental.pallas import tpu as pltpu
from jax.sharding import PartitionSpec as P

HD = 32
STEP = 10
NPARAM = 791552
CLIP_SCALE = 6.0
BETA_ONE = 0.9
BETA_TWO = 0.999
ADAM_EPS = 1e-08
DECAY_RATE = 0.05
RATE_MATRIX = 0.1
RATE_VECTOR = 0.6
GRID = 14
SPLIT = 7
CELLS = 196
PAD = 112
D = 256
FF = 1024
NORM_EPS = 1e-5
BF = jnp.bfloat16
F32 = jnp.float32
SCALE = HD ** -0.5
LOG2E = 1.4426950408889634


def slot_of(branch, cell):
    row, col = divmod(cell, GRID)
    if branch == 0:
        return row * 16 + col
    stripe, inner = divmod(col, SPLIT)
    return stripe * PAD + row * 8 + inner


def spread_tables():
    into = np.zeros((2, 4, 2 * PAD, 208), np.float32)
    for branch in range(2):
        for cell in range(CELLS):
            for j in range(4):
                into[branch, j, slot_of(branch, cell), cell + 4 * j] = 1.0
    return into.reshape(8, 2 * PAD, 208), into.transpose(0, 1, 3, 2).reshape(8, 208, 2 * PAD)


def key_mask():
    mask = np.full((2, PAD, 128), -1e30, np.float32)
    for branch in range(2):
        for cell in range(CELLS):
            slot = slot_of(branch, cell)
            if slot < PAD:
                mask[branch, slot] = 0.0
    return mask


def lane_table():
    table = np.zeros((512, 512), np.float32)
    for t in range(4):
        for j in range(4):
            for e in range(HD):
                table[t * 128 + j * 32 + e, j * 128 + t * 32 + e] = 1.0
    return table


def dot(a, b):
    return lax.dot_general(a, b, (((1,), (0,)), ((), ())), preferred_element_type=F32)


def dot_nt(a, b):
    return lax.dot_general(a, b, (((1,), (1,)), ((), ())), preferred_element_type=F32)


def norm_stats(v):
    centre = jnp.mean(v, -1, keepdims=True)
    centred = v - centre
    spread = jnp.mean(centred * centred, -1, keepdims=True)
    rate = lax.rsqrt(spread + NORM_EPS)
    return centred * rate, rate


def norm_back(grad, gain, xhat, rate):
    gx = grad * gain
    first = jnp.mean(gx, -1, keepdims=True)
    second = jnp.mean(gx * xhat, -1, keepdims=True)
    return rate * (gx - first - xhat * second)


def fold8(v):
    return jnp.sum(v.reshape(v.shape[0] // 8, 8, v.shape[1]), axis=0)


def gelu_pair(h):
    e = jnp.exp2(h * h * (-0.5 * LOG2E))
    phi = 0.5 + 0.5 * lax.erf(h * math.sqrt(0.5))
    return h * phi, phi + h * e * (1.0 / math.sqrt(2 * math.pi))


def head_masks():
    lane = lax.broadcasted_iota(jnp.int32, (128, 128), 1) // HD
    return [jnp.where(lane == h, 1.0, 0.0).astype(BF) for h in range(4)]


def head_blocks(z, masks):
    zp = jnp.concatenate([z, jnp.zeros((16, 128), BF)], 0)
    return [zp * masks[h] for h in range(4)]


def col_shift(v):
    return pltpu.roll(v, 1, 0), v, pltpu.roll(v, PAD - 1, 0)


def row_up(u, pitch):
    return jnp.concatenate([u[pitch:], jnp.zeros((pitch, 128), F32)], 0)


def row_down(u, pitch):
    return jnp.concatenate([jnp.zeros((pitch, 128), F32), u[:-pitch]], 0)


def window_sum(v, taps, pitch):
    cols = col_shift(v)
    rows = [sum(taps[3 * i + j] * cols[j] for j in range(3)) for i in range(3)]
    return row_down(rows[0], pitch) + rows[1] + row_up(rows[2], pitch)


def window_sum_back(d, taps, pitch):
    cols = col_shift(d)
    rows = [sum(taps[3 * i + j] * cols[2 - j] for j in range(3)) for i in range(3)]
    return row_up(rows[0], pitch) + rows[1] + row_down(rows[2], pitch)


def tap_sums(d, v, pitch):
    cols = col_shift(v)
    out = []
    for i in range(3):
        moved = row_up(d, pitch) if i == 0 else (d if i == 1 else row_down(d, pitch))
        for j in range(3):
            out.append(fold8(moved * cols[j]))
    return out


MT = 784
NT_TILES = 3
MESH = pl.DeviceIdType.MESH


def block_kernel(batch, tensor, linked, *refs):
    r = dict(zip(NAMES, refs))
    x_ref, cot_ref, out_ref, ig_ref = r["x"], r["cot"], r["out"], r["ig"]
    into_ref, outof_ref, lane_ref, mask_ref = r["into"], r["outof"], r["lane"], r["mask"]
    norm_ref, lepe_ref, bias_ref = r["norm"], r["lepe"], r["bias"]
    gather_s = [r["g0"], r["g1"], r["gm"]]
    wire_s = [r["h0"], r["h1"], r["hm"]]
    in_s = [r["in0"], r["in1"], r["inm"]]
    mid_s = [r["mid0"], r["mid1"], r["midm"]]
    last_s = [r["last0"], r["last1"], r["lastm"]]
    fc1_s, fc2_s, wcat_s, proj_s, lepe_s = r["fc1"], r["fc2"], r["wcat"], r["projw"], r["lepew"]
    n1_s, n1t_s, cott_s, q_s, k_s, v_s, a_s, p_s = r["n1"], r["n1t"], r["cott"], r["q"], r["k"], r["v"], r["a"], r["p"]
    att_s, n2_s, act_s, gh_s, gb_s, ga_s, do_s = r["att"], r["n2"], r["act"], r["gh"], r["gb"], r["ga"], r["do"]
    acc_s, tacc_s, s_s, ds_s, dk_s, dv_s = r["acc"], r["tacc"], r["s"], r["ds"], r["dk"], r["dv"]
    sq_s, rows_s = r["sq"], r["rows"]
    shard_ref, total_ref, size_ref = r["shard"], r["total"], r["size"]
    dq_s, dqkv_s = a_s, gh_s

    rows = x_ref.shape[0]
    images = rows // CELLS
    chunks = images // 4
    depth = r["m1"].shape[0]

    loads = []
    for n, name in enumerate(("x", "cot", "into", "lane", "outof")):
        copy = pltpu.make_async_copy(r[name + "_hbm"], r[name], r["load_sem"].at[n])
        copy.start()
        loads.append(copy)

    if linked:
        me_b, me_t = lax.axis_index("batch"), lax.axis_index("tensor")
    else:
        me_b, me_t = 0, 0
    along_b = [(lax.rem(me_b + k, batch), me_t) for k in range(1, batch)]
    along_t = [(me_b, lax.rem(me_t + k, tensor)) for k in range(1, tensor)]
    beyond = [(lax.rem(me_b + k, batch), lax.rem(me_t + n, tensor)) for n in range(1, tensor) for k in range(1, batch)]
    sent = []

    class Push:
        def __init__(self, source, dest, peer, send, recv):
            self.copy = None
            if linked:
                self.copy = pltpu.make_async_remote_copy(src_ref=source, dst_ref=dest, send_sem=send, recv_sem=recv, device_id=peer, device_id_type=MESH)
                self.copy.start()

        def wait_recv(self):
            if self.copy is not None:
                self.copy.wait_recv()

        def wait_send(self):
            if self.copy is not None:
                self.copy.wait_send()

    def push(source, dest, peer, sems, *at):
        got = Push(source, dest, peer, r[sems + "_s"].at[at], r[sems + "_r"].at[at])
        sent.append(got)
        return got

    def arrive(copies):
        for copy in copies:
            copy.wait_recv()

    q, k, v, p = r["qkv"][0], r["qkv"][1], r["qkv"][2], r["proj"][...]
    for b in range(2):
        at = slice(b * HD, (b + 1) * HD)
        gather_s[b][me_b, me_t] = jnp.concatenate([q[:, at], k[:, at], v[:, at], p[:, at]], 1).astype(BF)
    gather_s[2][me_b, me_t, :, 0:256] = r["m1"][...].astype(BF)
    gather_s[2][me_b, me_t, :, 256:512] = r["m2"][...].astype(BF)
    if linked:
        barrier = pltpu.get_barrier_semaphore()
        everyone = along_b + along_t + beyond
        for peer in everyone:
            pl.semaphore_signal(barrier, inc=1, device_id=peer, device_id_type=MESH)
        pl.semaphore_wait(barrier, len(everyone))

    plane = [(2 * k, n) for n in range(tensor) for k in range(batch // 2) if k + n > 0]
    pair = (me_b + 1 - 2 * lax.rem(me_b, 2), me_t)
    mine = gather_s[0].at[me_b, me_t]
    first = [push(mine, mine, (lax.rem(me_b + k, batch), lax.rem(me_t + n, tensor)), "gp", at) for at, (k, n) in enumerate(plane)]
    paired = [push(mine, mine, pair, "gc", 0)]

    acc_s[...] = jnp.zeros_like(acc_s)
    lp = lepe_ref[...]
    lepe_s[0:10, :] = jnp.concatenate([lp[:, h * 64 + b * 32:h * 64 + b * 32 + 32] for b in range(2) for h in range(4)], 1)
    loads[0].wait()

    @pl.loop(0, NT_TILES, unroll=NT_TILES)
    def _(i):
        sl = pl.ds(pl.multiple_of(i * MT, 16), MT)
        xhat, rate = norm_stats(x_ref[sl, :].astype(F32))
        n1_s[sl, :] = (xhat * norm_ref[0:1, :] + norm_ref[1:2, :]).astype(BF)

    masks = head_masks()

    def spread_rows(b, c, j, source, lanes):
        return dot(into_ref[b * 4 + j], source[pl.ds(pl.multiple_of(c * 784 + 192 * j, 16), 208), lanes]).astype(BF)

    over = [[push(gather_s[n].at[me_b, me_t], gather_s[n].at[me_b, me_t], peer, "gt", n - 1, k) for k, peer in enumerate(along_t)] for n in (1, 2)]
    for copy in loads[1:]:
        copy.wait()
    n1t_s[...] = jnp.transpose(n1_s[...])

    for c in range(chunks):
        for j in range(4):
            for b in range(2):
                rows_s[b, c * 4 + j] = spread_rows(b, c, j, n1_s, slice(None))

    for at, (k, n) in enumerate(plane):
        first[at].wait_recv()
        slot = gather_s[0].at[lax.rem(me_b + batch - k, batch), lax.rem(me_t + tensor - n, tensor)]
        paired.append(push(slot, slot, pair, "gc", at + 1))
    got = {0: paired}
    cott_s[...] = jnp.transpose(cot_ref[...])

    def onward():
        for n in (1, 2):
            arrive(over[n - 1])
            row = gather_s[n].at[me_b]
            got[n] = [push(row, row, peer, "gb", n - 1, k) for k, peer in enumerate(along_b)]

    def dense_rows(b, source, dest, width):
        lanes = slice(b * width, (b + 1) * width)

        for c in range(chunks):
            tail = None
            for j in range(4):
                both = jnp.concatenate([source(c * 8 + j * 2), source(c * 8 + j * 2 + 1)], 0)
                got = dot(outof_ref[b * 4 + j], both)
                head = got[0:16] if tail is None else got[0:16] + tail
                base = c * 784 + 192 * j
                dest[pl.ds(pl.multiple_of(base, 16), 16), lanes] = head.astype(BF)
                dest[pl.ds(pl.multiple_of(base + 16, 16), 176), lanes] = got[16:192].astype(BF)
                tail = got[192:208]
                if j == 3:
                    dest[pl.ds(pl.multiple_of(base + 192, 16), 16), lanes] = tail.astype(BF)

    def own_blocks(left, right):
        parts = []
        for g in range(2):
            both = dot(left[64 * g:64 * g + 64], right[:, 256 * g:256 * g + 256])
            parts += [both[0:32, 0:128], both[32:64, 128:256]]
        return jnp.concatenate(parts, 0)

    def scores_stage(b, s, at):
        s_s[s] = dot_nt(k_s[b, at], jnp.concatenate(head_blocks(q_s[b, at], masks), 0))

    def soft_stage(b, s, at):
        for h in range(4):
            lanes = slice(h * 128, (h + 1) * 128)
            score = s_s[s, :, lanes] * (SCALE * LOG2E) + mask_ref[b]
            e = jnp.exp2(score - jnp.max(score, 0, keepdims=True))
            p_s[b, at, :, lanes] = (e * (1.0 / jnp.sum(e, 0, keepdims=True))).astype(BF)

    def mix_stage(b, s, at):
        pitch = 16 - 8 * b
        v = v_s[b, at]
        vt = jnp.transpose(v)
        mixed = jnp.transpose(own_blocks(vt, p_s[b, at]))[:PAD]
        taps = [lepe_s[n:n + 1, b * 128:(b + 1) * 128] for n in range(10)]
        local = window_sum(v.astype(F32), taps, pitch) + taps[9]
        a_s[b, at] = (mixed + local).astype(BF)

    def qkv_stage(b):
        for c in range(images // 4):
            flat = jnp.concatenate([rows_s[b, c * 4 + j] for j in range(4)], 0)
            value = dot(flat, wcat_s[:, b * 384:b * 384 + 384]).astype(BF)
            for dest, at in ((q_s, 0), (k_s, 128), (v_s, 256)):
                for n in range(8):
                    dest[b, c * 8 + n] = value[n * PAD:(n + 1) * PAD, at:at + 128]

    for b in range(2):
        arrive(got[b])
        packed = jnp.concatenate([jnp.concatenate([gather_s[b][n, t] for n in range(batch)], 0) for t in range(4)], 1)
        work = dot(packed, lane_ref[...]).astype(BF)
        wcat_s[:, b * 384:(b + 1) * 384] = work[:, 0:384]
        proj_s[:, b * 128:(b + 1) * 128] = work[:, 384:512]
        qkv_stage(b)
        if b == 0:
            onward()
        for s in range(2):
            scores_stage(b, s, s)

        @pl.loop(0, images, unroll=2)
        def _(i):
            before, after = jnp.maximum(i - 1, 0), jnp.minimum(i + 1, images - 1)
            for s in range(2):
                mix_stage(b, s, before * 2 + s)
                soft_stage(b, s, i * 2 + s)
                scores_stage(b, s, after * 2 + s)

        for s in range(2):
            mix_stage(b, s, images * 2 - 2 + s)
        dense_rows(b, lambda at: a_s[b, at], att_s, 128)

    arrive(got[2])
    for t in range(4):
        for n in range(batch):
            at = slice(n * depth, (n + 1) * depth)
            fc1_s[at, t * 256:(t + 1) * 256] = gather_s[2][n, t, :, 0:256]
            fc2_s[at, t * 256:(t + 1) * 256] = gather_s[2][n, t, :, 256:512]

    @pl.loop(0, NT_TILES, unroll=NT_TILES)
    def _(i):
        sl = pl.ds(pl.multiple_of(i * MT, 16), MT)
        one = dot_nt(att_s[sl, :], proj_s[...]) + norm_ref[2:3, :]
        middle = x_ref[sl, :].astype(F32) + one
        xhat, rate = norm_stats(middle)
        n2 = (xhat * norm_ref[3:4, :] + norm_ref[4:5, :]).astype(BF)
        n2_s[sl, :] = n2
        cot = cot_ref[sl, :]
        two = jnp.zeros((MT, D), F32)
        gn = jnp.zeros((MT, D), F32)
        for f in range(4):
            fs = slice(f * 256, (f + 1) * 256)
            hidden = dot(n2, fc1_s[:, fs]) + jnp.concatenate([bias_ref[2 * f:2 * f + 1, :], bias_ref[2 * f + 1:2 * f + 2, :]], 1)
            gelu, slope = gelu_pair(hidden)
            act = gelu.astype(BF)
            act_s[sl, fs] = act
            two = two + dot_nt(act, fc2_s[:, fs])
            gh_f = dot(cot, fc2_s[:, fs]) * slope
            gh = gh_f.astype(BF)
            gh_s[sl, fs] = gh
            acc_s[10 + f] += fold8(gh.astype(F32))
            gn = gn + dot_nt(gh, fc1_s[:, fs])
        two = two + norm_ref[5:6, :]
        result = middle + two
        out_ref[sl, :] = result.astype(BF)
        acc_s[6] += fold8(one * one)
        acc_s[7] += fold8(middle * middle)
        acc_s[8] += fold8(two * two)
        acc_s[9] += fold8(result * result)
        cotf = cot.astype(F32)
        acc_s[5] += fold8(cotf)
        acc_s[3] += fold8(gn * xhat)
        acc_s[4] += fold8(gn)
        gm = cotf + norm_back(gn, norm_ref[3:4, :], xhat, rate)
        ig_ref[sl, :] = gm
        gb = gm.astype(BF)
        gb_s[sl, :] = gb
        acc_s[2] += fold8(gb.astype(F32))
        ga_s[sl, :] = dot(gb, proj_s[...]).astype(BF)

    stores = [pltpu.make_async_copy(out_ref, r["out_hbm"], r["store_sem"].at[0])]
    stores[0].start()

    def put_rows(ref, value, t, off):
        for n in range(batch):
            ref[n, t, :, off:off + value.shape[1]] = value[n * depth:(n + 1) * depth]

    def scatter_sum(n):
        return [push(wire_s[n].at[peer[0]], in_s[n].at[k], peer, "rb", n, k) for k, peer in enumerate(along_b)]

    def add_up(n, copies):
        arrive(copies)
        for t in range(tensor):
            value = wire_s[n][me_b, t].astype(F32)
            for k in range(batch - 1):
                value = value + in_s[n][k, t].astype(F32)
            mid_s[n][t] = value.astype(BF)
        return [push(mid_s[n].at[peer[1]], last_s[n].at[k], peer, "rt", n, k) for k, peer in enumerate(along_t)]

    def finish(n, copies, off):
        arrive(copies)
        shard = mid_s[n][me_t].astype(F32)
        for k in range(tensor - 1):
            shard = shard + last_s[n][k].astype(F32)
        shard_ref[:, off:off + shard.shape[1]] = shard
        squares = fold8(shard * shard)
        return sum(squares[:, m * 128:(m + 1) * 128] for m in range(shard.shape[1] // 128))

    n2t = jnp.transpose(n2_s[...])
    n1_s_t = r["n2t"]
    n1_s_t[...] = n2t
    for left, right, off in ((n1_s_t, gh_s, 0), (cott_s, act_s, 256)):
        for t in range(4):
            put_rows(wire_s[2], dot(left[...], right[:, t * 256:(t + 1) * 256]).astype(BF), t, off)
    sums_m = scatter_sum(2)
    gp = dot(jnp.transpose(gb_s[...]), att_s[...]).astype(BF)
    r["gp"][...] = gp

    def spread_do(b):
        for c in range(chunks):
            for j in range(4):
                rows_in = spread_rows(b, c, j, ga_s, slice(b * 128, (b + 1) * 128))
                for s in range(2):
                    do_s[b, c * 8 + j * 2 + s] = rows_in[s * PAD:(s + 1) * PAD]

    def dprobs_stage(b, s, at):
        s_s[s] = dot_nt(v_s[b, at], jnp.concatenate(head_blocks(do_s[b, at], masks), 0))

    def dscores_stage(b, s, at):
        for h in range(4):
            lanes = slice(h * 128, (h + 1) * 128)
            pf = p_s[b, at, :, lanes].astype(F32)
            t = pf * s_s[s, :, lanes]
            ds_s[s, :, lanes] = (t - pf * jnp.sum(t, 0, keepdims=True)).astype(BF)

    def dqkv_stage(b, s, at):
        pitch = 16 - 8 * b
        q, k, v, do = q_s[b, at], k_s[b, at], v_s[b, at], do_s[b, at]
        kt = jnp.transpose(k)
        dv = dot(p_s[b, at], jnp.concatenate(head_blocks(do, masks), 0))
        dk = dot(ds_s[s], jnp.concatenate(head_blocks(q, masks), 0))
        dq = jnp.transpose(own_blocks(kt, ds_s[s]))[:PAD]
        taps = [lepe_s[n:n + 1, b * 128:(b + 1) * 128] for n in range(10)]
        dof, vf = do.astype(F32), v.astype(F32)
        dv = dv + window_sum_back(dof, taps, pitch)
        for n, part in enumerate(tap_sums(dof, vf, pitch)):
            tacc_s[b, n] += part
        tacc_s[b, 9] += fold8(dof)
        dq_s[b, at] = (dq * SCALE).astype(BF)
        dk_s[b, at] = (dk * SCALE).astype(BF)
        dv_s[b, at] = dv.astype(BF)

    def branch_back(b):
        spread_do(b)
        for s in range(2):
            dprobs_stage(b, s, s)

        def step(i):
            before, after = jnp.maximum(i - 1, 0), jnp.minimum(i + 1, images - 1)

            @pl.when(i == 1)
            def _():
                tacc_s[b] = jnp.zeros((10, 8, 128), F32)

            for s in range(2):
                dqkv_stage(b, s, before * 2 + s)
                dscores_stage(b, s, i * 2 + s)
                dprobs_stage(b, s, after * 2 + s)

        pl.loop(0, images, unroll=2)(step)
        if b == 1:
            later["m"] = add_up(2, sums_m)
            later["e"] = small_on("e", smalls[0])
            later["0"] = add_up(0, sums_0)

        for s in range(2):
            dqkv_stage(b, s, images * 2 - 2 + s)
        if b == 1:
            smalls.append(small_out("l", pairs_of_taps(1)))
        dense_rows(b, lambda at: jnp.concatenate([dq_s[b, at], dk_s[b, at], dv_s[b, at]], 1), dqkv_s, 384)
        gw = dot(n1t_s[...], dqkv_s[:, b * 384:(b + 1) * 384]).astype(BF)
        packed = dot_nt(jnp.concatenate([gw, r["gp"][:, b * 128:(b + 1) * 128]], 1), lane_ref[...]).astype(BF)
        for t in range(4):
            for n in range(batch):
                part = packed[n * depth:(n + 1) * depth, t * 128:(t + 1) * 128]
                if b == 0:
                    wire_s[0][n, t] = part
                else:
                    wire_s[1][n % 2, n // 2, t] = part

    def pairs_of_taps(b):
        taps = jnp.sum(tacc_s[b], axis=1)
        return [jnp.concatenate([taps[2 * n:2 * n + 1], taps[2 * n + 1:2 * n + 2]], 1) for n in range(5)]

    def small_out(g, parts):
        own = r["small" + g]
        own[...] = jnp.zeros_like(own)
        for n, part in enumerate(parts):
            own[n:n + 1, :] = part
        r["smallb" + g][me_b] = own[...]
        return [push(own, r["smallb" + g].at[me_b], peer, "sb" + g, k) for k, peer in enumerate(along_b)]

    def in_order(ref, count):
        part = ref[0]
        for n in range(1, count):
            part = part + ref[n]
        return part

    def small_on(g, copies):
        arrive(copies)
        part = in_order(r["smallb" + g], batch)
        own = r["smalln" + g]
        own[...] = part
        r["smallt" + g][me_t] = part
        return [push(own, r["smallt" + g].at[me_t], peer, "st" + g, k) for k, peer in enumerate(along_t)]

    smalls, later = [], {}
    branch_back(0)
    sums_0 = scatter_sum(0)
    sums = jnp.sum(acc_s[2:14], axis=1)
    smalls.append(small_out("e", [sums[n:n + 1] for n in range(12)] + pairs_of_taps(0)))
    branch_back(1)
    side = lax.rem(me_b, 2)
    across = push(wire_s[1].at[1 - side], in_s[1], pair, "rc", 0)
    across.wait_recv()
    for n in range(batch // 2):
        mid_s[1][n] = (wire_s[1][side, n].astype(F32) + in_s[1][n].astype(F32)).astype(BF)
    half = lax.div(me_b, 2)
    last_1 = []
    for at, (k, n) in enumerate(plane):
        to_b, to_t = lax.rem(half + k // 2, batch // 2), lax.rem(me_t + n, tensor)
        last_1.append(push(mid_s[1].at[to_b, to_t], last_s[1].at[at], (2 * to_b + side, to_t), "rp", at))
    late = small_on("l", smalls[1])

    @pl.loop(0, NT_TILES, unroll=NT_TILES)
    def _(i):
        sl = pl.ds(pl.multiple_of(i * MT, 16), MT)
        gn = dot_nt(dqkv_s[sl, 0:768], wcat_s[...])
        xhat, rate = norm_stats(x_ref[sl, :].astype(F32))
        acc_s[0] += fold8(gn * xhat)
        acc_s[1] += fold8(gn)
        ig_ref[sl, :] = ig_ref[sl, :] + norm_back(gn, norm_ref[0:1, :], xhat, rate)

    stores.append(pltpu.make_async_copy(ig_ref, r["ig_hbm"], r["store_sem"].at[1]))
    stores[1].start()
    everyone = along_b + along_t + beyond
    me = me_b * tensor + me_t
    sums = jnp.sum(acc_s[0:2], axis=1)
    final = r["final"]
    final[...] = jnp.concatenate([sums[0:1], sums[1:2]], 1)
    r["finals"][me] = final[...]
    gains = [push(final, r["finals"].at[me], peer, "fn", k) for k, peer in enumerate(everyone)]
    lanes = finish(2, later["m"], 0) + finish(0, later["0"], 512)
    arrive(last_1)
    shard = mid_s[1][half, me_t].astype(F32)
    for at in range(len(plane)):
        shard = shard + last_s[1][at].astype(F32)
    shard_ref[:, 640:768] = shard
    lanes = jnp.sum(lanes + fold8(shard * shard), 0, keepdims=True)
    own = r["all"]
    own[...] = lanes
    sq_s[me] = own[...]
    square = [push(own, sq_s.at[me], peer, "sq", k) for k, peer in enumerate(everyone)]
    arrive(later["e"])
    arrive(late)
    first_sums, last_sums = in_order(r["smallte"], tensor), in_order(r["smalltl"], tensor)
    total_ref[2:14, :] = first_sums[0:12]
    for n in range(10):
        halves = [part[:, n % 2 * 128:n % 2 * 128 + 128] for part in (first_sums[12 + n // 2:13 + n // 2], last_sums[n // 2:1 + n // 2])]
        total_ref[14 + n:15 + n, :] = jnp.concatenate([halves[b][:, h * HD:(h + 1) * HD] for h in range(4) for b in range(2)], 1)
    row = lax.broadcasted_iota(jnp.int32, first_sums.shape, 0)
    first_sums = jnp.where((row < 4) | (row >= 8), first_sums, 0.0)
    vector = jnp.sum(first_sums * first_sums, 0, keepdims=True) + jnp.sum(last_sums * last_sums, 0, keepdims=True)
    vector = jnp.sum(vector, 1, keepdims=True)
    arrive(gains)
    whole = in_order(r["finals"], batch * tensor)
    total_ref[0:1, :] = whole[:, 0:256]
    total_ref[1:2, :] = whole[:, 256:512]
    vector = vector + jnp.sum(whole * whole, 1, keepdims=True)
    arrive(square)
    for copy in sent:
        copy.wait_send()
    matrix = jnp.sum(in_order(sq_s, batch * tensor), 1, keepdims=True)
    size_ref[...] = jnp.broadcast_to(jnp.sqrt(matrix + vector), (8, 128))
    for copy in stores:
        copy.wait()


NAMES_IN = ["x_hbm", "cot_hbm", "qkv", "proj", "m1", "m2", "norm", "lepe", "bias", "into_hbm", "outof_hbm", "mask", "lane_hbm"]
NAMES_OUT = ["out_hbm", "ig_hbm", "shard", "total", "size"]


def scratch_list(batch, tensor, rows, depth):
    n = rows // CELLS * 2
    V = pltpu.VMEM
    dma = pltpu.SemaphoreType.DMA
    stripe = (2, n, PAD, 128)
    items = [
        ("x", V((rows, D), BF)), ("cot", V((rows, D), BF)), ("out", V((rows, D), BF)), ("ig", V((rows, D), F32)),
        ("into", V((8, 2 * PAD, 208), BF)), ("outof", V((8, 208, 2 * PAD), BF)), ("lane", V((512, 512), BF)),
    ]
    for name, width in (("0", 128), ("m", 512)):
        items += [
            ("g" + name, V((batch, tensor, depth, width), BF)), ("h" + name, V((batch, tensor, depth, width), BF)), ("in" + name, V((batch - 1, tensor, depth, width), BF)),
            ("mid" + name, V((tensor, depth, width), BF)), ("last" + name, V((tensor - 1, depth, width), BF)),
        ]
    half = (batch // 2, tensor, depth, 128)
    items += [("g1", V((batch, tensor, depth, 128), BF)), ("h1", V((2,) + half, BF)), ("in1", V(half, BF)), ("mid1", V(half, BF)), ("last1", V((batch // 2 * tensor - 1, depth, 128), BF))]
    for name, count in (("e", 24), ("l", 8)):
        items += [("small" + name, V((count, D), F32)), ("smallb" + name, V((batch, count, D), F32)), ("smalln" + name, V((count, D), F32)), ("smallt" + name, V((tensor, count, D), F32))]
    items += [
        ("sq", V((batch * tensor, 1, 128), F32)), ("all", V((1, 128), F32)), ("finals", V((batch * tensor, 1, 512), F32)), ("final", V((1, 512), F32)), ("rows", V((2, n // 2, 2 * PAD, D), BF)),
        ("fc1", V((D, FF), BF)), ("fc2", V((D, FF), BF)), ("wcat", V((D, 768), BF)), ("projw", V((D, D), BF)), ("lepew", V((16, D), F32)), ("gp", V((D, D), BF)),
        ("n1", V((rows, D), BF)), ("n1t", V((D, rows), BF)), ("cott", V((D, rows), BF)), ("n2t", V((D, rows), BF)),
        ("q", V(stripe, BF)), ("k", V(stripe, BF)), ("v", V(stripe, BF)), ("a", V(stripe, BF)),
        ("p", V((2, n, PAD, 512), BF)), ("att", V((rows, D), BF)), ("n2", V((rows, D), BF)), ("act", V((rows, FF), BF)), ("gh", V((rows, FF), BF)),
        ("gb", V((rows, D), BF)), ("ga", V((rows, D), BF)), ("do", V(stripe, BF)),
        ("acc", V((14, 8, D), F32)), ("tacc", V((2, 10, 8, 128), F32)),
        ("s", V((2, PAD, 512), F32)), ("ds", V((2, PAD, 512), BF)), ("dk", V(stripe, BF)), ("dv", V(stripe, BF)),
        ("load_sem", dma((5,))), ("store_sem", dma((2,))),
    ]
    b, t = batch - 1, tensor - 1
    for name, shape in (("gp", (batch // 2 * tensor - 1,)), ("gc", (batch // 2 * tensor,)), ("gt", (2, t)), ("gb", (2, b)), ("rb", (3, b)), ("rt", (3, t)), ("rc", (1,)), ("rp", (batch // 2 * tensor - 1,)), ("sbe", (b,)), ("ste", (t,)), ("sbl", (b,)), ("stl", (t,)), ("sq", (batch * tensor - 1,)), ("fn", (batch * tensor - 1,))):
        items += [(name + "_s", dma(shape)), (name + "_r", dma(shape))]
    return items


NAMES = NAMES_IN + NAMES_OUT + [name for name, _ in scratch_list(8, 4, 2352, 32)]


def block_call(batch, tensor, linked, x, cot, qkv, proj, fc1, fc2, norm, lepe, bias):
    rows, depth = x.shape[0], fc1.shape[0]
    into, outof = spread_tables()
    args = (x, cot, qkv, proj, fc1, fc2, norm, lepe, bias, jnp.asarray(into, BF), jnp.asarray(outof, BF), jnp.asarray(key_mask()), jnp.asarray(lane_table(), BF))
    V = pl.BlockSpec(memory_space=pltpu.VMEM)
    H = pl.BlockSpec(memory_space=pl.ANY)
    extra = dict(collective_id=0, has_side_effects=True) if linked else {}
    return pl.pallas_call(
        functools.partial(block_kernel, batch, tensor, linked),
        out_shape=(
            jax.ShapeDtypeStruct((rows, D), BF),
            jax.ShapeDtypeStruct((rows, D), F32),
            jax.ShapeDtypeStruct((depth, 768), F32),
            jax.ShapeDtypeStruct((24, D), F32),
            jax.ShapeDtypeStruct((8, 128), F32),
        ),
        in_specs=[H, H] + [V] * 7 + [H, H, V, H],
        out_specs=(H, H, V, V, V),
        scratch_shapes=[shape for _, shape in scratch_list(batch, tensor, rows, depth)],
        compiler_params=pltpu.CompilerParams(vmem_limit_bytes=62 * 2**20, **extra),
    )(*args)


def adam(master, first, second, clipped, rate, decay):
    first = BETA_ONE * first + (1.0 - BETA_ONE) * clipped
    second = BETA_TWO * second + (1.0 - BETA_TWO) * clipped * clipped
    hat = first * (1.0 / (1.0 - BETA_ONE**STEP))
    spread = second * (1.0 / (1.0 - BETA_TWO**STEP))
    return master - rate * (hat / (jnp.sqrt(spread) + ADAM_EPS) + decay * master), first, second


def update_kernel(all_tokens, count_in, count_out, *refs):
    ins, refs = refs[:count_in], refs[count_in:]
    outs, refs = refs[:count_out], refs[count_out:]
    size_o, rms_o, refs = refs[0], refs[1], refs[2:]
    held_in, refs = refs[:count_in], refs[count_in:]
    held_out, (in_sem, out_sem, move_sem) = refs[:count_out], refs[count_out:]

    moves = []
    for n in range(2):
        step = held_in[n].shape[0] // 3
        for m in range(3):
            at = pl.ds(m * step, step)
            k = len(moves)
            moves.append((pltpu.make_async_copy(ins[n].at[at], held_in[n].at[at], move_sem.at[0, k]), pltpu.make_async_copy(held_in[n].at[at], outs[n].at[at], move_sem.at[1, k])))
    reads = [pltpu.make_async_copy(source, held, in_sem.at[n]) for n, (source, held) in enumerate(zip(ins[2:], held_in[2:]))]
    for copy in reads:
        copy.start()
    for into, _ in moves:
        into.start()
    for copy in reads:
        copy.wait()
    writes = []

    def write(n):
        copy = pltpu.make_async_copy(held_out[n], outs[n], out_sem.at[n - 2])
        copy.start()
        writes.append(copy)

    shard_ref, total_ref, norm_ref = held_in[2:5]
    size = norm_ref[0:1, 0:1]
    factor = jnp.minimum(1.0, CLIP_SCALE * math.sqrt(NPARAM) / (size + 1e-06))
    size_o[...] = size

    def one(grad, w, m, g_o, n_o, l_o, m_o, at, rate, decay, pair=lambda n, at: (n,) + at):
        clipped = grad * factor
        new, first, second = adam(w[at], m[pair(0, at)], m[pair(1, at)], clipped, rate, decay)
        g_o[at] = clipped
        n_o[at] = new
        if l_o is not None:
            l_o[at] = new.astype(BF)
        m_o[pair(0, at)] = first
        m_o[pair(1, at)] = second

    every = (slice(None), slice(None))
    middle = lambda n, at: (at[0], n, at[1])
    given = held_in[5:]
    lanes = lambda j: jnp.concatenate([shard_ref[:, 512 + 32 * j:544 + 32 * j], shard_ref[:, 640 + 32 * j:672 + 32 * j]], 1)
    grads = [[((j,) + every, lanes(j)) for j in range(3)], [(every, lanes(3))], [(every, shard_ref[:, 0:256])], [(every, shard_ref[:, 256:512])]]
    for n in range(4):
        made = held_out[2 + 4 * n:6 + 4 * n]
        for at, grad in grads[n]:
            one(grad, given[2 * n], given[2 * n + 1], *made, at, RATE_MATRIX, DECAY_RATE)
        for k in range(4):
            write(2 + 4 * n + k)
    bias = [((slice(f, f + 1), slice(None)), total_ref[10 + f // 2:11 + f // 2, 128 * (f % 2):128 * (f % 2) + 128]) for f in range(8)]
    for n, parts in enumerate(([(every, total_ref[0:6])], [(every, total_ref[14:24])], bias)):
        made = held_out[18 + 3 * n:21 + 3 * n]
        for at, grad in parts:
            one(grad, given[8 + 2 * n], given[9 + 2 * n], made[0], made[1], None, made[2], at, RATE_VECTOR, 0.0, middle)
        for k in range(3):
            write(18 + 3 * n + k)
    for into, away in moves:
        into.wait()
        away.start()
    lane = lax.broadcasted_iota(jnp.int32, (1, 4), 1)
    sums = jnp.zeros((1, 4), F32)
    for n in range(4):
        sums = jnp.where(lane == n, jnp.sum(total_ref[6 + n:7 + n], 1, keepdims=True), sums)
    rms_o[...] = jnp.sqrt(sums * (1.0 / (all_tokens * D)))
    for copy in writes:
        copy.wait()
    for _, away in moves:
        away.wait()


def update_call(all_tokens, out, ig, shard, total, norm, arrays):
    V = pltpu.VMEM
    dma = pltpu.SemaphoreType.DMA
    like = lambda a, dt=F32: jax.ShapeDtypeStruct(a.shape, dt)
    outs = [like(out, BF), like(ig)]
    for n in range(4):
        w, m = arrays[2 * n], arrays[2 * n + 1]
        outs += [like(w), like(w), like(w, BF), like(m)]
    for n in range(4, 7):
        w, m = arrays[2 * n], arrays[2 * n + 1]
        outs += [like(w), like(w), like(m)]
    ins = (out, ig, shard, total, norm, *arrays)
    H = pl.BlockSpec(memory_space=pl.ANY)
    held_out = [V((8, 128), F32)] * 2 + [V(o.shape, o.dtype) for o in outs[2:]]
    return list(pl.pallas_call(
        functools.partial(update_kernel, all_tokens, len(ins), len(outs)),
        out_shape=tuple(outs + [jax.ShapeDtypeStruct((1, 1), F32), jax.ShapeDtypeStruct((1, 4), F32)]),
        in_specs=[H] * len(ins),
        out_specs=tuple([H] * len(outs) + [pl.BlockSpec(memory_space=V)] * 2),
        scratch_shapes=[V(a.shape, a.dtype) for a in ins] + held_out + [dma((len(ins) - 2,)), dma((len(outs) - 2,)), dma((2, 6))],
        compiler_params=pltpu.CompilerParams(vmem_limit_bytes=60 * 2**20),
    )(*ins))


def flip(a):
    return jnp.swapaxes(a, -1, -2)


def shards(block_input, cotangent, *arrays):
    batch, tensor = lax.axis_size("batch"), lax.axis_size("tensor")
    arrays = list(arrays)
    for n in (2, 3, 6, 7):
        arrays[n] = flip(arrays[n])
    arrays[9], arrays[11] = jnp.swapaxes(arrays[9], 0, 1), jnp.swapaxes(arrays[11], 0, 1)
    arrays[12], arrays[13] = arrays[12].reshape(8, 128), jnp.swapaxes(arrays[13].reshape(2, 8, 128), 0, 1)
    qkv, _, proj, _, fc1, _, fc2, _, norm, _, lepe, _, bias, _ = arrays
    output, input_grad, shard, total, size = block_call(batch, tensor, True, block_input, cotangent, qkv, proj, fc1, fc2, norm, lepe, bias)
    output, input_grad, *got = update_call(block_input.shape[0] * batch * tensor, output, input_grad, shard, total, size, arrays)
    for n in (4, 5, 6, 7, 12, 13, 14, 15):
        got[n] = flip(got[n])
    got[18], got[21] = jnp.swapaxes(got[18], 0, 1), jnp.swapaxes(got[21], 0, 1)
    got[22], got[23], got[24] = got[22].reshape(1024), got[23].reshape(1024), jnp.swapaxes(got[24], 0, 1).reshape(2, 1024)
    got[25], got[26] = got[25].reshape(()), got[26].reshape(4)
    return (output, input_grad, *got)


def solution(mesh):
    token, matrix, moment = P(("batch", "tensor"), None), P("batch", "tensor"), P(None, "batch", "tensor")
    back, back_moment = P("tensor", "batch"), P(None, "tensor", "batch")
    stack, stack_moment = P(None, "batch", "tensor"), P(None, None, "batch", "tensor")
    return jax.shard_map(
        shards,
        mesh=mesh,
        in_specs=(token, token, stack, stack_moment, back, back_moment, matrix, moment, back, back_moment) + (P(),) * 6,
        out_specs=(token, token) + (stack,) * 3 + (stack_moment,) + (back,) * 3 + (back_moment,) + (matrix,) * 3 + (moment,) + (back,) * 3 + (back_moment,) + (P(),) * 11,
        check_vma=False,
    )
```

```python
import functools, math
import numpy as np
import jax, jax.numpy as jnp
from jax import lax
from jax.experimental import pallas as pl
from jax.experimental.pallas import tpu as pltpu
from jax.sharding import PartitionSpec as P

HD = 32
STEP = 10
NPARAM = 791552
CLIP_SCALE = 6.0
BETA_ONE = 0.9
BETA_TWO = 0.999
ADAM_EPS = 1e-08
DECAY_RATE = 0.05
RATE_MATRIX = 0.1
RATE_VECTOR = 0.6
GRID = 14
SPLIT = 7
CELLS = 196
PAD = 112
D = 256
FF = 1024
NORM_EPS = 1e-5
BF = jnp.bfloat16
F32 = jnp.float32
SCALE = HD ** -0.5
LOG2E = 1.4426950408889634


def slot_of(branch, cell):
    row, col = divmod(cell, GRID)
    if branch == 0:
        return row * 16 + col
    stripe, inner = divmod(col, SPLIT)
    return stripe * PAD + row * 8 + inner


def spread_tables():
    into = np.zeros((2, 4, 2 * PAD, 208), np.float32)
    for branch in range(2):
        for cell in range(CELLS):
            for j in range(4):
                into[branch, j, slot_of(branch, cell), cell + 4 * j] = 1.0
    return into.reshape(8, 2 * PAD, 208), into.transpose(0, 1, 3, 2).reshape(8, 208, 2 * PAD)


def key_mask():
    mask = np.full((2, PAD, 128), -1e30, np.float32)
    for branch in range(2):
        for cell in range(CELLS):
            slot = slot_of(branch, cell)
            if slot < PAD:
                mask[branch, slot] = 0.0
    return mask


def lane_table():
    table = np.zeros((512, 512), np.float32)
    for t in range(4):
        for j in range(4):
            for e in range(HD):
                table[t * 128 + j * 32 + e, j * 128 + t * 32 + e] = 1.0
    return table


def dot(a, b):
    return lax.dot_general(a, b, (((1,), (0,)), ((), ())), preferred_element_type=F32)


def dot_nt(a, b):
    return lax.dot_general(a, b, (((1,), (1,)), ((), ())), preferred_element_type=F32)


def norm_stats(v):
    centre = jnp.mean(v, -1, keepdims=True)
    centred = v - centre
    spread = jnp.mean(centred * centred, -1, keepdims=True)
    rate = lax.rsqrt(spread + NORM_EPS)
    return centred * rate, rate


def norm_back(grad, gain, xhat, rate):
    gx = grad * gain
    first = jnp.mean(gx, -1, keepdims=True)
    second = jnp.mean(gx * xhat, -1, keepdims=True)
    return rate * (gx - first - xhat * second)


def fold8(v):
    return jnp.sum(v.reshape(v.shape[0] // 8, 8, v.shape[1]), axis=0)


def gelu_pair(h):
    e = jnp.exp2(h * h * (-0.5 * LOG2E))
    phi = 0.5 + 0.5 * lax.erf(h * math.sqrt(0.5))
    return h * phi, phi + h * e * (1.0 / math.sqrt(2 * math.pi))


def head_masks():
    lane = lax.broadcasted_iota(jnp.int32, (128, 128), 1) // HD
    return [jnp.where(lane == h, 1.0, 0.0).astype(BF) for h in range(4)]


def head_blocks(z, masks):
    zp = jnp.concatenate([z, jnp.zeros((16, 128), BF)], 0)
    return [zp * masks[h] for h in range(4)]


def col_shift(v):
    return pltpu.roll(v, 1, 0), v, pltpu.roll(v, PAD - 1, 0)


def row_up(u, pitch):
    return jnp.concatenate([u[pitch:], jnp.zeros((pitch, 128), F32)], 0)


def row_down(u, pitch):
    return jnp.concatenate([jnp.zeros((pitch, 128), F32), u[:-pitch]], 0)


def window_sum(v, taps, pitch):
    cols = col_shift(v)
    rows = [sum(taps[3 * i + j] * cols[j] for j in range(3)) for i in range(3)]
    return row_down(rows[0], pitch) + rows[1] + row_up(rows[2], pitch)


def window_sum_back(d, taps, pitch):
    cols = col_shift(d)
    rows = [sum(taps[3 * i + j] * cols[2 - j] for j in range(3)) for i in range(3)]
    return row_up(rows[0], pitch) + rows[1] + row_down(rows[2], pitch)


def tap_sums(d, v, pitch):
    cols = col_shift(v)
    out = []
    for i in range(3):
        moved = row_up(d, pitch) if i == 0 else (d if i == 1 else row_down(d, pitch))
        for j in range(3):
            out.append(fold8(moved * cols[j]))
    return out


MT = 784
NT_TILES = 3
MESH = pl.DeviceIdType.MESH


def block_kernel(batch, tensor, linked, *refs):
    r = dict(zip(NAMES, refs))
    x_ref, cot_ref, out_ref, ig_ref = r["x"], r["cot"], r["out"], r["ig"]
    into_ref, outof_ref, lane_ref, mask_ref = r["into"], r["outof"], r["lane"], r["mask"]
    norm_ref, lepe_ref, bias_ref = r["norm"], r["lepe"], r["bias"]
    gather_s = [r["g0"], r["g1"], r["gm"]]
    wire_s = [r["h0"], r["h1"], r["hm"]]
    in_s = [r["in0"], r["in1"], r["inm"]]
    mid_s = [r["mid0"], r["mid1"], r["midm"]]
    last_s = [r["last0"], r["last1"], r["lastm"]]
    fc1_s, fc2_s, wcat_s, proj_s, lepe_s = r["fc1"], r["fc2"], r["wcat"], r["projw"], r["lepew"]
    n1_s, n1t_s, cott_s, q_s, k_s, v_s, a_s, p_s = r["n1"], r["n1t"], r["cott"], r["q"], r["k"], r["v"], r["a"], r["p"]
    att_s, n2_s, act_s, gh_s, gb_s, ga_s, do_s = r["att"], r["n2"], r["act"], r["gh"], r["gb"], r["ga"], r["do"]
    acc_s, tacc_s, s_s, ds_s, dk_s, dv_s = r["acc"], r["tacc"], r["s"], r["ds"], r["dk"], r["dv"]
    sq_s, rows_s = r["sq"], r["rows"]
    shard_ref, total_ref, size_ref = r["shard"], r["total"], r["size"]
    dq_s, dqkv_s = a_s, gh_s

    rows = x_ref.shape[0]
    images = rows // CELLS
    chunks = images // 4
    depth = r["m1"].shape[0]

    loads = []
    for n, name in enumerate(("x", "cot", "into", "lane", "outof")):
        copy = pltpu.make_async_copy(r[name + "_hbm"], r[name], r["load_sem"].at[n])
        copy.start()
        loads.append(copy)

    if linked:
        me_b, me_t = lax.axis_index("batch"), lax.axis_index("tensor")
    else:
        me_b, me_t = 0, 0
    along_b = [(lax.rem(me_b + k, batch), me_t) for k in range(1, batch)]
    along_t = [(me_b, lax.rem(me_t + k, tensor)) for k in range(1, tensor)]
    beyond = [(lax.rem(me_b + k, batch), lax.rem(me_t + n, tensor)) for n in range(1, tensor) for k in range(1, batch)]
    sent = []

    class Push:
        def __init__(self, source, dest, peer, send, recv):
            self.copy = None
            if linked:
                self.copy = pltpu.make_async_remote_copy(src_ref=source, dst_ref=dest, send_sem=send, recv_sem=recv, device_id=peer, device_id_type=MESH)
                self.copy.start()

        def wait_recv(self):
            if self.copy is not None:
                self.copy.wait_recv()

        def wait_send(self):
            if self.copy is not None:
                self.copy.wait_send()

    def push(source, dest, peer, sems, *at):
        got = Push(source, dest, peer, r[sems + "_s"].at[at], r[sems + "_r"].at[at])
        sent.append(got)
        return got

    def arrive(copies):
        for copy in copies:
            copy.wait_recv()

    q, k, v, p = r["qkv"][0], r["qkv"][1], r["qkv"][2], r["proj"][...]
    for b in range(2):
        at = slice(b * HD, (b + 1) * HD)
        gather_s[b][me_b, me_t] = jnp.concatenate([q[:, at], k[:, at], v[:, at], p[:, at]], 1).astype(BF)
    gather_s[2][me_b, me_t, :, 0:256] = r["m1"][...].astype(BF)
    gather_s[2][me_b, me_t, :, 256:512] = r["m2"][...].astype(BF)
    if linked:
        barrier = pltpu.get_barrier_semaphore()
        everyone = along_b + along_t + beyond
        for peer in everyone:
            pl.semaphore_signal(barrier, inc=1, device_id=peer, device_id_type=MESH)
        pl.semaphore_wait(barrier, len(everyone))

    plane = [(2 * k, n) for n in range(tensor) for k in range(batch // 2) if k + n > 0]
    pair = (me_b + 1 - 2 * lax.rem(me_b, 2), me_t)
    mine = gather_s[0].at[me_b, me_t]
    first = [push(mine, mine, (lax.rem(me_b + k, batch), lax.rem(me_t + n, tensor)), "gp", at) for at, (k, n) in enumerate(plane)]
    paired = [push(mine, mine, pair, "gc", 0)]

    acc_s[...] = jnp.zeros_like(acc_s)
    lp = lepe_ref[...]
    lepe_s[0:10, :] = jnp.concatenate([lp[:, h * 64 + b * 32:h * 64 + b * 32 + 32] for b in range(2) for h in range(4)], 1)
    loads[0].wait()

    @pl.loop(0, NT_TILES, unroll=NT_TILES)
    def _(i):
        sl = pl.ds(pl.multiple_of(i * MT, 16), MT)
        xhat, rate = norm_stats(x_ref[sl, :].astype(F32))
        n1_s[sl, :] = (xhat * norm_ref[0:1, :] + norm_ref[1:2, :]).astype(BF)

    masks = head_masks()

    def spread_rows(b, c, j, source, lanes):
        return dot(into_ref[b * 4 + j], source[pl.ds(pl.multiple_of(c * 784 + 192 * j, 16), 208), lanes]).astype(BF)

    over = [[push(gather_s[n].at[me_b, me_t], gather_s[n].at[me_b, me_t], peer, "gt", n - 1, k) for k, peer in enumerate(along_t)] for n in (1, 2)]
    for copy in loads[1:]:
        copy.wait()
    n1t_s[...] = jnp.transpose(n1_s[...])

    for c in range(chunks):
        for j in range(4):
            for b in range(2):
                rows_s[b, c * 4 + j] = spread_rows(b, c, j, n1_s, slice(None))

    for at, (k, n) in enumerate(plane):
        first[at].wait_recv()
        slot = gather_s[0].at[lax.rem(me_b + batch - k, batch), lax.rem(me_t + tensor - n, tensor)]
        paired.append(push(slot, slot, pair, "gc", at + 1))
    got = {0: paired}
    cott_s[...] = jnp.transpose(cot_ref[...])

    def onward():
        for n in (1, 2):
            arrive(over[n - 1])
            row = gather_s[n].at[me_b]
            got[n] = [push(row, row, peer, "gb", n - 1, k) for k, peer in enumerate(along_b)]

    def dense_rows(b, source, dest, width):
        lanes = slice(b * width, (b + 1) * width)

        for c in range(chunks):
            tail = None
            for j in range(4):
                both = jnp.concatenate([source(c * 8 + j * 2), source(c * 8 + j * 2 + 1)], 0)
                got = dot(outof_ref[b * 4 + j], both)
                head = got[0:16] if tail is None else got[0:16] + tail
                base = c * 784 + 192 * j
                dest[pl.ds(pl.multiple_of(base, 16), 16), lanes] = head.astype(BF)
                dest[pl.ds(pl.multiple_of(base + 16, 16), 176), lanes] = got[16:192].astype(BF)
                tail = got[192:208]
                if j == 3:
                    dest[pl.ds(pl.multiple_of(base + 192, 16), 16), lanes] = tail.astype(BF)

    def own_blocks(left, right):
        parts = []
        for g in range(2):
            both = dot(left[64 * g:64 * g + 64], right[:, 256 * g:256 * g + 256])
            parts += [both[0:32, 0:128], both[32:64, 128:256]]
        return jnp.concatenate(parts, 0)

    def scores_stage(b, s, at):
        s_s[s] = dot_nt(k_s[b, at], jnp.concatenate(head_blocks(q_s[b, at], masks), 0))

    def soft_stage(b, s, at):
        for h in range(4):
            lanes = slice(h * 128, (h + 1) * 128)
            score = s_s[s, :, lanes] * (SCALE * LOG2E) + mask_ref[b]
            e = jnp.exp2(score - jnp.max(score, 0, keepdims=True))
            p_s[b, at, :, lanes] = (e * (1.0 / jnp.sum(e, 0, keepdims=True))).astype(BF)

    def mix_stage(b, s, at):
        pitch = 16 - 8 * b
        v = v_s[b, at]
        vt = jnp.transpose(v)
        mixed = jnp.transpose(own_blocks(vt, p_s[b, at]))[:PAD]
        taps = [lepe_s[n:n + 1, b * 128:(b + 1) * 128] for n in range(10)]
        local = window_sum(v.astype(F32), taps, pitch) + taps[9]
        a_s[b, at] = (mixed + local).astype(BF)

    def qkv_stage(b):
        for c in range(images // 4):
            flat = jnp.concatenate([rows_s[b, c * 4 + j] for j in range(4)], 0)
            value = dot(flat, wcat_s[:, b * 384:b * 384 + 384]).astype(BF)
            for dest, at in ((q_s, 0), (k_s, 128), (v_s, 256)):
                for n in range(8):
                    dest[b, c * 8 + n] = value[n * PAD:(n + 1) * PAD, at:at + 128]

    for b in range(2):
        arrive(got[b])
        packed = jnp.concatenate([jnp.concatenate([gather_s[b][n, t] for n in range(batch)], 0) for t in range(4)], 1)
        work = dot(packed, lane_ref[...]).astype(BF)
        wcat_s[:, b * 384:(b + 1) * 384] = work[:, 0:384]
        proj_s[:, b * 128:(b + 1) * 128] = work[:, 384:512]
        qkv_stage(b)
        if b == 0:
            onward()
        for s in range(2):
            scores_stage(b, s, s)

        @pl.loop(0, images, unroll=2)
        def _(i):
            before, after = jnp.maximum(i - 1, 0), jnp.minimum(i + 1, images - 1)
            for s in range(2):
                mix_stage(b, s, before * 2 + s)
                soft_stage(b, s, i * 2 + s)
                scores_stage(b, s, after * 2 + s)

        for s in range(2):
            mix_stage(b, s, images * 2 - 2 + s)
        dense_rows(b, lambda at: a_s[b, at], att_s, 128)

    arrive(got[2])
    for t in range(4):
        for n in range(batch):
            at = slice(n * depth, (n + 1) * depth)
            fc1_s[at, t * 256:(t + 1) * 256] = gather_s[2][n, t, :, 0:256]
            fc2_s[at, t * 256:(t + 1) * 256] = gather_s[2][n, t, :, 256:512]

    @pl.loop(0, NT_TILES, unroll=NT_TILES)
    def _(i):
        sl = pl.ds(pl.multiple_of(i * MT, 16), MT)
        one = dot_nt(att_s[sl, :], proj_s[...]) + norm_ref[2:3, :]
        middle = x_ref[sl, :].astype(F32) + one
        xhat, rate = norm_stats(middle)
        n2 = (xhat * norm_ref[3:4, :] + norm_ref[4:5, :]).astype(BF)
        n2_s[sl, :] = n2
        cot = cot_ref[sl, :]
        two = jnp.zeros((MT, D), F32)
        gn = jnp.zeros((MT, D), F32)
        for f in range(4):
            fs = slice(f * 256, (f + 1) * 256)
            hidden = dot(n2, fc1_s[:, fs]) + jnp.concatenate([bias_ref[2 * f:2 * f + 1, :], bias_ref[2 * f + 1:2 * f + 2, :]], 1)
            gelu, slope = gelu_pair(hidden)
            act = gelu.astype(BF)
            act_s[sl, fs] = act
            two = two + dot_nt(act, fc2_s[:, fs])
            gh_f = dot(cot, fc2_s[:, fs]) * slope
            gh = gh_f.astype(BF)
            gh_s[sl, fs] = gh
            acc_s[10 + f] += fold8(gh.astype(F32))
            gn = gn + dot_nt(gh, fc1_s[:, fs])
        two = two + norm_ref[5:6, :]
        result = middle + two
        out_ref[sl, :] = result.astype(BF)
        acc_s[6] += fold8(one * one)
        acc_s[7] += fold8(middle * middle)
        acc_s[8] += fold8(two * two)
        acc_s[9] += fold8(result * result)
        cotf = cot.astype(F32)
        acc_s[5] += fold8(cotf)
        acc_s[3] += fold8(gn * xhat)
        acc_s[4] += fold8(gn)
        gm = cotf + norm_back(gn, norm_ref[3:4, :], xhat, rate)
        ig_ref[sl, :] = gm
        gb = gm.astype(BF)
        gb_s[sl, :] = gb
        acc_s[2] += fold8(gb.astype(F32))
        ga_s[sl, :] = dot(gb, proj_s[...]).astype(BF)

    stores = [pltpu.make_async_copy(out_ref, r["out_hbm"], r["store_sem"].at[0])]
    stores[0].start()

    def put_rows(ref, value, t, off):
        for n in range(batch):
            ref[n, t, :, off:off + value.shape[1]] = value[n * depth:(n + 1) * depth]

    def scatter_sum(n):
        return [push(wire_s[n].at[peer[0]], in_s[n].at[k], peer, "rb", n, k) for k, peer in enumerate(along_b)]

    def add_up(n, copies):
        arrive(copies)
        for t in range(tensor):
            value = wire_s[n][me_b, t].astype(F32)
            for k in range(batch - 1):
                value = value + in_s[n][k, t].astype(F32)
            mid_s[n][t] = value.astype(BF)
        return [push(mid_s[n].at[peer[1]], last_s[n].at[k], peer, "rt", n, k) for k, peer in enumerate(along_t)]

    def finish(n, copies, off):
        arrive(copies)
        shard = mid_s[n][me_t].astype(F32)
        for k in range(tensor - 1):
            shard = shard + last_s[n][k].astype(F32)
        shard_ref[:, off:off + shard.shape[1]] = shard
        squares = fold8(shard * shard)
        return sum(squares[:, m * 128:(m + 1) * 128] for m in range(shard.shape[1] // 128))

    n2t = jnp.transpose(n2_s[...])
    n1_s_t = r["n2t"]
    n1_s_t[...] = n2t
    for left, right, off in ((n1_s_t, gh_s, 0), (cott_s, act_s, 256)):
        for t in range(4):
            put_rows(wire_s[2], dot(left[...], right[:, t * 256:(t + 1) * 256]).astype(BF), t, off)
    sums_m = scatter_sum(2)
    gp = dot(jnp.transpose(gb_s[...]), att_s[...]).astype(BF)
    r["gp"][...] = gp

    def spread_do(b):
        for c in range(chunks):
            for j in range(4):
                rows_in = spread_rows(b, c, j, ga_s, slice(b * 128, (b + 1) * 128))
                for s in range(2):
                    do_s[b, c * 8 + j * 2 + s] = rows_in[s * PAD:(s + 1) * PAD]

    def dprobs_stage(b, s, at):
        s_s[s] = dot_nt(v_s[b, at], jnp.concatenate(head_blocks(do_s[b, at], masks), 0))

    def dscores_stage(b, s, at):
        for h in range(4):
            lanes = slice(h * 128, (h + 1) * 128)
            pf = p_s[b, at, :, lanes].astype(F32)
            t = pf * s_s[s, :, lanes]
            ds_s[s, :, lanes] = (t - pf * jnp.sum(t, 0, keepdims=True)).astype(BF)

    def dqkv_stage(b, s, at):
        pitch = 16 - 8 * b
        q, k, v, do = q_s[b, at], k_s[b, at], v_s[b, at], do_s[b, at]
        kt = jnp.transpose(k)
        dv = dot(p_s[b, at], jnp.concatenate(head_blocks(do, masks), 0))
        dk = dot(ds_s[s], jnp.concatenate(head_blocks(q, masks), 0))
        dq = jnp.transpose(own_blocks(kt, ds_s[s]))[:PAD]
        taps = [lepe_s[n:n + 1, b * 128:(b + 1) * 128] for n in range(10)]
        dof, vf = do.astype(F32), v.astype(F32)
        dv = dv + window_sum_back(dof, taps, pitch)
        for n, part in enumerate(tap_sums(dof, vf, pitch)):
            tacc_s[b, n] += part
        tacc_s[b, 9] += fold8(dof)
        dq_s[b, at] = (dq * SCALE).astype(BF)
        dk_s[b, at] = (dk * SCALE).astype(BF)
        dv_s[b, at] = dv.astype(BF)

    def branch_back(b):
        spread_do(b)
        for s in range(2):
            dprobs_stage(b, s, s)

        def step(i):
            before, after = jnp.maximum(i - 1, 0), jnp.minimum(i + 1, images - 1)

            @pl.when(i == 1)
            def _():
                tacc_s[b] = jnp.zeros((10, 8, 128), F32)

            for s in range(2):
                dqkv_stage(b, s, before * 2 + s)
                dscores_stage(b, s, i * 2 + s)
                dprobs_stage(b, s, after * 2 + s)

        pl.loop(0, images, unroll=2)(step)
        for s in range(2):
            dqkv_stage(b, s, images * 2 - 2 + s)
        if b == 1:
            smalls.append(small_out("l", pairs_of_taps(1)))
            later["m"] = add_up(2, sums_m)
            later["e"] = small_on("e", smalls[0])
            later["0"] = add_up(0, sums_0)
        dense_rows(b, lambda at: jnp.concatenate([dq_s[b, at], dk_s[b, at], dv_s[b, at]], 1), dqkv_s, 384)
        gw = dot(n1t_s[...], dqkv_s[:, b * 384:(b + 1) * 384]).astype(BF)
        packed = dot_nt(jnp.concatenate([gw, r["gp"][:, b * 128:(b + 1) * 128]], 1), lane_ref[...]).astype(BF)
        for t in range(4):
            for n in range(batch):
                part = packed[n * depth:(n + 1) * depth, t * 128:(t + 1) * 128]
                if b == 0:
                    wire_s[0][n, t] = part
                else:
                    wire_s[1][n % 2, n // 2, t] = part

    def pairs_of_taps(b):
        taps = jnp.sum(tacc_s[b], axis=1)
        return [jnp.concatenate([taps[2 * n:2 * n + 1], taps[2 * n + 1:2 * n + 2]], 1) for n in range(5)]

    def small_out(g, parts):
        own = r["small" + g]
        own[...] = jnp.zeros_like(own)
        for n, part in enumerate(parts):
            own[n:n + 1, :] = part
        r["smallb" + g][me_b] = own[...]
        return [push(own, r["smallb" + g].at[me_b], peer, "sb" + g, k) for k, peer in enumerate(along_b)]

    def in_order(ref, count):
        part = ref[0]
        for n in range(1, count):
            part = part + ref[n]
        return part

    def small_on(g, copies):
        arrive(copies)
        part = in_order(r["smallb" + g], batch)
        own = r["smalln" + g]
        own[...] = part
        r["smallt" + g][me_t] = part
        return [push(own, r["smallt" + g].at[me_t], peer, "st" + g, k) for k, peer in enumerate(along_t)]

    smalls, later = [], {}
    branch_back(0)
    sums_0 = scatter_sum(0)
    sums = jnp.sum(acc_s[2:14], axis=1)
    smalls.append(small_out("e", [sums[n:n + 1] for n in range(12)] + pairs_of_taps(0)))
    branch_back(1)
    side = lax.rem(me_b, 2)
    across = push(wire_s[1].at[1 - side], in_s[1], pair, "rc", 0)
    across.wait_recv()
    for n in range(batch // 2):
        mid_s[1][n] = (wire_s[1][side, n].astype(F32) + in_s[1][n].astype(F32)).astype(BF)
    half = lax.div(me_b, 2)
    last_1 = []
    for at, (k, n) in enumerate(plane):
        to_b, to_t = lax.rem(half + k // 2, batch // 2), lax.rem(me_t + n, tensor)
        last_1.append(push(mid_s[1].at[to_b, to_t], last_s[1].at[at], (2 * to_b + side, to_t), "rp", at))
    late = small_on("l", smalls[1])

    @pl.loop(0, NT_TILES, unroll=NT_TILES)
    def _(i):
        sl = pl.ds(pl.multiple_of(i * MT, 16), MT)
        gn = dot_nt(dqkv_s[sl, 0:768], wcat_s[...])
        xhat, rate = norm_stats(x_ref[sl, :].astype(F32))
        acc_s[0] += fold8(gn * xhat)
        acc_s[1] += fold8(gn)
        ig_ref[sl, :] = ig_ref[sl, :] + norm_back(gn, norm_ref[0:1, :], xhat, rate)

    stores.append(pltpu.make_async_copy(ig_ref, r["ig_hbm"], r["store_sem"].at[1]))
    stores[1].start()
    everyone = along_b + along_t + beyond
    me = me_b * tensor + me_t
    sums = jnp.sum(acc_s[0:2], axis=1)
    final = r["final"]
    final[...] = jnp.concatenate([sums[0:1], sums[1:2]], 1)
    r["finals"][me] = final[...]
    gains = [push(final, r["finals"].at[me], peer, "fn", k) for k, peer in enumerate(everyone)]
    lanes = finish(2, later["m"], 0) + finish(0, later["0"], 512)
    arrive(last_1)
    shard = mid_s[1][half, me_t].astype(F32)
    for at in range(len(plane)):
        shard = shard + last_s[1][at].astype(F32)
    shard_ref[:, 640:768] = shard
    lanes = jnp.sum(lanes + fold8(shard * shard), 0, keepdims=True)
    own = r["all"]
    own[...] = lanes
    sq_s[me] = own[...]
    square = [push(own, sq_s.at[me], peer, "sq", k) for k, peer in enumerate(everyone)]
    arrive(later["e"])
    arrive(late)
    first_sums, last_sums = in_order(r["smallte"], tensor), in_order(r["smalltl"], tensor)
    total_ref[2:14, :] = first_sums[0:12]
    for n in range(10):
        halves = [part[:, n % 2 * 128:n % 2 * 128 + 128] for part in (first_sums[12 + n // 2:13 + n // 2], last_sums[n // 2:1 + n // 2])]
        total_ref[14 + n:15 + n, :] = jnp.concatenate([halves[b][:, h * HD:(h + 1) * HD] for h in range(4) for b in range(2)], 1)
    row = lax.broadcasted_iota(jnp.int32, first_sums.shape, 0)
    first_sums = jnp.where((row < 4) | (row >= 8), first_sums, 0.0)
    vector = jnp.sum(first_sums * first_sums, 0, keepdims=True) + jnp.sum(last_sums * last_sums, 0, keepdims=True)
    vector = jnp.sum(vector, 1, keepdims=True)
    arrive(gains)
    whole = in_order(r["finals"], batch * tensor)
    total_ref[0:1, :] = whole[:, 0:256]
    total_ref[1:2, :] = whole[:, 256:512]
    vector = vector + jnp.sum(whole * whole, 1, keepdims=True)
    arrive(square)
    for copy in sent:
        copy.wait_send()
    matrix = jnp.sum(in_order(sq_s, batch * tensor), 1, keepdims=True)
    size_ref[...] = jnp.broadcast_to(jnp.sqrt(matrix + vector), (8, 128))
    for copy in stores:
        copy.wait()


NAMES_IN = ["x_hbm", "cot_hbm", "qkv", "proj", "m1", "m2", "norm", "lepe", "bias", "into_hbm", "outof_hbm", "mask", "lane_hbm"]
NAMES_OUT = ["out_hbm", "ig_hbm", "shard", "total", "size"]


def scratch_list(batch, tensor, rows, depth):
    n = rows // CELLS * 2
    V = pltpu.VMEM
    dma = pltpu.SemaphoreType.DMA
    stripe = (2, n, PAD, 128)
    items = [
        ("x", V((rows, D), BF)), ("cot", V((rows, D), BF)), ("out", V((rows, D), BF)), ("ig", V((rows, D), F32)),
        ("into", V((8, 2 * PAD, 208), BF)), ("outof", V((8, 208, 2 * PAD), BF)), ("lane", V((512, 512), BF)),
    ]
    for name, width in (("0", 128), ("m", 512)):
        items += [
            ("g" + name, V((batch, tensor, depth, width), BF)), ("h" + name, V((batch, tensor, depth, width), BF)), ("in" + name, V((batch - 1, tensor, depth, width), BF)),
            ("mid" + name, V((tensor, depth, width), BF)), ("last" + name, V((tensor - 1, depth, width), BF)),
        ]
    half = (batch // 2, tensor, depth, 128)
    items += [("g1", V((batch, tensor, depth, 128), BF)), ("h1", V((2,) + half, BF)), ("in1", V(half, BF)), ("mid1", V(half, BF)), ("last1", V((batch // 2 * tensor - 1, depth, 128), BF))]
    for name, count in (("e", 24), ("l", 8)):
        items += [("small" + name, V((count, D), F32)), ("smallb" + name, V((batch, count, D), F32)), ("smalln" + name, V((count, D), F32)), ("smallt" + name, V((tensor, count, D), F32))]
    items += [
        ("sq", V((batch * tensor, 1, 128), F32)), ("all", V((1, 128), F32)), ("finals", V((batch * tensor, 1, 512), F32)), ("final", V((1, 512), F32)), ("rows", V((2, n // 2, 2 * PAD, D), BF)),
        ("fc1", V((D, FF), BF)), ("fc2", V((D, FF), BF)), ("wcat", V((D, 768), BF)), ("projw", V((D, D), BF)), ("lepew", V((16, D), F32)), ("gp", V((D, D), BF)),
        ("n1", V((rows, D), BF)), ("n1t", V((D, rows), BF)), ("cott", V((D, rows), BF)), ("n2t", V((D, rows), BF)),
        ("q", V(stripe, BF)), ("k", V(stripe, BF)), ("v", V(stripe, BF)), ("a", V(stripe, BF)),
        ("p", V((2, n, PAD, 512), BF)), ("att", V((rows, D), BF)), ("n2", V((rows, D), BF)), ("act", V((rows, FF), BF)), ("gh", V((rows, FF), BF)),
        ("gb", V((rows, D), BF)), ("ga", V((rows, D), BF)), ("do", V(stripe, BF)),
        ("acc", V((14, 8, D), F32)), ("tacc", V((2, 10, 8, 128), F32)),
        ("s", V((2, PAD, 512), F32)), ("ds", V((2, PAD, 512), BF)), ("dk", V(stripe, BF)), ("dv", V(stripe, BF)),
        ("load_sem", dma((5,))), ("store_sem", dma((2,))),
    ]
    b, t = batch - 1, tensor - 1
    for name, shape in (("gp", (batch // 2 * tensor - 1,)), ("gc", (batch // 2 * tensor,)), ("gt", (2, t)), ("gb", (2, b)), ("rb", (3, b)), ("rt", (3, t)), ("rc", (1,)), ("rp", (batch // 2 * tensor - 1,)), ("sbe", (b,)), ("ste", (t,)), ("sbl", (b,)), ("stl", (t,)), ("sq", (batch * tensor - 1,)), ("fn", (batch * tensor - 1,))):
        items += [(name + "_s", dma(shape)), (name + "_r", dma(shape))]
    return items


NAMES = NAMES_IN + NAMES_OUT + [name for name, _ in scratch_list(8, 4, 2352, 32)]


def block_call(batch, tensor, linked, x, cot, qkv, proj, fc1, fc2, norm, lepe, bias):
    rows, depth = x.shape[0], fc1.shape[0]
    into, outof = spread_tables()
    args = (x, cot, qkv, proj, fc1, fc2, norm, lepe, bias, jnp.asarray(into, BF), jnp.asarray(outof, BF), jnp.asarray(key_mask()), jnp.asarray(lane_table(), BF))
    V = pl.BlockSpec(memory_space=pltpu.VMEM)
    H = pl.BlockSpec(memory_space=pl.ANY)
    extra = dict(collective_id=0, has_side_effects=True) if linked else {}
    return pl.pallas_call(
        functools.partial(block_kernel, batch, tensor, linked),
        out_shape=(
            jax.ShapeDtypeStruct((rows, D), BF),
            jax.ShapeDtypeStruct((rows, D), F32),
            jax.ShapeDtypeStruct((depth, 768), F32),
            jax.ShapeDtypeStruct((24, D), F32),
            jax.ShapeDtypeStruct((8, 128), F32),
        ),
        in_specs=[H, H] + [V] * 7 + [H, H, V, H],
        out_specs=(H, H, V, V, V),
        scratch_shapes=[shape for _, shape in scratch_list(batch, tensor, rows, depth)],
        compiler_params=pltpu.CompilerParams(vmem_limit_bytes=62 * 2**20, **extra),
    )(*args)


def adam(master, first, second, clipped, rate, decay):
    first = BETA_ONE * first + (1.0 - BETA_ONE) * clipped
    second = BETA_TWO * second + (1.0 - BETA_TWO) * clipped * clipped
    hat = first * (1.0 / (1.0 - BETA_ONE**STEP))
    spread = second * (1.0 / (1.0 - BETA_TWO**STEP))
    return master - rate * (hat / (jnp.sqrt(spread) + ADAM_EPS) + decay * master), first, second


def update_kernel(all_tokens, count_in, count_out, *refs):
    ins, refs = refs[:count_in], refs[count_in:]
    outs, refs = refs[:count_out], refs[count_out:]
    size_o, rms_o, refs = refs[0], refs[1], refs[2:]
    held_in, refs = refs[:count_in], refs[count_in:]
    held_out, (in_sem, out_sem, move_sem) = refs[:count_out], refs[count_out:]

    moves = []
    for n in range(2):
        step = held_in[n].shape[0] // 3
        for m in range(3):
            at = pl.ds(m * step, step)
            k = len(moves)
            moves.append((pltpu.make_async_copy(ins[n].at[at], held_in[n].at[at], move_sem.at[0, k]), pltpu.make_async_copy(held_in[n].at[at], outs[n].at[at], move_sem.at[1, k])))
    reads = [pltpu.make_async_copy(source, held, in_sem.at[n]) for n, (source, held) in enumerate(zip(ins[2:], held_in[2:]))]
    for copy in reads:
        copy.start()
    for into, _ in moves:
        into.start()
    for copy in reads:
        copy.wait()
    writes = []

    def write(n):
        copy = pltpu.make_async_copy(held_out[n], outs[n], out_sem.at[n - 2])
        copy.start()
        writes.append(copy)

    shard_ref, total_ref, norm_ref = held_in[2:5]
    size = norm_ref[0:1, 0:1]
    factor = jnp.minimum(1.0, CLIP_SCALE * math.sqrt(NPARAM) / (size + 1e-06))
    size_o[...] = size

    def one(grad, w, m, g_o, n_o, l_o, m_o, at, rate, decay, pair=lambda n, at: (n,) + at):
        clipped = grad * factor
        new, first, second = adam(w[at], m[pair(0, at)], m[pair(1, at)], clipped, rate, decay)
        g_o[at] = clipped
        n_o[at] = new
        if l_o is not None:
            l_o[at] = new.astype(BF)
        m_o[pair(0, at)] = first
        m_o[pair(1, at)] = second

    every = (slice(None), slice(None))
    middle = lambda n, at: (at[0], n, at[1])
    given = held_in[5:]
    lanes = lambda j: jnp.concatenate([shard_ref[:, 512 + 32 * j:544 + 32 * j], shard_ref[:, 640 + 32 * j:672 + 32 * j]], 1)
    grads = [[((j,) + every, lanes(j)) for j in range(3)], [(every, lanes(3))], [(every, shard_ref[:, 0:256])], [(every, shard_ref[:, 256:512])]]
    for n in range(4):
        made = held_out[2 + 4 * n:6 + 4 * n]
        for at, grad in grads[n]:
            one(grad, given[2 * n], given[2 * n + 1], *made, at, RATE_MATRIX, DECAY_RATE)
        for k in range(4):
            write(2 + 4 * n + k)
    bias = [((slice(f, f + 1), slice(None)), total_ref[10 + f // 2:11 + f // 2, 128 * (f % 2):128 * (f % 2) + 128]) for f in range(8)]
    for n, parts in enumerate(([(every, total_ref[0:6])], [(every, total_ref[14:24])], bias)):
        made = held_out[18 + 3 * n:21 + 3 * n]
        for at, grad in parts:
            one(grad, given[8 + 2 * n], given[9 + 2 * n], made[0], made[1], None, made[2], at, RATE_VECTOR, 0.0, middle)
        for k in range(3):
            write(18 + 3 * n + k)
    for into, away in moves:
        into.wait()
        away.start()
    lane = lax.broadcasted_iota(jnp.int32, (1, 4), 1)
    sums = jnp.zeros((1, 4), F32)
    for n in range(4):
        sums = jnp.where(lane == n, jnp.sum(total_ref[6 + n:7 + n], 1, keepdims=True), sums)
    rms_o[...] = jnp.sqrt(sums * (1.0 / (all_tokens * D)))
    for copy in writes:
        copy.wait()
    for _, away in moves:
        away.wait()


def update_call(all_tokens, out, ig, shard, total, norm, arrays):
    V = pltpu.VMEM
    dma = pltpu.SemaphoreType.DMA
    like = lambda a, dt=F32: jax.ShapeDtypeStruct(a.shape, dt)
    outs = [like(out, BF), like(ig)]
    for n in range(4):
        w, m = arrays[2 * n], arrays[2 * n + 1]
        outs += [like(w), like(w), like(w, BF), like(m)]
    for n in range(4, 7):
        w, m = arrays[2 * n], arrays[2 * n + 1]
        outs += [like(w), like(w), like(m)]
    ins = (out, ig, shard, total, norm, *arrays)
    H = pl.BlockSpec(memory_space=pl.ANY)
    held_out = [V((8, 128), F32)] * 2 + [V(o.shape, o.dtype) for o in outs[2:]]
    return list(pl.pallas_call(
        functools.partial(update_kernel, all_tokens, len(ins), len(outs)),
        out_shape=tuple(outs + [jax.ShapeDtypeStruct((1, 1), F32), jax.ShapeDtypeStruct((1, 4), F32)]),
        in_specs=[H] * len(ins),
        out_specs=tuple([H] * len(outs) + [pl.BlockSpec(memory_space=V)] * 2),
        scratch_shapes=[V(a.shape, a.dtype) for a in ins] + held_out + [dma((len(ins) - 2,)), dma((len(outs) - 2,)), dma((2, 6))],
        compiler_params=pltpu.CompilerParams(vmem_limit_bytes=60 * 2**20),
    )(*ins))


def flip(a):
    return jnp.swapaxes(a, -1, -2)


def shards(block_input, cotangent, *arrays):
    batch, tensor = lax.axis_size("batch"), lax.axis_size("tensor")
    arrays = list(arrays)
    for n in (2, 3, 6, 7):
        arrays[n] = flip(arrays[n])
    arrays[9], arrays[11] = jnp.swapaxes(arrays[9], 0, 1), jnp.swapaxes(arrays[11], 0, 1)
    arrays[12], arrays[13] = arrays[12].reshape(8, 128), jnp.swapaxes(arrays[13].reshape(2, 8, 128), 0, 1)
    qkv, _, proj, _, fc1, _, fc2, _, norm, _, lepe, _, bias, _ = arrays
    output, input_grad, shard, total, size = block_call(batch, tensor, True, block_input, cotangent, qkv, proj, fc1, fc2, norm, lepe, bias)
    output, input_grad, *got = update_call(block_input.shape[0] * batch * tensor, output, input_grad, shard, total, size, arrays)
    for n in (4, 5, 6, 7, 12, 13, 14, 15):
        got[n] = flip(got[n])
    got[18], got[21] = jnp.swapaxes(got[18], 0, 1), jnp.swapaxes(got[21], 0, 1)
    got[22], got[23], got[24] = got[22].reshape(1024), got[23].reshape(1024), jnp.swapaxes(got[24], 0, 1).reshape(2, 1024)
    got[25], got[26] = got[25].reshape(()), got[26].reshape(4)
    return (output, input_grad, *got)


def solution(mesh):
    token, matrix, moment = P(("batch", "tensor"), None), P("batch", "tensor"), P(None, "batch", "tensor")
    back, back_moment = P("tensor", "batch"), P(None, "tensor", "batch")
    stack, stack_moment = P(None, "batch", "tensor"), P(None, None, "batch", "tensor")
    return jax.shard_map(
        shards,
        mesh=mesh,
        in_specs=(token, token, stack, stack_moment, back, back_moment, matrix, moment, back, back_moment) + (P(),) * 6,
        out_specs=(token, token) + (stack,) * 3 + (stack_moment,) + (back,) * 3 + (back_moment,) + (matrix,) * 3 + (moment,) + (back,) * 3 + (back_moment,) + (P(),) * 11,
        check_vma=False,
    )
```
